32 devices in a mesh: role: 4 (over x, core), contr: 2 (over y), horiz: 4 (over z).
Axes of the slice: x: 2, y: 2, z: 4, core: 2. Of those that a mesh axis runs over, the one named last changes fastest.
Arguments:
- tops: bfloat16 [3, 320, 320, 320], P(None, 'contr', 'horiz', 'role'), may hold values from -6 to 6
- bottoms: bfloat16 [3, 320, 320, 2, 320], P(None, 'contr', 'horiz'), may hold values from -0.01953125 to 0.01953125
- left_iso: bfloat16 [320, 8, 320], P(None, None, 'horiz'), may hold values from -0.3125 to 0.3125
- right_iso: bfloat16 [320, 320, 320], P(('contr', 'horiz')), may hold values from -0.01953125 to 0.01953125
Outputs:
- coarse: float32 [2, 2, 8, 320], replicated
The draws below stay inside these ranges and needn't reach their ends.
All inputs are finite; a program needn't handle non-finite values.
Results may differ from the reference program's by a relative error of at most 0.0081.
Values may be sent and summed in bfloat16 or wider, within the bound.
No kernel may reach another device: no remote copies, remote signals or barrier semaphores. Data moves between devices by JAX's collectives and lax.ppermute only.
A program may use at most 320 MiB of HBM per device.

```python
import jax
import jax.numpy as jnp
from jax import lax

CHI = 320
DOWN = 2
A_OUT = 8


def block_levels(own_key, extent, shards, least, largest):
    def one(position, parts):
        heights = jax.random.uniform(jax.random.fold_in(jax.random.fold_in(own_key, 6), position), (parts,), jnp.float32, least / len(shards), largest / len(shards))
        return jnp.repeat(jnp.exp(heights), extent[position] // parts).reshape((-1,) + (1,) * (len(extent) - position - 1))

    gain = one(*shards[0])
    for cut in shards[1:]:
        gain = gain * one(*cut)
    return gain


def bell_draw(stream_key, dims, deviation, most, cuts=(), kind=jnp.bfloat16):
    drawn = deviation * jax.random.normal(stream_key, dims, jnp.float32)
    if cuts:
        drawn = drawn * block_levels(stream_key, dims, cuts, -0.22, 0.18)
    return jnp.clip(drawn, -most, most).astype(kind)


def setup_inputs(seed: int = 0) -> dict:
    seeds = jax.random.split(jax.random.key(seed), 5)
    return {
        "tops": bell_draw(seeds[0], (3, CHI, CHI, CHI), 1.0, 6.0, ((1, 2), (2, 4), (3, 4))),
        "bottoms": bell_draw(seeds[1], (3, CHI, CHI, DOWN, CHI), (CHI * CHI) ** -0.5, 0.01953125, ((1, 2), (2, 4))),
        "left_iso": bell_draw(seeds[2], (CHI, A_OUT, CHI), CHI ** -0.5, 0.3125, ((2, 4),)),
        "right_iso": bell_draw(seeds[3], (CHI, CHI, CHI), (CHI * CHI) ** -0.5, 0.01953125, ((0, 8),)),
    }


def pair_product(top, bottom, left_iso, right_iso):
    count = 8
    width = CHI // count
    top_blocks = jnp.transpose(top.reshape(CHI, count, width, CHI), (1, 0, 2, 3))
    iso_blocks = right_iso.reshape(count, width, CHI, CHI)
    bottom_mat = bottom.reshape(CHI * CHI, DOWN * CHI)
    left_wide = left_iso.astype(jnp.float32)

    def one_block(pieces):
        top_block, iso_block = pieces
        expanded = jnp.einsum('krl,lam->rakm', top_block.astype(jnp.float32), left_wide).astype(jnp.bfloat16)
        summed = jnp.dot(expanded.reshape(width * A_OUT, CHI * CHI), bottom_mat, preferred_element_type=jnp.float32)
        rounded = summed.astype(jnp.bfloat16).reshape(width, A_OUT, DOWN, CHI)
        return jnp.einsum('xadr,xrb->dab', rounded.astype(jnp.float32), iso_block.astype(jnp.float32))

    return jnp.sum(lax.map(one_block, (top_blocks, iso_blocks)), axis=0)


def reference(tops, bottoms, left_iso, right_iso):
    bulk = pair_product(tops[0], bottoms[0], left_iso, right_iso)
    second = pair_product(tops[2], bottoms[0], left_iso, right_iso)
    mixed = pair_product(tops[1], bottoms[1], left_iso, right_iso)
    last = pair_product(tops[0], bottoms[2], left_iso, right_iso)
    moment = 0.25 * second + 0.5 * mixed + 0.25 * last
    return jnp.stack([bulk, moment])
```

```python
import functools

import jax
import jax.numpy as jnp
from jax import lax
from jax.experimental import pallas as pl
from jax.experimental.pallas import tpu as pltpu
from jax.sharding import PartitionSpec as P

LANES = 128
ROWS = 16


def split_sizes(total, count):
    best = 1
    for n in range(1, count + 1):
        if count % n == 0 and total % n == 0 and (total // n) % ROWS == 0:
            best = n
    return best


def group_size(depth):
    best = depth
    for size in range(2, 11, 2):
        if depth % size == 0:
            best = size
    return best


def pack_kernel(group, *refs):
    pieces, (even_ref, odd_ref) = refs[:-2], refs[-2:]
    kinds, depth, rows, width = pieces[0].shape
    total = width * len(pieces)
    mains = total // LANES
    rest = total - mains * LANES
    groups = depth // group
    half = (group + 1) // 2

    def place(slot, shift):
        shape = (width, (mains + 1) * LANES)
        target = slot * width + lax.broadcasted_iota(jnp.int32, shape, 0)
        target = jnp.where(target >= mains * LANES, target + shift, target)
        hit = lax.broadcasted_iota(jnp.int32, shape, 1) == target
        return jnp.where(hit, 1.0, 0.0).astype(jnp.bfloat16)

    tables = [[place(s, shift) for s in range(len(pieces))] for shift in (0, rest)]
    for kind in range(kinds):
        out_ref, at = (odd_ref, 0) if kind == 1 else (even_ref, kind // 2)
        tails = []
        for part, (lo, hi) in enumerate(((0, half), (half, group))):
            if lo == hi:
                continue
            got = 0.0
            for slot, ref in enumerate(pieces):
                block = ref[kind].reshape(groups, group, rows, width)[:, lo:hi]
                got = got + jnp.dot(
                    block.reshape(groups * (hi - lo) * rows, width),
                    tables[part][slot],
                    preferred_element_type=jnp.float32,
                )
            got = got.reshape(groups, hi - lo, rows, (mains + 1) * LANES)
            for main in range(mains):
                out_ref[at, :, main * group + lo:main * group + hi] = got[
                    ..., main * LANES:(main + 1) * LANES
                ].astype(jnp.bfloat16)
            tails.append(got[..., mains * LANES:])
        base = mains * group
        first = tails[0]
        if len(tails) == 1:
            out_ref[at, :, base:base + half] = first.astype(jnp.bfloat16)
        else:
            both = tails[1].shape[1]
            out_ref[at, :, base:base + both] = (first[:, :both] + tails[1]).astype(jnp.bfloat16)
            if both < half:
                out_ref[at, :, base + both:base + half] = first[:, both:].astype(jnp.bfloat16)


def pack(pieces, group):
    kinds, depth, rows, width = pieces[0].shape
    mains = width * len(pieces) // LANES
    planes = mains * group + (group + 1) // 2
    shape = (depth // group, planes, rows, LANES)
    out = [
        jax.ShapeDtypeStruct((2,) + shape, jnp.bfloat16),
        jax.ShapeDtypeStruct((1,) + shape, jnp.bfloat16),
    ]
    return pl.pallas_call(
        functools.partial(pack_kernel, group),
        out_shape=out,
        in_specs=[pl.BlockSpec(memory_space=pltpu.VMEM)] * len(pieces),
        out_specs=[pl.BlockSpec(memory_space=pltpu.VMEM)] * 2,
        compiler_params=pltpu.CompilerParams(vmem_limit_bytes=32 * 2 ** 20),
        cost_estimate=pl.CostEstimate(flops=2 * 10 ** 9, bytes_accessed=4 * 2 ** 20, transcendentals=0),
        name="pack",
    )(*pieces)


def chunk_kernel(sides, group, outs, spot_ref, *refs):
    steps = sides - 1
    even_own, odd_own = refs[0], refs[1]
    even_right, even_left = refs[2:2 + steps], refs[2 + steps:2 + 2 * steps]
    at = 2 + 2 * steps
    odd_right, odd_left = refs[at:at + steps - 1], refs[at + steps - 1:at + 2 * (steps - 1)]
    at += 2 * (steps - 1)
    left_ref, next_left_ref, low_ref, next_low_ref = refs[at:at + 4]
    out_refs = refs[at + 4:at + 4 + outs]
    even, odd, spread, total, sems = refs[at + 4 + outs:]
    here, role = spot_ref[0], spot_ref[1]
    step, last = pl.program_id(0), pl.num_programs(0) - 1
    inner = jnp.logical_and(here > 0, here < sides - 1)
    rows = even.shape[-2]
    half = (group + 1) // 2
    mains = (even.shape[3] - half) // group
    windows = left_ref.shape[2] // LANES

    @pl.when(step == 0)
    def _():
        total[...] = jnp.zeros_like(total)

        def fetch(src, dst, sem, act):
            copy = pltpu.make_async_copy(src, dst, sem)
            if act:
                copy.start()
            else:
                copy.wait()

        fetch(even_own, even.at[here], sems.at[0], True)
        for gap in range(1, sides):
            slot = lax.rem(here + sides - gap, sides)

            @pl.when(here >= gap)
            def _():
                fetch(even_right[gap - 1], even.at[slot], sems.at[gap], True)

            @pl.when(here < gap)
            def _():
                fetch(even_left[sides - gap - 1], even.at[slot], sems.at[gap], True)

        @pl.when(inner)
        def _():
            fetch(odd_own, odd.at[here], sems.at[sides], True)
            for gap in range(1, sides):
                slot = lax.rem(here + sides - gap, sides)
                if gap <= steps - 1:
                    @pl.when(here >= gap)
                    def _():
                        fetch(odd_right[gap - 1], odd.at[slot], sems.at[sides + gap], True)
                if sides - gap <= steps - 1:
                    @pl.when(here < gap)
                    def _():
                        fetch(odd_left[sides - gap - 1], odd.at[slot], sems.at[sides + gap], True)

        for gap in range(sides):
            fetch(even_own, even.at[lax.rem(here + sides - gap, sides)], sems.at[gap], False)

        @pl.when(inner)
        def _():
            for gap in range(sides):
                fetch(odd_own, odd.at[lax.rem(here + sides - gap, sides)], sems.at[sides + gap], False)

    def expand(source, kind, table, slot):
        for part, (lo, hi) in enumerate(((0, half), (half, group))):
            if lo == hi:
                continue
            count = hi - lo
            planes = [
                source[:, kind, step, main * group + lo:main * group + hi] for main in range(mains)
            ] + [source[:, kind, step, mains * group:mains * group + count]]
            wide = jnp.concatenate([p.reshape(sides * count * rows, LANES) for p in planes], axis=1)
            got = jnp.dot(wide, table[part], preferred_element_type=jnp.float32).astype(jnp.bfloat16)
            got = got.reshape(sides, count, rows, windows * LANES)
            for k in range(count):
                for a in range(windows):
                    spread[slot, a, :, (lo + k) * LANES:(lo + k + 1) * LANES] = got[
                        :, k, :, a * LANES:(a + 1) * LANES
                    ].reshape(sides * rows, LANES)

    def product(slot, low):
        full = spread[slot].reshape(windows * sides * rows, group * LANES)
        return jnp.dot(
            full, low.reshape(group * LANES, low.shape[-1]), preferred_element_type=jnp.float32
        )

    expand(even, 0, left_ref, 0)
    expand(even, 1, left_ref, 1)
    total[0] += product(0, low_ref[0])
    total[1] += product(1, low_ref[0])
    total[1] += product(0, low_ref[2])

    @pl.when(inner)
    def _():
        expand(odd, 0, left_ref, 0)
        expand(odd, 0, next_left_ref, 1)
        total[1] += product(0, low_ref[1])
        total[1] += product(1, next_low_ref[...])

    @pl.when(step == last)
    def _():
        for offset in range(outs):
            which = offset ^ role
            value = total[which // 2]
            width = value.shape[1] // 2
            value = jnp.where(which % 2 == 1, value[:, width:], value[:, :width])
            out_refs[offset][...] = value.reshape(out_refs[offset].shape).astype(jnp.bfloat16)


def chunk_product(spot, blocks, tables, lows, sides, group, outs):
    even_own = blocks[0]
    _, groups, planes, rows, _ = even_own.shape
    left_table, next_table = tables
    low, next_low = lows
    windows = left_table.shape[2] // LANES
    full = low.shape[-1]
    count = windows * sides * rows
    whole = lambda arr: pl.BlockSpec(arr.shape, lambda g, s: (0,) * arr.ndim)
    out = [jax.ShapeDtypeStruct((windows, sides * rows, full // 2), jnp.bfloat16)] * outs
    depth = groups * group
    flops = 2 * count * depth * LANES * (5 * full) + 2 * 4 * sides * rows * depth * 3 * LANES * windows * LANES
    return pl.pallas_call(
        functools.partial(chunk_kernel, sides, group, outs),
        out_shape=out,
        grid_spec=pltpu.PrefetchScalarGridSpec(
            num_scalar_prefetch=1,
            grid=(groups,),
            in_specs=[pl.BlockSpec(memory_space=pl.ANY)] * len(blocks)
            + [
                whole(left_table),
                whole(next_table),
                pl.BlockSpec((3, group) + low.shape[2:], lambda g, s: (0, g, 0, 0)),
                pl.BlockSpec((group,) + next_low.shape[1:], lambda g, s: (g, 0, 0)),
            ],
            out_specs=[pl.BlockSpec(o.shape, lambda g, s: (0, 0, 0)) for o in out],
            scratch_shapes=[
                pltpu.VMEM((sides, 2, groups, planes, rows, LANES), jnp.bfloat16),
                pltpu.VMEM((sides, 1, groups, planes, rows, LANES), jnp.bfloat16),
                pltpu.VMEM((2, windows, sides * rows, group * LANES), jnp.bfloat16),
                pltpu.VMEM((2, count, full), jnp.float32),
                pltpu.SemaphoreType.DMA((2 * sides,)),
            ],
        ),
        compiler_params=pltpu.CompilerParams(vmem_limit_bytes=56 * 2 ** 20),
        cost_estimate=pl.CostEstimate(flops=flops, bytes_accessed=30 * 2 ** 20, transcendentals=0),
        name="chunk_product",
    )(spot, *blocks, left_table, next_table, low, next_low)


def tied(value, *after):
    return lax.optimization_barrier((value,) + after)[0]


def on_device(sizes, tops, bottoms, left_iso, right_iso):
    roles, contrs, sides = sizes
    role = lax.axis_index("role")
    here = lax.axis_index("horiz")
    kinds, depth_all, rows_all, width = tops.shape
    depth = depth_all // roles
    group = group_size(depth)
    share = right_iso.shape[0]
    chunks = split_sizes(rows_all, share)
    unit = share // chunks
    windows = left_iso.shape[1]
    slab = left_iso.shape[2]
    spot = jnp.stack([here, role]).astype(jnp.int32)

    cut = tops.reshape(kinds, depth_all, contrs, chunks, unit, width)

    def exchange(t):
        part = cut[:, :, :, t].reshape(kinds, depth_all, contrs * unit, width)
        pieces = []
        for s in range(roles):
            piece = lax.dynamic_slice_in_dim(part, (role ^ s) * depth, depth, 1)
            if s:
                piece = lax.ppermute(piece, "role", [(j, j ^ s) for j in range(roles)])
            pieces.append(piece)
        return pieces

    def flows(block, reach, low_end, high_end):
        right, left = [], []
        now = block
        for d in range(1, reach + 1):
            now = lax.ppermute(
                now, "horiz", [(z, z + 1) for z in range(d - 1, sides - 1) if low_end <= z + 1 <= high_end]
            )
            right.append(now)
        now = block
        for d in range(1, reach + 1):
            now = lax.ppermute(
                now, "horiz", [(z, z - 1) for z in range(sides - d, 0, -1) if low_end <= z - 1 <= high_end]
            )
            left.append(now)
        return right, left

    hand = [(0, 1), (sides - 1, sides - 2)]
    left_all = jnp.concatenate(
        [lax.dynamic_slice_in_dim(left_iso, (role ^ s) * width, width, 0) for s in range(roles)], axis=0
    )
    total = left_all.shape[0]
    mains = total // LANES * LANES
    rest = total - mains

    def table(flat):
        wide = jnp.pad(flat.reshape(total, windows, slab), ((0, 0), (0, 0), (0, LANES - slab)))
        wide = wide.reshape(total, windows * LANES)
        first = jnp.pad(wide, ((0, LANES - rest), (0, 0)))
        blank = jnp.zeros((rest, windows * LANES), wide.dtype)
        second = jnp.concatenate([wide[:mains], blank, wide[mains:]], axis=0)
        second = jnp.pad(second, ((0, LANES - 2 * rest), (0, 0)))
        return jnp.stack([first, second])

    flat_left = left_all.reshape(total, windows * slab)
    low = lax.dynamic_slice_in_dim(bottoms, role * depth, depth, 1)
    downs, full = low.shape[3], low.shape[4]
    low = low.reshape(kinds, depth, slab, downs * full)
    low = low * jnp.array([1, 2, 1], low.dtype).reshape(kinds, 1, 1, 1)

    packed = []
    for t in range(chunks):
        packed.append(pack(exchange(t), group))
    next_flat = lax.ppermute(flat_left, "horiz", hand)
    next_low = lax.ppermute(low[1], "horiz", hand)
    pad_low = lambda arr: jnp.pad(arr, [(0, 0)] * (arr.ndim - 2) + [(0, LANES - slab), (0, 0)])
    tables = (table(flat_left), table(next_flat))
    lows = (pad_low(low), pad_low(next_low))

    projected = 0.0
    for t in range(chunks):
        even, odd = packed[t]
        even_right, even_left = flows(even, sides - 1, 0, sides - 1)
        odd_right, odd_left = flows(odd, sides - 2, 1, sides - 2)
        blocks = [even, odd] + even_right + even_left + odd_right + odd_left
        parts = chunk_product(spot, blocks, tables, lows, sides, group, roles)
        summed = parts[0].astype(jnp.float32)
        for s in range(1, roles):
            got = lax.ppermute(parts[s], "role", [(j, j ^ s) for j in range(roles)])
            summed = summed + got.astype(jnp.float32)
        summed = summed.reshape(windows, sides * contrs, unit, full)
        count = sides * contrs
        step = contrs // 2
        place = lax.axis_index("contr")
        while step:
            count //= 2
            bit = (place // step) % 2
            keep = lax.dynamic_slice_in_dim(summed, bit * count, count, 1)
            give = lax.dynamic_slice_in_dim(summed, (1 - bit) * count, count, 1).astype(jnp.bfloat16)
            got = lax.ppermute(give, "contr", [(j, j ^ step) for j in range(contrs)])
            summed = keep + got.astype(jnp.float32)
            step //= 2
        mine = lax.dynamic_slice_in_dim(summed, here, 1, 1)
        for s in range(1, sides):
            give = lax.dynamic_slice_in_dim(summed, lax.rem(here + s, sides), 1, 1).astype(jnp.bfloat16)
            got = lax.ppermute(give, "horiz", [(z, (z + s) % sides) for z in range(sides)])
            mine = mine + got.astype(jnp.float32)
        mine = mine.reshape(windows, unit, full).astype(jnp.bfloat16)
        projected = projected + jnp.einsum(
            "aur,urb->ab", mine, right_iso[t * unit:(t + 1) * unit], preferred_element_type=jnp.float32
        )

    projected = projected * jnp.where(role >= downs, 0.25, 1.0)
    for axis, size in (("contr", contrs), ("horiz", sides)):
        s = 1
        while s < size:
            projected = projected + lax.ppermute(projected, axis, [(j, j ^ s) for j in range(size)])
            s *= 2
    pieces = [projected] + [
        lax.ppermute(projected, "role", [(j, j ^ s) for j in range(roles)]) for s in range(1, roles)
    ]
    pieces = jnp.stack(pieces)
    order = [lax.dynamic_index_in_dim(pieces, q ^ role, 0, keepdims=False) for q in range(roles)]
    return jnp.stack(order).reshape(roles // downs, downs, windows, -1)


def solution(mesh):
    placed = (
        P(None, "contr", "horiz", "role"),
        P(None, "contr", "horiz", None, None),
        P(None, None, "horiz"),
        P(("contr", "horiz"), None, None),
    )
    sizes = tuple(mesh.shape[axis] for axis in ("role", "contr", "horiz"))
    body = functools.partial(on_device, sizes)
    return jax.shard_map(body, mesh=mesh, in_specs=placed, out_specs=P(), check_vma=False)
```

```python
import functools

import jax
import jax.numpy as jnp
from jax import lax
from jax.experimental import pallas as pl
from jax.experimental.pallas import tpu as pltpu
from jax.sharding import PartitionSpec as P

LANES = 128
ROWS = 16


def split_sizes(total, count):
    best = 1
    for n in range(1, count + 1):
        if count % n == 0 and total % n == 0 and (total // n) % ROWS == 0:
            best = n
    return best


def group_size(depth):
    best = depth
    for size in range(2, 11, 2):
        if depth % size == 0:
            best = size
    return best


def pack_kernel(group, *refs):
    pieces, (even_ref, odd_ref) = refs[:-2], refs[-2:]
    kinds, depth, rows, width = pieces[0].shape
    total = width * len(pieces)
    mains = total // LANES
    rest = total - mains * LANES
    groups = depth // group
    half = (group + 1) // 2

    def place(slot, shift):
        shape = (width, (mains + 1) * LANES)
        target = slot * width + lax.broadcasted_iota(jnp.int32, shape, 0)
        target = jnp.where(target >= mains * LANES, target + shift, target)
        hit = lax.broadcasted_iota(jnp.int32, shape, 1) == target
        return jnp.where(hit, 1.0, 0.0).astype(jnp.bfloat16)

    tables = [[place(s, shift) for s in range(len(pieces))] for shift in (0, rest)]
    for kind in range(kinds):
        out_ref, at = (odd_ref, 0) if kind == 1 else (even_ref, kind // 2)
        tails = []
        for part, (lo, hi) in enumerate(((0, half), (half, group))):
            if lo == hi:
                continue
            got = 0.0
            for slot, ref in enumerate(pieces):
                block = ref[kind].reshape(groups, group, rows, width)[:, lo:hi]
                got = got + jnp.dot(
                    block.reshape(groups * (hi - lo) * rows, width),
                    tables[part][slot],
                    preferred_element_type=jnp.float32,
                )
            got = got.reshape(groups, hi - lo, rows, (mains + 1) * LANES)
            for main in range(mains):
                out_ref[at, :, main * group + lo:main * group + hi] = got[
                    ..., main * LANES:(main + 1) * LANES
                ].astype(jnp.bfloat16)
            tails.append(got[..., mains * LANES:])
        base = mains * group
        first = tails[0]
        if len(tails) == 1:
            out_ref[at, :, base:base + half] = first.astype(jnp.bfloat16)
        else:
            both = tails[1].shape[1]
            out_ref[at, :, base:base + both] = (first[:, :both] + tails[1]).astype(jnp.bfloat16)
            if both < half:
                out_ref[at, :, base + both:base + half] = first[:, both:].astype(jnp.bfloat16)


def pack(pieces, group):
    kinds, depth, rows, width = pieces[0].shape
    mains = width * len(pieces) // LANES
    planes = mains * group + (group + 1) // 2
    shape = (depth // group, planes, rows, LANES)
    out = [
        jax.ShapeDtypeStruct((2,) + shape, jnp.bfloat16),
        jax.ShapeDtypeStruct((1,) + shape, jnp.bfloat16),
    ]
    return pl.pallas_call(
        functools.partial(pack_kernel, group),
        out_shape=out,
        in_specs=[pl.BlockSpec(memory_space=pltpu.VMEM)] * len(pieces),
        out_specs=[pl.BlockSpec(memory_space=pltpu.VMEM)] * 2,
        compiler_params=pltpu.CompilerParams(vmem_limit_bytes=32 * 2 ** 20),
        cost_estimate=pl.CostEstimate(flops=2 * 10 ** 9, bytes_accessed=4 * 2 ** 20, transcendentals=0),
        name="pack",
    )(*pieces)


def fetch(src, dst, sem):
    pltpu.make_async_copy(src, dst, sem).start()


def expand(source, step, group, tables, spread):
    sides, kinds, _, _, rows, _ = source.shape
    half = (group + 1) // 2
    mains = (source.shape[3] - half) // group
    windows = spread[0].shape[0]
    for part, (lo, hi) in enumerate(((0, half), (half, group))):
        if lo == hi:
            continue
        count = hi - lo
        planes = [
            source[:, :, step, main * group + lo:main * group + hi] for main in range(mains)
        ] + [source[:, :, step, mains * group:mains * group + count]]
        wide = jnp.concatenate([p.reshape(sides * kinds * count * rows, LANES) for p in planes], axis=1)
        for slot, table in enumerate(tables):
            got = jnp.dot(wide, table[part], preferred_element_type=jnp.float32).astype(jnp.bfloat16)
            got = got.reshape(sides, kinds, count, rows, windows * LANES)
            for kind in range(kinds):
                for k in range(count):
                    for a in range(windows):
                        spread[slot + kind][a, :, (lo + k) * LANES:(lo + k + 1) * LANES] = got[
                            :, kind, k, :, a * LANES:(a + 1) * LANES
                        ].reshape(sides * rows, LANES)


def flat(ref):
    windows, rows, lanes = ref.shape
    return ref[...].reshape(windows * rows, lanes)


def even_kernel(sides, group, use_ends, use_inner, spot_ref, *refs):
    inner_blocks, end_blocks = refs[:sides], refs[sides:2 * sides]
    left_ref, first_ref, last_ref, total = refs[2 * sides:2 * sides + 4]
    even, spread_a, spread_b, sems = refs[2 * sides + 4:]
    here = spot_ref[0]
    step = pl.program_id(0)
    inner = jnp.logical_and(here > 0, here < sides - 1)
    work = jnp.logical_or(jnp.logical_and(inner, use_inner), jnp.logical_and(jnp.logical_not(inner), use_ends))

    @pl.when(work)
    def _():
        @pl.when(step == 0)
        def _():
            total[...] = jnp.zeros_like(total)

            @pl.when(inner)
            def _():
                for at, turn in enumerate((0, 1, 3, 2)):
                    fetch(inner_blocks[at], even.at[here ^ turn], sems.at[at])

            @pl.when(jnp.logical_not(inner))
            def _():
                for at, turn in enumerate((0, 1, 2, 3)):
                    fetch(end_blocks[at], even.at[here ^ turn], sems.at[at])

            for at in range(sides):
                pltpu.make_async_copy(inner_blocks[at], even.at[at], sems.at[at]).wait()

        expand(even, step, group, (left_ref,), (spread_a, spread_b))
        first = first_ref[...].reshape(group * LANES, first_ref.shape[-1])
        last = last_ref[...].reshape(group * LANES, last_ref.shape[-1])
        total[0] += jnp.dot(flat(spread_a), first, preferred_element_type=jnp.float32)
        total[1] += jnp.dot(flat(spread_b), first, preferred_element_type=jnp.float32)
        total[1] += jnp.dot(flat(spread_a), last, preferred_element_type=jnp.float32)

    @pl.when(jnp.logical_and(step == 0, jnp.logical_not(work)))
    def _():
        total[...] = jnp.zeros_like(total)


def even_product(spot, inner_blocks, end_blocks, table, first, last, sides, group):
    some = inner_blocks or end_blocks
    use_inner, use_ends = inner_blocks is not None, end_blocks is not None
    _, groups, planes, rows, _ = some[0].shape
    windows = table.shape[2] // LANES
    full = first.shape[-1]
    count = windows * sides * rows
    whole = lambda arr: pl.BlockSpec(arr.shape, lambda g, s: (0,) * len(arr.shape))
    low = pl.BlockSpec((group,) + first.shape[1:], lambda g, s: (g, 0, 0))
    out = jax.ShapeDtypeStruct((2, count, full), jnp.float32)
    depth = groups * group
    flops = 2 * count * depth * LANES * 3 * full + 4 * sides * rows * depth * 3 * LANES * windows * LANES
    return pl.pallas_call(
        functools.partial(even_kernel, sides, group, use_ends, use_inner),
        out_shape=out,
        grid_spec=pltpu.PrefetchScalarGridSpec(
            num_scalar_prefetch=1,
            grid=(groups,),
            in_specs=[pl.BlockSpec(memory_space=pl.ANY)] * (2 * sides) + [whole(table), low, low],
            out_specs=whole(out),
            scratch_shapes=[
                pltpu.VMEM((sides, 2, groups, planes, rows, LANES), jnp.bfloat16),
                pltpu.VMEM((windows, sides * rows, group * LANES), jnp.bfloat16),
                pltpu.VMEM((windows, sides * rows, group * LANES), jnp.bfloat16),
                pltpu.SemaphoreType.DMA((sides,)),
            ],
        ),
        compiler_params=pltpu.CompilerParams(vmem_limit_bytes=40 * 2 ** 20),
        cost_estimate=pl.CostEstimate(flops=flops, bytes_accessed=20 * 2 ** 20, transcendentals=0),
        name="even_product",
    )(spot, *(inner_blocks or some), *(end_blocks or some), table, first, last)


def odd_kernel(sides, group, outs, spot_ref, *refs):
    blocks = refs[:sides]
    inner_part, end_part = refs[sides:sides + 2]
    left_ref, next_left_ref, low_ref, next_low_ref = refs[sides + 2:sides + 6]
    out_refs = refs[sides + 6:sides + 6 + outs]
    odd, spread_a, spread_b, total, sems = refs[sides + 6 + outs:]
    here, role = spot_ref[0], spot_ref[1]
    step, last = pl.program_id(0), pl.num_programs(0) - 1
    inner = jnp.logical_and(here > 0, here < sides - 1)

    @pl.when(step == 0)
    def _():
        @pl.when(inner)
        def _():
            fetch(inner_part, total, sems.at[sides])
            for at, turn in enumerate((0, 1, 3, 2)):
                fetch(blocks[at], odd.at[here ^ turn], sems.at[at])
            for at in range(sides):
                pltpu.make_async_copy(blocks[at], odd.at[at], sems.at[at]).wait()

        @pl.when(jnp.logical_not(inner))
        def _():
            fetch(end_part, total, sems.at[sides])

        pltpu.make_async_copy(inner_part, total, sems.at[sides]).wait()

    @pl.when(inner)
    def _():
        expand(odd, step, group, (left_ref, next_left_ref), (spread_a, spread_b))
        low = low_ref[...].reshape(group * LANES, low_ref.shape[-1])
        next_low = next_low_ref[...].reshape(group * LANES, low_ref.shape[-1])
        total[1] += jnp.dot(flat(spread_a), low, preferred_element_type=jnp.float32)
        total[1] += jnp.dot(flat(spread_b), next_low, preferred_element_type=jnp.float32)

    @pl.when(step == last)
    def _():
        for offset in range(outs):
            which = offset ^ role
            value = total[which // 2]
            width = value.shape[1] // 2
            value = jnp.where(which % 2 == 1, value[:, width:], value[:, :width])
            out_refs[offset][...] = value.reshape(out_refs[offset].shape).astype(jnp.bfloat16)


def odd_product(spot, blocks, inner_part, end_part, tables, lows, sides, group, outs):
    _, groups, planes, rows, _ = blocks[0].shape
    table, next_table = tables
    low, next_low = lows
    windows = table.shape[2] // LANES
    full = low.shape[-1]
    count = windows * sides * rows
    whole = lambda arr: pl.BlockSpec(arr.shape, lambda g, s: (0,) * len(arr.shape))
    part = pl.BlockSpec((group,) + low.shape[1:], lambda g, s: (g, 0, 0))
    out = [jax.ShapeDtypeStruct((windows, sides * rows, full // 2), jnp.bfloat16)] * outs
    depth = groups * group
    flops = 2 * count * depth * LANES * 2 * full + 4 * sides * rows * depth * 3 * LANES * windows * LANES
    return pl.pallas_call(
        functools.partial(odd_kernel, sides, group, outs),
        out_shape=out,
        grid_spec=pltpu.PrefetchScalarGridSpec(
            num_scalar_prefetch=1,
            grid=(groups,),
            in_specs=[pl.BlockSpec(memory_space=pl.ANY)] * (sides + 2)
            + [whole(table), whole(next_table), part, part],
            out_specs=[whole(o) for o in out],
            scratch_shapes=[
                pltpu.VMEM((sides, 1, groups, planes, rows, LANES), jnp.bfloat16),
                pltpu.VMEM((windows, sides * rows, group * LANES), jnp.bfloat16),
                pltpu.VMEM((windows, sides * rows, group * LANES), jnp.bfloat16),
                pltpu.VMEM((2, count, full), jnp.float32),
                pltpu.SemaphoreType.DMA((sides + 1,)),
            ],
        ),
        compiler_params=pltpu.CompilerParams(vmem_limit_bytes=40 * 2 ** 20),
        cost_estimate=pl.CostEstimate(flops=flops, bytes_accessed=20 * 2 ** 20, transcendentals=0),
        name="odd_product",
    )(spot, *blocks, inner_part, end_part, table, next_table, low, next_low)


def tie(*values):
    return lax.optimization_barrier(values)


def on_device(sizes, tops, bottoms, left_iso, right_iso):
    roles, contrs, sides = sizes
    role = lax.axis_index("role")
    here = lax.axis_index("horiz")
    kinds, depth_all, rows_all, width = tops.shape
    depth = depth_all // roles
    group = group_size(depth)
    share = right_iso.shape[0]
    chunks = split_sizes(rows_all, share)
    unit = share // chunks
    windows = left_iso.shape[1]
    slab = left_iso.shape[2]
    downs, full = bottoms.shape[3], bottoms.shape[4]
    spot = jnp.stack([here, role]).astype(jnp.int32)

    cut = tops.reshape(kinds, depth_all, contrs, chunks, unit, width)

    def exchange(t, place):
        part = cut[:, :, :, t].reshape(kinds, depth_all, contrs * unit, width)
        pieces = []
        for s in range(roles):
            piece = lax.dynamic_slice_in_dim(part, (place ^ s) * depth, depth, 1)
            if s:
                piece = lax.ppermute(piece, "role", [(j, j ^ s) for j in range(roles)])
            pieces.append(piece)
        return pieces

    def lower(kind, place):
        low = lax.dynamic_slice_in_dim(bottoms[kind], place * depth, depth, 0)
        return low.reshape(depth, slab, downs * full)

    def padded(low):
        return jnp.pad(low, ((0, 0), (0, LANES - slab), (0, 0)))

    pairs = [(z, z ^ 1) for z in range(sides)]
    hand = [(z, z ^ 1) for z in (0, sides - 1)]
    cross = [(z, z ^ 3) for z in range(1, sides - 1)]
    back = [(z, z ^ 1) for z in range(1, sides - 1)]
    move = lambda value, perm: lax.ppermute(value, "horiz", perm)

    pieces = exchange(0, role)
    left_all = jnp.concatenate(
        [lax.dynamic_slice_in_dim(left_iso, (role ^ s) * width, width, 0) for s in range(roles)], axis=0
    )
    total = left_all.shape[0]
    mains = total // LANES * LANES
    rest = total - mains

    def table(flat_left):
        wide = jnp.pad(
            flat_left.reshape(total, windows, slab), ((0, 0), (0, 0), (0, LANES - slab))
        ).reshape(total, windows * LANES)
        first = jnp.pad(wide, ((0, LANES - rest), (0, 0)))
        blank = jnp.zeros((rest, windows * LANES), wide.dtype)
        second = jnp.concatenate([wide[:mains], blank, wide[mains:]], axis=0)
        second = jnp.pad(second, ((0, LANES - 2 * rest), (0, 0)))
        return jnp.stack([first, second])

    flat_left = left_all.reshape(total, windows * slab)
    middle = lower(1, role) * jnp.asarray(2, bottoms.dtype)
    next_middle = move(middle, hand)
    own = {0: pack(pieces, group)}
    next_left = move(flat_left, hand)
    late, _ = tie(role, own[0][0])
    pieces = exchange(1, late) if chunks > 1 else None

    near = {}
    far = {}
    sums, shares = {}, {}
    lows = tables = None
    mark = own[0][0]
    for r in range(chunks + 3):
        if r < chunks:
            a, b, mark = tie(*own[r], mark)
            if r:
                held = tie(a, b, mark, *near[r - 1])
                a, b, mark, near[r - 1] = held[0], held[1], held[2], held[3:]
            own[r] = (a, b)
            near[r] = (move(a, pairs), move(b, hand), move(a, cross), move(b, cross))
        elif r == chunks:
            held = tie(mark, *near[r - 1])
            mark, near[r - 1] = held[0], held[1:]
        if r + 1 < chunks:
            own[r + 1] = pack(pieces, group)
            late, _ = tie(role, own[r + 1][0])
            pieces = exchange(r + 2, late) if r + 2 < chunks else None
        if r == 0:
            late, _ = tie(role, own[0][0])
            lows = (padded(lower(0, late)), padded(lower(2, late)), padded(middle))
            tables = (table(flat_left), table(next_left))
            mark = lows[1]
        t = r - 4
        if 0 <= t < chunks:
            shares[t] = odd_product(
                spot, (own[t][1], near[t][1], near[t][3], far[t][1]), sums[t + 2], sums[t + 3],
                tables, (lows[2], padded(next_middle)), sides, group, roles,
            )
            mark = shares[t][0]
        ready = [mark]
        for t in (r - 1, r - 2):
            if 0 <= t < chunks:
                ready += list(near[t])
        for t in (r - 2, r - 3):
            if t in far:
                ready += list(far[t])
        ready = list(tie(*ready))
        mark = ready.pop(0)
        for t in (r - 1, r - 2):
            if 0 <= t < chunks:
                near[t], ready = tuple(ready[:4]), ready[4:]
        for t in (r - 2, r - 3):
            if t in far:
                count = len(far[t])
                far[t], ready = tuple(ready[:count]), ready[count:]
        t = r - 1
        if 0 <= t < chunks:
            far[t] = (move(near[t][0], cross), move(near[t][1], cross), move(near[t][2], back))
        t = r - 2
        if 0 <= t < chunks:
            far[t] = far[t] + (move(far[t][0], back),)
        if r >= 2:
            t = r - 2
            inner_blocks = (own[t][0], near[t][0], near[t][2], far[t][0]) if t < chunks else None
            t = r - 3
            end_blocks = (own[t][0], near[t][0], far[t][2], far[t][3]) if 0 <= t else None
            sums[r] = even_product(spot, inner_blocks, end_blocks, tables[0], lows[0], lows[1], sides, group)
            mark = sums[r]
    t = chunks - 1
    shares[t] = odd_product(
        spot, (own[t][1], near[t][1], near[t][3], far[t][1]), sums[t + 2], sums[t + 3],
        tables, (lows[2], padded(next_middle)), sides, group, roles,
    )

    projected = 0.0
    for t in range(chunks):
        parts = shares[t]
        summed = parts[0].astype(jnp.float32)
        for s in range(1, roles):
            got = lax.ppermute(parts[s], "role", [(j, j ^ s) for j in range(roles)])
            summed = summed + got.astype(jnp.float32)
        summed = summed.reshape(windows, sides * contrs, unit, full)
        count = sides * contrs
        step = contrs // 2
        place = lax.axis_index("contr")
        while step:
            count //= 2
            bit = (place // step) % 2
            keep = lax.dynamic_slice_in_dim(summed, bit * count, count, 1)
            give = lax.dynamic_slice_in_dim(summed, (1 - bit) * count, count, 1).astype(jnp.bfloat16)
            got = lax.ppermute(give, "contr", [(j, j ^ step) for j in range(contrs)])
            summed = keep + got.astype(jnp.float32)
            step //= 2
        mine = lax.dynamic_slice_in_dim(summed, here, 1, 1)
        for s in range(1, sides):
            give = lax.dynamic_slice_in_dim(summed, here ^ s, 1, 1).astype(jnp.bfloat16)
            got = lax.ppermute(give, "horiz", [(z, z ^ s) for z in range(sides)])
            mine = mine + got.astype(jnp.float32)
        mine = mine.reshape(windows, unit, full).astype(jnp.bfloat16)
        projected = projected + jnp.einsum(
            "aur,urb->ab", mine, right_iso[t * unit:(t + 1) * unit], preferred_element_type=jnp.float32
        )

    projected = projected * jnp.where(role >= downs, 0.25, 1.0)
    for axis, size in (("contr", contrs), ("horiz", sides)):
        s = 1
        while s < size:
            projected = projected + lax.ppermute(projected, axis, [(j, j ^ s) for j in range(size)])
            s *= 2
    pieces = [projected] + [
        lax.ppermute(projected, "role", [(j, j ^ s) for j in range(roles)]) for s in range(1, roles)
    ]
    pieces = jnp.stack(pieces)
    order = [lax.dynamic_index_in_dim(pieces, q ^ role, 0, keepdims=False) for q in range(roles)]
    return jnp.stack(order).reshape(roles // downs, downs, windows, -1)


def solution(mesh):
    placed = (
        P(None, "contr", "horiz", "role"),
        P(None, "contr", "horiz", None, None),
        P(None, None, "horiz"),
        P(("contr", "horiz"), None, None),
    )
    sizes = tuple(mesh.shape[axis] for axis in ("role", "contr", "horiz"))
    body = functools.partial(on_device, sizes)
    return jax.shard_map(body, mesh=mesh, in_specs=placed, out_specs=P(), check_vma=False)
```

```python
import functools

import jax
import jax.numpy as jnp
from jax import lax
from jax.experimental import pallas as pl
from jax.experimental.pallas import tpu as pltpu
from jax.sharding import PartitionSpec as P

LANES = 128
ROWS = 16


def split_sizes(total, count):
    best = 1
    for n in range(1, count + 1):
        if count % n == 0 and total % n == 0 and (total // n) % ROWS == 0:
            best = n
    return best


def group_size(depth):
    best = depth
    for size in range(2, 11, 2):
        if depth % size == 0:
            best = size
    return best


def pack_kernel(group, parts, given, spot_ref, *refs):
    pieces, crossed_ref, low_ref = refs[:parts], refs[parts], refs[parts + 1]
    sent_ref, own_ref, mark_ref, sem = refs[-4:] if parts else (refs[-3], None, refs[-2], refs[-1])
    here = spot_ref[0]
    sides = given["sides"]
    inner = jnp.logical_and(here > 0, here < sides - 1)
    groups, back_at, low_at, low_count, kind_at = (
        given["groups"], given["back"], given["low"], given["count"], given["kind"]
    )
    mark_ref[0] = spot_ref[0]
    mark_ref[1] = spot_ref[1]

    def back():
        return pltpu.make_async_copy(
            crossed_ref.at[0:2 * groups], sent_ref.at[back_at:back_at + 2 * groups], sem
        )

    def lower():
        return pltpu.make_async_copy(
            low_ref.at[low_at:low_at + low_count], sent_ref.at[kind_at:kind_at + low_count], sem
        )

    if given["has_back"]:
        @pl.when(inner)
        def _():
            back().start()
    if low_count:
        @pl.when(jnp.logical_not(inner))
        def _():
            lower().start()

    if parts:
        kinds, depth, rows, width = pieces[0].shape
        total = width * parts
        mains = total // LANES
        rest = total - mains * LANES
        half = (group + 1) // 2

        def place(slot, shift):
            shape = (width, (mains + 1) * LANES)
            target = slot * width + lax.broadcasted_iota(jnp.int32, shape, 0)
            target = jnp.where(target >= mains * LANES, target + shift, target)
            hit = lax.broadcasted_iota(jnp.int32, shape, 1) == target
            return jnp.where(hit, 1.0, 0.0).astype(jnp.bfloat16)

        tables = [[place(s, shift) for s in range(parts)] for shift in (0, rest)]
        for kind in range(kinds):
            base = (0, 2, 1)[kind] * groups

            def put(lo, hi, value):
                value = value.astype(jnp.bfloat16)
                own_ref[base:base + groups, lo:hi] = value
                if kind != 1:
                    sent_ref[base:base + groups, lo:hi] = value
                else:
                    @pl.when(jnp.logical_not(inner))
                    def _():
                        sent_ref[base:base + groups, lo:hi] = value

            tails = []
            for part, (lo, hi) in enumerate(((0, half), (half, group))):
                if lo == hi:
                    continue
                got = 0.0
                for slot, ref in enumerate(pieces):
                    block = ref[kind].reshape(groups, group, rows, width)[:, lo:hi]
                    got = got + jnp.dot(
                        block.reshape(groups * (hi - lo) * rows, width),
                        tables[part][slot],
                        preferred_element_type=jnp.float32,
                    )
                got = got.reshape(groups, hi - lo, rows, (mains + 1) * LANES)
                for main in range(mains):
                    put(main * group + lo, main * group + hi, got[..., main * LANES:(main + 1) * LANES])
                tails.append(got[..., mains * LANES:])
            start = mains * group
            first = tails[0]
            if len(tails) == 1:
                put(start, start + half, first)
            else:
                both = tails[1].shape[1]
                put(start, start + both, first[:, :both] + tails[1])
                if both < half:
                    put(start + both, start + half, first[:, both:])

    if given["has_back"]:
        @pl.when(inner)
        def _():
            back().wait()
    if low_count:
        @pl.when(jnp.logical_not(inner))
        def _():
            lower().wait()


def pack(spot, pieces, crossed, low, deps, given, group, plane, length):
    has_back = crossed is not None
    given = dict(given, has_back=has_back)
    groups = given["groups"]
    out = [jax.ShapeDtypeStruct((length,) + plane, jnp.bfloat16)]
    specs = [pl.BlockSpec(memory_space=pltpu.VMEM)]
    if pieces:
        out.append(jax.ShapeDtypeStruct((3 * groups,) + plane, jnp.bfloat16))
        specs.append(pl.BlockSpec(memory_space=pltpu.VMEM))
    out.append(jax.ShapeDtypeStruct((2,), jnp.int32))
    specs.append(pl.BlockSpec(memory_space=pltpu.SMEM))
    anywhere = pl.BlockSpec(memory_space=pl.ANY)
    operands = [crossed if has_back else low, low] + list(deps)
    got = pl.pallas_call(
        functools.partial(pack_kernel, group, len(pieces), given),
        out_shape=out,
        in_specs=[pl.BlockSpec(memory_space=pltpu.SMEM)]
        + [pl.BlockSpec(memory_space=pltpu.VMEM)] * len(pieces)
        + [anywhere] * len(operands),
        out_specs=specs,
        scratch_shapes=[pltpu.SemaphoreType.DMA],
        compiler_params=pltpu.CompilerParams(vmem_limit_bytes=32 * 2 ** 20),
        cost_estimate=pl.CostEstimate(flops=2 * 10 ** 9, bytes_accessed=6 * 2 ** 20, transcendentals=0),
        name="pack",
    )(spot, *pieces, *operands)
    return (got[0], got[1], got[2]) if pieces else (got[0], None, got[1])


def pass_kernel(given, spot_ref, *refs):
    received_ref, crossed_ref, low_ref = refs[:3]
    outs, sems = refs[given["inputs"]:-1], refs[-1]
    here = spot_ref[0]
    sides, groups = given["sides"], given["groups"]
    inner = jnp.logical_and(here > 0, here < sides - 1)
    low_at, low_count = given["low"], given["count"]
    copies = []
    if given["cross"]:
        copies.append((None, pltpu.make_async_copy(received_ref.at[0:3 * groups], outs[0], sems.at[0])))
    if given["back"]:
        copies.append((inner, pltpu.make_async_copy(crossed_ref.at[0:2 * groups], outs[-1], sems.at[1])))
    if low_count:
        copies.append(
            (
                jnp.logical_not(inner),
                pltpu.make_async_copy(
                    low_ref.at[low_at:low_at + low_count], outs[-1].at[0:low_count], sems.at[2]
                ),
            )
        )
    for act in ("start", "wait"):
        for where, copy in copies:
            if where is None:
                getattr(copy, act)()
            else:
                pl.when(where)(getattr(copy, act))


def pass_on(spot, received, crossed, low, deps, given, plane):
    groups = given["groups"]
    given = dict(given, back=crossed is not None, inputs=3 + len(deps))
    out = []
    if given["cross"]:
        out.append(jax.ShapeDtypeStruct((3 * groups,) + plane, jnp.bfloat16))
    if given["back"]:
        out.append(jax.ShapeDtypeStruct((2 * groups,) + plane, jnp.bfloat16))
    anywhere = pl.BlockSpec(memory_space=pl.ANY)
    operands = [received, crossed if crossed is not None else low, low] + list(deps)
    return pl.pallas_call(
        functools.partial(pass_kernel, given),
        out_shape=out,
        in_specs=[pl.BlockSpec(memory_space=pltpu.SMEM)] + [anywhere] * len(operands),
        out_specs=[anywhere] * len(out),
        scratch_shapes=[pltpu.SemaphoreType.DMA((3,))],
        cost_estimate=pl.CostEstimate(flops=0, bytes_accessed=4 * 2 ** 20, transcendentals=0),
        name="pass_on",
    )(spot, *operands)


def fetch(src, dst, sem):
    pltpu.make_async_copy(src, dst, sem).start()


def expand(source, step, group, groups, tables, spread):
    sides, _, plane, rows, _ = source.shape
    kinds = source.shape[1] // groups
    half = (group + 1) // 2
    mains = (plane - half) // group
    windows = spread[0].shape[0]
    for part, (lo, hi) in enumerate(((0, half), (half, group))):
        if lo == hi:
            continue
        count = hi - lo
        spans = [(main * group + lo, main * group + hi) for main in range(mains)]
        spans.append((mains * group, mains * group + count))
        wide = jnp.concatenate(
            [
                jnp.concatenate(
                    [
                        source[:, kind * groups + step, first:stop].reshape(sides * count * rows, LANES)
                        for first, stop in spans
                    ],
                    axis=1,
                )
                for kind in range(kinds)
            ],
            axis=0,
        )
        for slot, table in enumerate(tables):
            got = jnp.dot(wide, table[part], preferred_element_type=jnp.float32).astype(jnp.bfloat16)
            got = got.reshape(kinds, sides, count, rows, windows * LANES)
            for kind in range(kinds):
                for k in range(count):
                    for a in range(windows):
                        spread[slot + kind][a, :, (lo + k) * LANES:(lo + k + 1) * LANES] = got[
                            kind, :, k, :, a * LANES:(a + 1) * LANES
                        ].reshape(sides * rows, LANES)


def flat(ref):
    windows, rows, lanes = ref.shape
    return ref[...].reshape(windows * rows, lanes)


def even_kernel(sides, group, groups, use_ends, use_inner, starts, spot_ref, *refs):
    views = [ref.at[at:at + 2 * groups] for ref, at in zip(refs[:2 * sides], starts)]
    inner_blocks, end_blocks = views[:sides], views[sides:]
    left_ref, first_ref, last_ref = refs[2 * sides:2 * sides + 3]
    total, even, spread_a, spread_b, sems = refs[-5:]
    here = spot_ref[0]
    step = pl.program_id(0)
    inner = jnp.logical_and(here > 0, here < sides - 1)
    work = jnp.logical_or(jnp.logical_and(inner, use_inner), jnp.logical_and(jnp.logical_not(inner), use_ends))

    @pl.when(work)
    def _():
        @pl.when(step == 0)
        def _():
            total[...] = jnp.zeros_like(total)

            @pl.when(inner)
            def _():
                for at, turn in enumerate((0, 1, 3, 2)):
                    fetch(inner_blocks[at], even.at[here ^ turn], sems.at[at])

            @pl.when(jnp.logical_not(inner))
            def _():
                for at, turn in enumerate((0, 1, 2, 3)):
                    fetch(end_blocks[at], even.at[here ^ turn], sems.at[at])

            for at in range(sides):
                pltpu.make_async_copy(inner_blocks[at], even.at[at], sems.at[at]).wait()

        expand(even, step, group, groups, (left_ref,), (spread_a, spread_b))
        first = first_ref[...].reshape(group * LANES, first_ref.shape[-1])
        last = last_ref[...].reshape(group * LANES, last_ref.shape[-1])
        total[0] += jnp.dot(flat(spread_a), first, preferred_element_type=jnp.float32)
        total[1] += jnp.dot(flat(spread_b), first, preferred_element_type=jnp.float32)
        total[1] += jnp.dot(flat(spread_a), last, preferred_element_type=jnp.float32)

    @pl.when(jnp.logical_and(step == 0, jnp.logical_not(work)))
    def _():
        total[...] = jnp.zeros_like(total)


def even_product(spot, inner_blocks, end_blocks, deps, table, first, last, sides, group, groups):
    some = inner_blocks or end_blocks
    use_inner, use_ends = inner_blocks is not None, end_blocks is not None
    blocks = (inner_blocks or some) + (end_blocks or some)
    starts = [at for _, at in blocks]
    _, planes, rows, _ = some[0][0].shape
    windows = table.shape[2] // LANES
    full = first.shape[-1]
    count = windows * sides * rows
    whole = lambda arr: pl.BlockSpec(arr.shape, lambda g, s: (0,) * len(arr.shape))
    low = pl.BlockSpec((group,) + first.shape[1:], lambda g, s: (g, 0, 0))
    out = jax.ShapeDtypeStruct((2, count, full), jnp.float32)
    depth = groups * group
    flops = 2 * count * depth * LANES * 3 * full + 4 * sides * rows * depth * 3 * LANES * windows * LANES
    return pl.pallas_call(
        functools.partial(even_kernel, sides, group, groups, use_ends, use_inner, starts),
        out_shape=out,
        grid_spec=pltpu.PrefetchScalarGridSpec(
            num_scalar_prefetch=1,
            grid=(groups,),
            in_specs=[pl.BlockSpec(memory_space=pl.ANY)] * (2 * sides)
            + [whole(table), low, low]
            + [pl.BlockSpec(memory_space=pl.ANY)] * len(deps),
            out_specs=whole(out),
            scratch_shapes=[
                pltpu.VMEM((sides, 2 * groups, planes, rows, LANES), jnp.bfloat16),
                pltpu.VMEM((windows, sides * rows, group * LANES), jnp.bfloat16),
                pltpu.VMEM((windows, sides * rows, group * LANES), jnp.bfloat16),
                pltpu.SemaphoreType.DMA((sides,)),
            ],
        ),
        compiler_params=pltpu.CompilerParams(vmem_limit_bytes=40 * 2 ** 20),
        cost_estimate=pl.CostEstimate(flops=flops, bytes_accessed=20 * 2 ** 20, transcendentals=0),
        name="even_product",
    )(spot, *[ref for ref, _ in blocks], table, first, last, *deps)


def odd_kernel(sides, group, groups, outs, starts, spot_ref, *refs):
    blocks = [ref.at[at:at + groups] for ref, at in zip(refs[:sides], starts)]
    inner_part, end_part = refs[sides:sides + 2]
    left_ref, next_left_ref, low_ref, next_low_ref = refs[sides + 2:sides + 6]
    out_refs = refs[-5 - outs:-5]
    odd, spread_a, spread_b, total, sems = refs[-5:]
    here, role = spot_ref[0], spot_ref[1]
    step, last = pl.program_id(0), pl.num_programs(0) - 1
    inner = jnp.logical_and(here > 0, here < sides - 1)

    @pl.when(step == 0)
    def _():
        @pl.when(inner)
        def _():
            fetch(inner_part, total, sems.at[sides])
            for at, turn in enumerate((0, 1, 3, 2)):
                fetch(blocks[at], odd.at[here ^ turn], sems.at[at])
            for at in range(sides):
                pltpu.make_async_copy(blocks[at], odd.at[at], sems.at[at]).wait()

        @pl.when(jnp.logical_not(inner))
        def _():
            fetch(end_part, total, sems.at[sides])

        pltpu.make_async_copy(inner_part, total, sems.at[sides]).wait()

    @pl.when(inner)
    def _():
        expand(odd, step, group, groups, (left_ref, next_left_ref), (spread_a, spread_b))
        low = low_ref[...].reshape(group * LANES, low_ref.shape[-1])
        next_low = next_low_ref[...].reshape(group * LANES, low_ref.shape[-1])
        total[1] += jnp.dot(flat(spread_a), low, preferred_element_type=jnp.float32)
        total[1] += jnp.dot(flat(spread_b), next_low, preferred_element_type=jnp.float32)

    @pl.when(step == last)
    def _():
        for offset in range(outs):
            which = offset ^ role
            value = total[which // 2]
            width = value.shape[1] // 2
            value = jnp.where(which % 2 == 1, value[:, width:], value[:, :width])
            out_refs[offset][...] = value.reshape(out_refs[offset].shape).astype(jnp.bfloat16)


def odd_product(spot, blocks, inner_part, end_part, deps, tables, lows, sides, group, groups, outs):
    starts = [at for _, at in blocks]
    _, planes, rows, _ = blocks[0][0].shape
    table, next_table = tables
    low, next_low = lows
    windows = table.shape[2] // LANES
    full = low.shape[-1]
    count = windows * sides * rows
    whole = lambda arr: pl.BlockSpec(arr.shape, lambda g, s: (0,) * len(arr.shape))
    part = pl.BlockSpec((group,) + low.shape[1:], lambda g, s: (g, 0, 0))
    out = [jax.ShapeDtypeStruct((windows, sides * rows, full // 2), jnp.bfloat16)] * outs
    depth = groups * group
    flops = 2 * count * depth * LANES * 2 * full + 4 * sides * rows * depth * 3 * LANES * windows * LANES
    return pl.pallas_call(
        functools.partial(odd_kernel, sides, group, groups, outs, starts),
        out_shape=out,
        grid_spec=pltpu.PrefetchScalarGridSpec(
            num_scalar_prefetch=1,
            grid=(groups,),
            in_specs=[pl.BlockSpec(memory_space=pl.ANY)] * (sides + 2)
            + [whole(table), whole(next_table), part, part]
            + [pl.BlockSpec(memory_space=pl.ANY)] * len(deps),
            out_specs=[whole(o) for o in out],
            scratch_shapes=[
                pltpu.VMEM((sides, groups, planes, rows, LANES), jnp.bfloat16),
                pltpu.VMEM((windows, sides * rows, group * LANES), jnp.bfloat16),
                pltpu.VMEM((windows, sides * rows, group * LANES), jnp.bfloat16),
                pltpu.VMEM((2, count, full), jnp.float32),
                pltpu.SemaphoreType.DMA((sides + 1,)),
            ],
        ),
        compiler_params=pltpu.CompilerParams(vmem_limit_bytes=40 * 2 ** 20),
        cost_estimate=pl.CostEstimate(flops=flops, bytes_accessed=20 * 2 ** 20, transcendentals=0),
        name="odd_product",
    )(spot, *[ref for ref, _ in blocks], inner_part, end_part, table, next_table, low, next_low, *deps)


def on_device(sizes, tops, bottoms, left_iso, right_iso):
    roles, contrs, sides = sizes
    role = lax.axis_index("role")
    here = lax.axis_index("horiz")
    kinds, depth_all, rows_all, width = tops.shape
    depth = depth_all // roles
    group = group_size(depth)
    groups = depth // group
    share = right_iso.shape[0]
    chunks = split_sizes(rows_all, share)
    unit = share // chunks
    rows = rows_all // chunks
    windows = left_iso.shape[1]
    slab = left_iso.shape[2]
    downs, full = bottoms.shape[3], bottoms.shape[4]
    spot = jnp.stack([here, role]).astype(jnp.int32)

    cut = tops.reshape(kinds, depth_all, contrs, chunks, unit, width)

    def exchange(t, place):
        pieces = []
        for s in range(roles):
            piece = lax.dynamic_slice(
                cut, (0, (place ^ s) * depth, 0, t, 0, 0), (kinds, depth, contrs, 1, unit, width)
            ).reshape(kinds, depth, rows, width)
            if s:
                piece = lax.ppermute(piece, "role", [(j, j ^ s) for j in range(roles)])
            pieces.append(piece)
        return pieces

    def lower(kind, place):
        low = lax.dynamic_slice_in_dim(bottoms[kind], place * depth, depth, 0)
        return low.reshape(depth, slab, downs * full)

    def padded(low):
        return jnp.pad(low, ((0, 0), (0, LANES - slab), (0, 0)))

    pairs = [(z, z ^ 1) for z in range(sides)]
    hand = [(z, z ^ 1) for z in (0, sides - 1)]
    cross = [(z, z ^ 3) for z in range(1, sides - 1)]
    move = lambda value, perm: lax.ppermute(value, "horiz", perm)

    pieces = {0: exchange(0, role)}
    left_all = jnp.concatenate(
        [lax.dynamic_slice_in_dim(left_iso, (role ^ s) * width, width, 0) for s in range(roles)], axis=0
    )
    total = left_all.shape[0]
    mains = total // LANES
    rest = total - mains * LANES
    plane = (mains * group + (group + 1) // 2, rows, LANES)

    def table(flat_left):
        wide = jnp.pad(
            flat_left.reshape(total, windows, slab), ((0, 0), (0, 0), (0, LANES - slab))
        ).reshape(total, windows * LANES)
        first = jnp.pad(wide, ((0, LANES - rest), (0, 0)))
        blank = jnp.zeros((rest, windows * LANES), wide.dtype)
        second = jnp.concatenate([wide[:mains * LANES], blank, wide[mains * LANES:]], axis=0)
        second = jnp.pad(second, ((0, LANES - 2 * rest), (0, 0)))
        return jnp.stack([first, second])

    flat_left = left_all.reshape(total, windows * slab)
    middle = lower(1, role) * jnp.asarray(2, bottoms.dtype)
    tiles = (slab // rows, downs * full // LANES)
    count = depth * tiles[0] * tiles[1]
    units = -(-count // plane[0])
    carried = middle.reshape(depth, tiles[0], rows, tiles[1], LANES).transpose(0, 1, 3, 2, 4)
    carried = jnp.pad(carried.reshape(count, rows, LANES), ((0, units * plane[0] - count), (0, 0), (0, 0)))
    carried = carried.reshape((units,) + plane)
    taken = 0

    def take(most):
        nonlocal taken
        at, size = taken, min(most, units - taken)
        taken += size
        return at, size

    own, sent, straight, turned, last = {}, {}, {}, {}, {}
    sums, shares, reduced = {}, {}, {}
    parts = []
    lows = tables = next_low = None
    done = None

    def reduce_roles(t):
        summed = shares[t][0].astype(jnp.float32)
        for s in range(1, roles):
            got = lax.ppermute(shares[t][s], "role", [(j, j ^ s) for j in range(roles)])
            summed = summed + got.astype(jnp.float32)
        summed = summed.reshape(windows, sides * contrs, unit, full)
        size = sides * contrs
        step = contrs // 2
        place = lax.axis_index("contr")
        while step:
            size //= 2
            bit = (place // step) % 2
            keep = lax.dynamic_slice_in_dim(summed, bit * size, size, 1)
            give = lax.dynamic_slice_in_dim(summed, (1 - bit) * size, size, 1).astype(jnp.bfloat16)
            got = lax.ppermute(give, "contr", [(j, j ^ step) for j in range(contrs)])
            summed = keep + got.astype(jnp.float32)
            step //= 2
        return summed

    for r in range(chunks + 3):
        if r <= chunks:
            fresh = r < chunks
            base = 3 * groups if fresh else 0
            extra = {0: 2, 1: 3}.get(r, 1) * groups if fresh else 0
            at, size = take(extra)
            length = max(base + size, 4 * groups) if fresh else 2 * groups
            given = dict(
                sides=sides, groups=groups, back=2 * groups if fresh else 0, kind=base, low=at, count=size
            )
            deps = [sent[r - 1]] if r else []
            deps += [sums[r - 1]] if r - 1 in sums else []
            out, mine, mark = pack(
                spot, pieces.pop(r) if fresh else [], straight.get(r - 1), carried, deps, given, group,
                plane, length,
            )
            sent[r] = move(out, pairs)
            if size:
                parts.append((at, sent[r], base, size))
            if fresh:
                own[r] = mine
                straight[r] = move(mine, cross)
            done = out
            for t in {0: (1, 2), 1: (3,), 2: (4,)}.get(r, (r + 2,)):
                if t < chunks:
                    pieces[t] = exchange(t, mark[1])
            if r == 0:
                late = mark[1]
                lows = (padded(lower(0, late)), padded(lower(2, late)), padded(middle))
                tables = (table(flat_left), table(move(flat_left, hand)))
        t = r - 4
        if 0 <= t < chunks:
            if next_low is None:
                arrived = [got[first:first + size] for _, got, first, size in sorted(parts, key=lambda p: p[0])]
                arrived = jnp.concatenate(arrived, axis=0).reshape(-1, rows, LANES)[:count]
                arrived = arrived.reshape(depth, tiles[0], tiles[1], rows, LANES).transpose(0, 1, 3, 2, 4)
                next_low = padded(arrived.reshape(depth, slab, downs * full))
            blocks = [(own[t], 2 * groups), (sent[t], 2 * groups), (straight[t], 2 * groups), (turned[t + 1], 2 * groups)]
            shares[t] = odd_product(
                spot, blocks, sums[t + 2], sums[t + 3], [done], tables, (lows[2], next_low),
                sides, group, groups, roles,
            )
            done = shares[t][0]
        if 1 <= r <= chunks + 1:
            at, size = take(2 * groups) if 2 <= r else (0, 0)
            given = dict(sides=sides, groups=groups, cross=r <= chunks, low=at, count=size)
            deps = [done] + ([last[r - 1]] if r - 1 in last else [])
            if r - 5 in shares:
                reduced[r - 5] = reduce_roles(r - 5)
                deps.append(reduced[r - 5])
            outs = pass_on(spot, sent[r - 1], turned.get(r - 1), carried, deps, given, plane)
            if r <= chunks:
                turned[r] = move(outs[0], cross)
            if r - 1 in turned:
                last[r] = move(outs[-1], pairs)
                if size:
                    parts.append((at, last[r], 0, size))
            done = outs[0]
        if r >= 2:
            t = r - 2
            inner_blocks = end_blocks = None
            if t < chunks:
                inner_blocks = [(own[t], 0), (sent[t], 0), (straight[t], 0), (turned[t + 1], 0)]
            t = r - 3
            if 0 <= t:
                end_blocks = [
                    (own[t], 0), (sent[t], 0), (sent[t + 1], 2 * groups if t + 1 < chunks else 0), (last[t + 2], 0)
                ]
            sums[r] = even_product(
                spot, inner_blocks, end_blocks, [done], tables[0], lows[0], lows[1], sides, group, groups
            )
            done = sums[r]
    t = chunks - 1
    blocks = [(own[t], 2 * groups), (sent[t], 2 * groups), (straight[t], 2 * groups), (turned[t + 1], 2 * groups)]
    shares[t] = odd_product(
        spot, blocks, sums[t + 2], sums[t + 3], [done], tables, (lows[2], next_low), sides, group, groups, roles
    )

    for t in range(chunks):
        if t not in reduced:
            reduced[t] = reduce_roles(t)
    summed = jnp.concatenate([reduced[t] for t in range(chunks)], axis=2)
    mine = lax.dynamic_slice_in_dim(summed, here, 1, 1)
    for s in range(1, sides):
        give = lax.dynamic_slice_in_dim(summed, here ^ s, 1, 1).astype(jnp.bfloat16)
        got = lax.ppermute(give, "horiz", [(z, z ^ s) for z in range(sides)])
        mine = mine + got.astype(jnp.float32)
    mine = mine.reshape(windows, share, full).astype(jnp.bfloat16)
    projected = jnp.einsum("aur,urb->ab", mine, right_iso, preferred_element_type=jnp.float32)
    projected = projected * jnp.where(role >= downs, 0.25, 1.0)
    for axis, size in (("contr", contrs), ("horiz", sides)):
        s = 1
        while s < size:
            projected = projected + lax.ppermute(projected, axis, [(j, j ^ s) for j in range(size)])
            s *= 2
    found = [projected] + [
        lax.ppermute(projected, "role", [(j, j ^ s) for j in range(roles)]) for s in range(1, roles)
    ]
    found = jnp.stack(found)
    order = [lax.dynamic_index_in_dim(found, q ^ role, 0, keepdims=False) for q in range(roles)]
    return jnp.stack(order).reshape(roles // downs, downs, windows, -1)


def solution(mesh):
    placed = (
        P(None, "contr", "horiz", "role"),
        P(None, "contr", "horiz", None, None),
        P(None, None, "horiz"),
        P(("contr", "horiz"), None, None),
    )
    sizes = tuple(mesh.shape[axis] for axis in ("role", "contr", "horiz"))
    body = functools.partial(on_device, sizes)
    return jax.shard_map(body, mesh=mesh, in_specs=placed, out_specs=P(), check_vma=False)
```

```python
import functools

import jax
import jax.numpy as jnp
from jax import lax
from jax.experimental import pallas as pl
from jax.experimental.pallas import tpu as pltpu
from jax.sharding import PartitionSpec as P

LANES = 128
ROWS = 16


def split_sizes(total, count):
    best = 1
    for n in range(1, count + 1):
        if count % n == 0 and total % n == 0 and (total // n) % ROWS == 0:
            best = n
    return best


def group_size(depth):
    best = depth
    for size in range(2, 21, 2):
        if depth % size == 0:
            best = size
    return best


def pack_kernel(group, parts, given, spot_ref, *refs):
    pieces, crossed_ref, low_ref = refs[:parts], refs[parts], refs[parts + 1]
    sent_ref, own_ref, mark_ref, sem = refs[-4:] if parts else (refs[-3], None, refs[-2], refs[-1])
    here = spot_ref[0]
    sides = given["sides"]
    inner = jnp.logical_and(here > 0, here < sides - 1)
    groups, back_at, low_at, low_count, kind_at = (
        given["groups"], given["back"], given["low"], given["count"], given["kind"]
    )
    mark_ref[0] = spot_ref[0]
    mark_ref[1] = spot_ref[1]

    def back():
        return pltpu.make_async_copy(
            crossed_ref.at[0:2 * groups], sent_ref.at[back_at:back_at + 2 * groups], sem
        )

    def lower():
        return pltpu.make_async_copy(
            low_ref.at[low_at:low_at + low_count], sent_ref.at[kind_at:kind_at + low_count], sem
        )

    if given["has_back"]:
        @pl.when(inner)
        def _():
            back().start()
    if low_count:
        @pl.when(jnp.logical_not(inner))
        def _():
            lower().start()

    if parts:
        kinds, depth, rows, width = pieces[0].shape
        total = width * parts
        mains = total // LANES
        rest = total - mains * LANES
        half = (group + 1) // 2

        def place(slot, shift):
            shape = (width, (mains + 1) * LANES)
            target = slot * width + lax.broadcasted_iota(jnp.int32, shape, 0)
            target = jnp.where(target >= mains * LANES, target + shift, target)
            hit = lax.broadcasted_iota(jnp.int32, shape, 1) == target
            return jnp.where(hit, 1.0, 0.0).astype(jnp.bfloat16)

        tables = [[place(s, shift) for s in range(parts)] for shift in (0, rest)]
        for kind in range(kinds):
            base = (0, 2, 1)[kind] * groups

            def put(lo, hi, value):
                value = value.astype(jnp.bfloat16)
                own_ref[base:base + groups, lo:hi] = value
                if kind != 1:
                    sent_ref[base:base + groups, lo:hi] = value
                else:
                    @pl.when(jnp.logical_not(inner))
                    def _():
                        sent_ref[base:base + groups, lo:hi] = value

            tails = []
            for part, (lo, hi) in enumerate(((0, half), (half, group))):
                if lo == hi:
                    continue
                got = 0.0
                for slot, ref in enumerate(pieces):
                    block = ref[kind].reshape(groups, group, rows, width)[:, lo:hi]
                    got = got + jnp.dot(
                        block.reshape(groups * (hi - lo) * rows, width),
                        tables[part][slot],
                        preferred_element_type=jnp.float32,
                    )
                got = got.reshape(groups, hi - lo, rows, (mains + 1) * LANES)
                for main in range(mains):
                    put(main * group + lo, main * group + hi, got[..., main * LANES:(main + 1) * LANES])
                tails.append(got[..., mains * LANES:])
            start = mains * group
            first = tails[0]
            if len(tails) == 1:
                put(start, start + half, first)
            else:
                both = tails[1].shape[1]
                put(start, start + both, first[:, :both] + tails[1])
                if both < half:
                    put(start + both, start + half, first[:, both:])

    if given["has_back"]:
        @pl.when(inner)
        def _():
            back().wait()
    if low_count:
        @pl.when(jnp.logical_not(inner))
        def _():
            lower().wait()


def pack(spot, pieces, crossed, low, deps, given, group, plane, length):
    has_back = crossed is not None
    given = dict(given, has_back=has_back)
    groups = given["groups"]
    out = [jax.ShapeDtypeStruct((length,) + plane, jnp.bfloat16)]
    specs = [pl.BlockSpec(memory_space=pltpu.VMEM)]
    if pieces:
        out.append(jax.ShapeDtypeStruct((3 * groups,) + plane, jnp.bfloat16))
        specs.append(pl.BlockSpec(memory_space=pltpu.VMEM))
    out.append(jax.ShapeDtypeStruct((2,), jnp.int32))
    specs.append(pl.BlockSpec(memory_space=pltpu.SMEM))
    anywhere = pl.BlockSpec(memory_space=pl.ANY)
    operands = [crossed if has_back else low, low] + list(deps)
    got = pl.pallas_call(
        functools.partial(pack_kernel, group, len(pieces), given),
        out_shape=out,
        in_specs=[pl.BlockSpec(memory_space=pltpu.SMEM)]
        + [pl.BlockSpec(memory_space=pltpu.VMEM)] * len(pieces)
        + [anywhere] * len(operands),
        out_specs=specs,
        scratch_shapes=[pltpu.SemaphoreType.DMA],
        compiler_params=pltpu.CompilerParams(vmem_limit_bytes=32 * 2 ** 20),
        cost_estimate=pl.CostEstimate(flops=2 * 10 ** 9, bytes_accessed=6 * 2 ** 20, transcendentals=0),
        name="pack",
    )(spot, *pieces, *operands)
    return (got[0], got[1], got[2]) if pieces else (got[0], None, got[1])


def pass_kernel(given, spot_ref, *refs):
    received_ref, crossed_ref, low_ref = refs[:3]
    outs, sems = refs[given["inputs"]:-1], refs[-1]
    here = spot_ref[0]
    sides, groups = given["sides"], given["groups"]
    inner = jnp.logical_and(here > 0, here < sides - 1)
    low_at, low_count = given["low"], given["count"]
    copies = []
    if given["cross"]:
        copies.append((None, pltpu.make_async_copy(received_ref.at[0:3 * groups], outs[0], sems.at[0])))
    if given["back"]:
        copies.append((inner, pltpu.make_async_copy(crossed_ref.at[0:2 * groups], outs[-1], sems.at[1])))
    if low_count:
        copies.append(
            (
                jnp.logical_not(inner),
                pltpu.make_async_copy(
                    low_ref.at[low_at:low_at + low_count], outs[-1].at[0:low_count], sems.at[2]
                ),
            )
        )
    for act in ("start", "wait"):
        for where, copy in copies:
            if where is None:
                getattr(copy, act)()
            else:
                pl.when(where)(getattr(copy, act))


def pass_on(spot, received, crossed, low, deps, given, plane):
    groups = given["groups"]
    given = dict(given, back=crossed is not None, inputs=3 + len(deps))
    out = []
    if given["cross"]:
        out.append(jax.ShapeDtypeStruct((3 * groups,) + plane, jnp.bfloat16))
    if given["back"]:
        out.append(jax.ShapeDtypeStruct((2 * groups,) + plane, jnp.bfloat16))
    anywhere = pl.BlockSpec(memory_space=pl.ANY)
    operands = [received, crossed if crossed is not None else low, low] + list(deps)
    return pl.pallas_call(
        functools.partial(pass_kernel, given),
        out_shape=out,
        in_specs=[pl.BlockSpec(memory_space=pltpu.SMEM)] + [anywhere] * len(operands),
        out_specs=[pl.BlockSpec(memory_space=pltpu.VMEM)] * len(out),
        scratch_shapes=[pltpu.SemaphoreType.DMA((3,))],
        compiler_params=pltpu.CompilerParams(vmem_limit_bytes=32 * 2 ** 20),
        cost_estimate=pl.CostEstimate(flops=0, bytes_accessed=4 * 2 ** 20, transcendentals=0),
        name="pass_on",
    )(spot, *operands)


def fetch(src, dst, sem):
    pltpu.make_async_copy(src, dst, sem).start()


def expand(source, step, group, groups, tables, spread):
    sides, _, plane, rows, _ = source.shape
    kinds = source.shape[1] // groups
    half = (group + 1) // 2
    mains = (plane - half) // group
    windows = spread.shape[1]
    for part, (lo, hi) in enumerate(((0, half), (half, group))):
        if lo == hi:
            continue
        count = hi - lo
        spans = [(main * group + lo, main * group + hi) for main in range(mains)]
        spans.append((mains * group, mains * group + count))
        wide = jnp.concatenate(
            [
                jnp.concatenate(
                    [
                        source[:, kind * groups + step, first:stop].reshape(sides * count * rows, LANES)
                        for first, stop in spans
                    ],
                    axis=1,
                )
                for kind in range(kinds)
            ],
            axis=0,
        )
        for slot, table in enumerate(tables):
            got = jnp.dot(wide, table[part], preferred_element_type=jnp.float32).astype(jnp.bfloat16)
            got = got.reshape(kinds, sides, count, rows, windows * LANES)
            for kind in range(kinds):
                for k in range(count):
                    for a in range(windows):
                        spread[slot + kind, a, :, (lo + k) * LANES:(lo + k + 1) * LANES] = got[
                            kind, :, k, :, a * LANES:(a + 1) * LANES
                        ].reshape(sides * rows, LANES)


def set_tables(ref, table_ref, rest):
    total, lanes = table_ref.shape
    mains = total - rest
    ref[...] = jnp.zeros_like(ref)
    for part in range(2):
        ref[part, 0:mains] = table_ref[0:mains]
        ref[part, mains + part * rest:mains + (part + 1) * rest] = table_ref[mains:total]


def set_low(ref, low_ref):
    for k in range(low_ref.shape[0]):
        ref[k * LANES:k * LANES + low_ref.shape[1]] = low_ref[k]


def set_low_planes(ref, low_ref, depth, tiles):
    rows = low_ref.shape[-2]
    for k in range(depth):
        for i in range(tiles[0]):
            for j in range(tiles[1]):
                ref[k * LANES + i * rows:k * LANES + (i + 1) * rows, j * LANES:(j + 1) * LANES] = low_ref[
                    (k * tiles[0] + i) * tiles[1] + j
                ]


def even_kernel(sides, group, groups, use_ends, use_inner, starts, spot_ref, *refs):
    views = [ref.at[at:at + 2 * groups] for ref, at in zip(refs[:2 * sides], starts)]
    inner_blocks, end_blocks = views[:sides], views[sides:]
    left_ref, first_ref, last_ref = refs[2 * sides:2 * sides + 3]
    total, even, spread, tables, first, last, sems = refs[-7:]
    here = spot_ref[0]
    step = pl.program_id(0)
    inner = jnp.logical_and(here > 0, here < sides - 1)
    work = jnp.logical_or(jnp.logical_and(inner, use_inner), jnp.logical_and(jnp.logical_not(inner), use_ends))

    @pl.when(work)
    def _():
        @pl.when(step == 0)
        def _():
            @pl.when(inner)
            def _():
                for at, turn in enumerate((0, 1, 3, 2)):
                    fetch(inner_blocks[at], even.at[here ^ turn], sems.at[at])

            @pl.when(jnp.logical_not(inner))
            def _():
                for at, turn in enumerate((0, 1, 2, 3)):
                    fetch(end_blocks[at], even.at[here ^ turn], sems.at[at])

            total[...] = jnp.zeros_like(total)
            first[...] = jnp.zeros_like(first)
            last[...] = jnp.zeros_like(last)
            set_tables(tables, left_ref, tables.shape[1] - left_ref.shape[0])
            for at in range(sides):
                pltpu.make_async_copy(inner_blocks[at], even.at[at], sems.at[at]).wait()

        expand(even, step, group, groups, (tables,), spread)
        set_low(first, first_ref)
        set_low(last, last_ref)
        count = spread.shape[1] * spread.shape[2]
        both = spread[...].reshape(2 * count, group * LANES)
        total[...] += jnp.dot(both, first[...], preferred_element_type=jnp.float32).reshape(total.shape)
        total[1] += jnp.dot(both[:count], last[...], preferred_element_type=jnp.float32)

    @pl.when(jnp.logical_and(step == 0, jnp.logical_not(work)))
    def _():
        total[...] = jnp.zeros_like(total)


def even_product(spot, inner_blocks, end_blocks, deps, table, first, last, sides, group, groups):
    some = inner_blocks or end_blocks
    use_inner, use_ends = inner_blocks is not None, end_blocks is not None
    blocks = (inner_blocks or some) + (end_blocks or some)
    starts = [at for _, at in blocks]
    _, planes, rows, _ = some[0][0].shape
    windows = table.shape[1] // LANES
    full = first.shape[-1]
    count = windows * sides * rows
    whole = lambda arr: pl.BlockSpec(arr.shape, lambda g, s: (0,) * len(arr.shape))
    low = pl.BlockSpec((group,) + first.shape[1:], lambda g, s: (g, 0, 0))
    out = jax.ShapeDtypeStruct((2, count, full), jnp.float32)
    depth = groups * group
    flops = 2 * count * depth * LANES * 3 * full + 4 * sides * rows * depth * 3 * LANES * windows * LANES
    return pl.pallas_call(
        functools.partial(even_kernel, sides, group, groups, use_ends, use_inner, starts),
        out_shape=out,
        grid_spec=pltpu.PrefetchScalarGridSpec(
            num_scalar_prefetch=1,
            grid=(groups,),
            in_specs=[pl.BlockSpec(memory_space=pl.ANY)] * (2 * sides)
            + [whole(table), low, low]
            + [pl.BlockSpec(memory_space=pl.ANY)] * len(deps),
            out_specs=whole(out),
            scratch_shapes=[
                pltpu.VMEM((sides, 2 * groups, planes, rows, LANES), jnp.bfloat16),
                pltpu.VMEM((2, windows, sides * rows, group * LANES), jnp.bfloat16),
                pltpu.VMEM((2, -(-table.shape[0] // LANES) * LANES, table.shape[1]), jnp.bfloat16),
                pltpu.VMEM((group * LANES, full), jnp.bfloat16),
                pltpu.VMEM((group * LANES, full), jnp.bfloat16),
                pltpu.SemaphoreType.DMA((sides,)),
            ],
        ),
        compiler_params=pltpu.CompilerParams(vmem_limit_bytes=56 * 2 ** 20),
        cost_estimate=pl.CostEstimate(flops=flops, bytes_accessed=20 * 2 ** 20, transcendentals=0),
        name="even_product",
    )(spot, *[ref for ref, _ in blocks], table, first, last, *deps)


def odd_kernel(sides, group, groups, outs, tiles, starts, spot_ref, *refs):
    blocks = [ref.at[at:at + groups] for ref, at in zip(refs[:sides], starts)]
    inner_part, end_part = refs[sides:sides + 2]
    left_ref, next_left_ref, low_ref, next_low_ref = refs[sides + 2:sides + 6]
    out_refs = refs[-8 - outs:-8]
    odd, spread, tables, next_tables, low, next_low, total, sems = refs[-8:]
    here, role = spot_ref[0], spot_ref[1]
    step, last = pl.program_id(0), pl.num_programs(0) - 1
    inner = jnp.logical_and(here > 0, here < sides - 1)

    @pl.when(step == 0)
    def _():
        @pl.when(inner)
        def _():
            fetch(inner_part, total, sems.at[sides])
            for at, turn in enumerate((0, 1, 3, 2)):
                fetch(blocks[at], odd.at[here ^ turn], sems.at[at])
            low[...] = jnp.zeros_like(low)
            next_low[...] = jnp.zeros_like(next_low)
            set_tables(tables, left_ref, tables.shape[1] - left_ref.shape[0])
            set_tables(next_tables, next_left_ref, tables.shape[1] - left_ref.shape[0])
            for at in range(sides):
                pltpu.make_async_copy(blocks[at], odd.at[at], sems.at[at]).wait()

        @pl.when(jnp.logical_not(inner))
        def _():
            fetch(end_part, total, sems.at[sides])

        pltpu.make_async_copy(inner_part, total, sems.at[sides]).wait()

    @pl.when(inner)
    def _():
        expand(odd, step, group, groups, (tables, next_tables), spread)
        set_low_planes(low, low_ref, group, tiles)
        set_low_planes(next_low, next_low_ref, group, tiles)
        count = spread.shape[1] * spread.shape[2]
        rows = spread[...].reshape(2, count, group * LANES)
        total[1] += jnp.dot(rows[0], low[...], preferred_element_type=jnp.float32)
        total[1] += jnp.dot(rows[1], next_low[...], preferred_element_type=jnp.float32)

    @pl.when(step == last)
    def _():
        for offset in range(outs):
            which = offset ^ role
            value = total[which // 2]
            width = value.shape[1] // 2
            value = jnp.where(which % 2 == 1, value[:, width:], value[:, :width])
            out_refs[offset][...] = value.reshape(out_refs[offset].shape).astype(jnp.bfloat16)


def odd_product(spot, blocks, inner_part, end_part, deps, tables, lows, sides, group, groups, outs, tiles):
    starts = [at for _, at in blocks]
    _, planes, rows, _ = blocks[0][0].shape
    table, next_table = tables
    low, next_low = lows
    windows = table.shape[1] // LANES
    full = tiles[1] * LANES
    count = windows * sides * rows
    whole = lambda arr: pl.BlockSpec(arr.shape, lambda g, s: (0,) * len(arr.shape))
    part = pl.BlockSpec((group * tiles[0] * tiles[1],) + low.shape[1:], lambda g, s: (g, 0, 0))
    out = [jax.ShapeDtypeStruct((windows, sides * rows, full // 2), jnp.bfloat16)] * outs
    depth = groups * group
    flops = 2 * count * depth * LANES * 2 * full + 4 * sides * rows * depth * 3 * LANES * windows * LANES
    return pl.pallas_call(
        functools.partial(odd_kernel, sides, group, groups, outs, tiles, starts),
        out_shape=out,
        grid_spec=pltpu.PrefetchScalarGridSpec(
            num_scalar_prefetch=1,
            grid=(groups,),
            in_specs=[pl.BlockSpec(memory_space=pl.ANY)] * (sides + 2)
            + [whole(table), whole(next_table), part, part]
            + [pl.BlockSpec(memory_space=pl.ANY)] * len(deps),
            out_specs=[whole(o) for o in out],
            scratch_shapes=[
                pltpu.VMEM((sides, groups, planes, rows, LANES), jnp.bfloat16),
                pltpu.VMEM((2, windows, sides * rows, group * LANES), jnp.bfloat16),
                pltpu.VMEM((2, -(-table.shape[0] // LANES) * LANES, table.shape[1]), jnp.bfloat16),
                pltpu.VMEM((2, -(-table.shape[0] // LANES) * LANES, table.shape[1]), jnp.bfloat16),
                pltpu.VMEM((group * LANES, full), jnp.bfloat16),
                pltpu.VMEM((group * LANES, full), jnp.bfloat16),
                pltpu.VMEM((2, count, full), jnp.float32),
                pltpu.SemaphoreType.DMA((sides + 1,)),
            ],
        ),
        compiler_params=pltpu.CompilerParams(vmem_limit_bytes=56 * 2 ** 20),
        cost_estimate=pl.CostEstimate(flops=flops, bytes_accessed=20 * 2 ** 20, transcendentals=0),
        name="odd_product",
    )(spot, *[ref for ref, _ in blocks], inner_part, end_part, table, next_table, low, next_low, *deps)


def on_device(sizes, tops, bottoms, left_iso, right_iso):
    roles, contrs, sides = sizes
    role = lax.axis_index("role")
    here = lax.axis_index("horiz")
    kinds, depth_all, rows_all, width = tops.shape
    depth = depth_all // roles
    group = group_size(depth)
    groups = depth // group
    share = right_iso.shape[0]
    chunks = split_sizes(rows_all, share)
    unit = share // chunks
    rows = rows_all // chunks
    windows = left_iso.shape[1]
    slab = left_iso.shape[2]
    downs, full = bottoms.shape[3], bottoms.shape[4]
    spot = jnp.stack([here, role]).astype(jnp.int32)

    cut = tops.reshape(kinds, depth_all, contrs, chunks, unit, width)

    def exchange(t, place):
        pieces = []
        for s in range(roles):
            piece = lax.dynamic_slice(
                cut, (0, (place ^ s) * depth, 0, t, 0, 0), (kinds, depth, contrs, 1, unit, width)
            ).reshape(kinds, depth, rows, width)
            if s:
                piece = lax.ppermute(piece, "role", [(j, j ^ s) for j in range(roles)])
            pieces.append(piece)
        return pieces

    def lower(kind, place):
        low = lax.dynamic_slice(
            bottoms, (kind, place * depth, 0, 0, 0), (1, depth, slab, downs, full)
        )
        return low.reshape(depth, slab, downs * full)

    pairs = [(z, z ^ 1) for z in range(sides)]
    hand = [(z, z ^ 1) for z in (0, sides - 1)]
    cross = [(z, z ^ 3) for z in range(1, sides - 1)]
    move = lambda value, perm: lax.ppermute(value, "horiz", perm)

    pieces = {0: exchange(0, role)}
    left_all = jnp.concatenate(
        [lax.dynamic_slice_in_dim(left_iso, (role ^ s) * width, width, 0) for s in range(roles)], axis=0
    )
    total = left_all.shape[0]
    mains = total // LANES
    rest = total - mains * LANES
    plane = (mains * group + (group + 1) // 2, rows, LANES)

    def table(flat_left):
        wide = flat_left.reshape(total, windows, slab)
        return jnp.pad(wide, ((0, 0), (0, 0), (0, LANES - slab))).reshape(total, windows * LANES)

    flat_left = left_all.reshape(total, windows * slab)
    middle = lower(1, role) * jnp.asarray(2, bottoms.dtype)
    tiles = (slab // rows, downs * full // LANES)
    count = depth * tiles[0] * tiles[1]
    units = -(-count // plane[0])
    carried = middle.reshape(depth, tiles[0], rows, tiles[1], LANES).transpose(0, 1, 3, 2, 4)
    carried = middle_planes = carried.reshape(count, rows, LANES)
    carried = jnp.pad(carried, ((0, units * plane[0] - count), (0, 0), (0, 0)))
    carried = carried.reshape((units,) + plane)
    taken = 0

    def take(most):
        nonlocal taken
        at, size = taken, min(most, units - taken)
        taken += size
        return at, size

    own, sent, straight, turned, last = {}, {}, {}, {}, {}
    sums, shares, reduced = {}, {}, {}
    parts = []
    lows = tables = next_low = None
    done = None

    def reduce(t):
        ones = [lax.ppermute(shares[t][s], "role", [(j, j ^ 1) for j in range(roles)]) for s in (1, 3)]
        kept = [shares[t][s].astype(jnp.float32) + got.astype(jnp.float32) for s, got in zip((0, 2), ones)]
        got = lax.ppermute(kept[1].astype(jnp.bfloat16), "role", [(j, j ^ 2) for j in range(roles)])
        summed = kept[0] + got.astype(jnp.float32)
        summed = summed.reshape(windows, sides * contrs, unit, full)
        size = sides * contrs
        step = contrs // 2
        place = lax.axis_index("contr")
        while step:
            size //= 2
            bit = (place // step) % 2
            keep = lax.dynamic_slice_in_dim(summed, bit * size, size, 1)
            give = lax.dynamic_slice_in_dim(summed, (1 - bit) * size, size, 1).astype(jnp.bfloat16)
            got = lax.ppermute(give, "contr", [(j, j ^ step) for j in range(contrs)])
            summed = keep + got.astype(jnp.float32)
            step //= 2
        mine = lax.dynamic_slice_in_dim(summed, here, 1, 1)
        for s in range(1, sides):
            give = lax.dynamic_slice_in_dim(summed, here ^ s, 1, 1).astype(jnp.bfloat16)
            got = lax.ppermute(give, "horiz", [(z, z ^ s) for z in range(sides)])
            mine = mine + got.astype(jnp.float32)
        mine = mine.reshape(windows, unit, full).astype(jnp.bfloat16)
        return jnp.einsum(
            "aur,urb->ab", mine, right_iso[t * unit:(t + 1) * unit], preferred_element_type=jnp.float32
        )

    for r in range(chunks + 3):
        if r <= chunks:
            fresh = r < chunks
            base = 3 * groups if fresh else 0
            extra = {0: 2, 1: 3}.get(r, 1) * groups if fresh else 0
            at, size = take(extra)
            length = max(base + size, 4 * groups) if fresh else 2 * groups
            given = dict(
                sides=sides, groups=groups, back=2 * groups if fresh else 0, kind=base, low=at, count=size
            )
            deps = [sent[r - 1]] if r else []
            deps += [sums[r - 1]] if r - 1 in sums else []
            out, mine, mark = pack(
                spot, pieces.pop(r) if fresh else [], straight.get(r - 1), carried, deps, given, group,
                plane, length,
            )
            sent[r] = move(out, pairs)
            if size:
                parts.append((at, sent[r], base, size))
            if fresh:
                own[r] = mine
                straight[r] = move(mine, cross)
            done = out
            for t in {0: (1, 2), 1: (3,), 2: (4,)}.get(r, (r + 2,)):
                if t < chunks:
                    pieces[t] = exchange(t, mark[1])
            if r == 0:
                late = mark[1]
                lows = (lower(0, late), lower(2, late))
                tables = (table(flat_left), table(move(flat_left, hand)))
        t = r - 4
        if 0 <= t < chunks:
            if next_low is None:
                arrived = [got[first:first + size] for _, got, first, size in sorted(parts, key=lambda p: p[0])]
                next_low = jnp.concatenate(arrived, axis=0).reshape(-1, rows, LANES)
            blocks = [(own[t], 2 * groups), (sent[t], 2 * groups), (straight[t], 2 * groups), (turned[t + 1], 2 * groups)]
            shares[t] = odd_product(
                spot, blocks, sums[t + 2], sums[t + 3], [done], tables, (middle_planes, next_low),
                sides, group, groups, roles, tiles,
            )
            done = shares[t][0]
        if 1 <= r <= chunks + 1:
            at, size = take(2 * groups) if 2 <= r else (0, 0)
            given = dict(sides=sides, groups=groups, cross=r <= chunks, low=at, count=size)
            deps = [done] + ([last[r - 1]] if r - 1 in last else [])
            if r - 5 in shares:
                reduced[r - 5] = reduce(r - 5)
                deps.append(reduced[r - 5])
            outs = pass_on(spot, sent[r - 1], turned.get(r - 1), carried, deps, given, plane)
            if r <= chunks:
                turned[r] = move(outs[0], cross)
            if r - 1 in turned:
                last[r] = move(outs[-1], pairs)
                if size:
                    parts.append((at, last[r], 0, size))
            done = outs[0]
        if r >= 2:
            t = r - 2
            inner_blocks = end_blocks = None
            if t < chunks:
                inner_blocks = [(own[t], 0), (sent[t], 0), (straight[t], 0), (turned[t + 1], 0)]
            t = r - 3
            if 0 <= t:
                end_blocks = [
                    (own[t], 0), (sent[t], 0), (sent[t + 1], 2 * groups if t + 1 < chunks else 0), (last[t + 2], 0)
                ]
            sums[r] = even_product(
                spot, inner_blocks, end_blocks, [done], tables[0], lows[0], lows[1], sides, group, groups
            )
            done = sums[r]
    t = chunks - 1
    blocks = [(own[t], 2 * groups), (sent[t], 2 * groups), (straight[t], 2 * groups), (turned[t + 1], 2 * groups)]
    shares[t] = odd_product(
        spot, blocks, sums[t + 2], sums[t + 3], [done], tables, (middle_planes, next_low), sides, group, groups, roles,
        tiles,
    )

    projected = 0.0
    for t in range(chunks):
        projected = projected + (reduced[t] if t in reduced else reduce(t))
    projected = projected * jnp.where(role >= downs, 0.25, 1.0)
    for axis, size in (("contr", contrs), ("horiz", sides)):
        s = 1
        while s < size:
            projected = projected + lax.ppermute(projected, axis, [(j, j ^ s) for j in range(size)])
            s *= 2
    found = [projected] + [
        lax.ppermute(projected, "role", [(j, j ^ s) for j in range(roles)]) for s in range(1, roles)
    ]
    found = jnp.stack(found)
    order = [lax.dynamic_index_in_dim(found, q ^ role, 0, keepdims=False) for q in range(roles)]
    return jnp.stack(order).reshape(roles // downs, downs, windows, -1)


def solution(mesh):
    placed = (
        P(None, "contr", "horiz", "role"),
        P(None, "contr", "horiz", None, None),
        P(None, None, "horiz"),
        P(("contr", "horiz"), None, None),
    )
    sizes = tuple(mesh.shape[axis] for axis in ("role", "contr", "horiz"))
    body = functools.partial(on_device, sizes)
    return jax.shard_map(body, mesh=mesh, in_specs=placed, out_specs=P(), check_vma=False)
```

```python
import functools

import jax
import jax.numpy as jnp
from jax import lax
from jax.experimental import pallas as pl
from jax.experimental.pallas import tpu as pltpu
from jax.sharding import PartitionSpec as P

LANES = 128
ROWS = 16


def split_sizes(total, count):
    best = 1
    for n in range(1, count + 1):
        if count % n == 0 and total % n == 0 and (total // n) % ROWS == 0:
            best = n
    return best


def group_size(depth):
    best = depth
    for size in range(2, 11, 2):
        if depth % size == 0:
            best = size
    return best


def pack_kernel(group, parts, given, spot_ref, *refs):
    pieces, crossed_ref, low_ref = refs[:parts], refs[parts], refs[parts + 1]
    sent_ref, own_ref, mark_ref, sem = refs[-4:] if parts else (refs[-3], None, refs[-2], refs[-1])
    here = spot_ref[0]
    sides = given["sides"]
    inner = jnp.logical_and(here > 0, here < sides - 1)
    groups, back_at, low_at, low_count, kind_at = (
        given["groups"], given["back"], given["low"], given["count"], given["kind"]
    )
    mark_ref[0] = spot_ref[0]
    mark_ref[1] = spot_ref[1]

    def back():
        return pltpu.make_async_copy(
            crossed_ref.at[0:2 * groups], sent_ref.at[back_at:back_at + 2 * groups], sem
        )

    def lower():
        return pltpu.make_async_copy(
            low_ref.at[low_at:low_at + low_count], sent_ref.at[kind_at:kind_at + low_count], sem
        )

    if given["has_back"]:
        @pl.when(inner)
        def _():
            back().start()
    if low_count:
        @pl.when(jnp.logical_not(inner))
        def _():
            lower().start()

    if parts:
        kinds, depth, rows, width = pieces[0].shape
        total = width * parts
        mains = total // LANES
        rest = total - mains * LANES
        half = (group + 1) // 2

        def place(slot, shift):
            shape = (width, (mains + 1) * LANES)
            target = slot * width + lax.broadcasted_iota(jnp.int32, shape, 0)
            target = jnp.where(target >= mains * LANES, target + shift, target)
            hit = lax.broadcasted_iota(jnp.int32, shape, 1) == target
            return jnp.where(hit, 1.0, 0.0).astype(jnp.bfloat16)

        tables = [[place(s, shift) for s in range(parts)] for shift in (0, rest)]
        for kind in range(kinds):
            base = (0, 2, 1)[kind] * groups

            def put(lo, hi, value):
                value = value.astype(jnp.bfloat16)
                own_ref[base:base + groups, lo:hi] = value
                if kind != 1:
                    sent_ref[base:base + groups, lo:hi] = value
                else:
                    @pl.when(jnp.logical_not(inner))
                    def _():
                        sent_ref[base:base + groups, lo:hi] = value

            tails = []
            for part, (lo, hi) in enumerate(((0, half), (half, group))):
                if lo == hi:
                    continue
                got = 0.0
                for slot, ref in enumerate(pieces):
                    block = ref[kind].reshape(groups, group, rows, width)[:, lo:hi]
                    got = got + jnp.dot(
                        block.reshape(groups * (hi - lo) * rows, width),
                        tables[part][slot],
                        preferred_element_type=jnp.float32,
                    )
                got = got.reshape(groups, hi - lo, rows, (mains + 1) * LANES)
                for main in range(mains):
                    put(main * group + lo, main * group + hi, got[..., main * LANES:(main + 1) * LANES])
                tails.append(got[..., mains * LANES:])
            start = mains * group
            first = tails[0]
            if len(tails) == 1:
                put(start, start + half, first)
            else:
                both = tails[1].shape[1]
                put(start, start + both, first[:, :both] + tails[1])
                if both < half:
                    put(start + both, start + half, first[:, both:])

    if given["has_back"]:
        @pl.when(inner)
        def _():
            back().wait()
    if low_count:
        @pl.when(jnp.logical_not(inner))
        def _():
            lower().wait()


def pack(spot, pieces, crossed, low, deps, given, group, plane, length):
    has_back = crossed is not None
    given = dict(given, has_back=has_back)
    groups = given["groups"]
    out = [jax.ShapeDtypeStruct((length,) + plane, jnp.bfloat16)]
    specs = [pl.BlockSpec(memory_space=pltpu.VMEM)]
    if pieces:
        out.append(jax.ShapeDtypeStruct((3 * groups,) + plane, jnp.bfloat16))
        specs.append(pl.BlockSpec(memory_space=pltpu.VMEM))
    out.append(jax.ShapeDtypeStruct((2,), jnp.int32))
    specs.append(pl.BlockSpec(memory_space=pltpu.SMEM))
    anywhere = pl.BlockSpec(memory_space=pl.ANY)
    operands = [crossed if has_back else low, low] + list(deps)
    got = pl.pallas_call(
        functools.partial(pack_kernel, group, len(pieces), given),
        out_shape=out,
        in_specs=[pl.BlockSpec(memory_space=pltpu.SMEM)]
        + [pl.BlockSpec(memory_space=pltpu.VMEM)] * len(pieces)
        + [anywhere] * len(operands),
        out_specs=specs,
        scratch_shapes=[pltpu.SemaphoreType.DMA],
        compiler_params=pltpu.CompilerParams(vmem_limit_bytes=32 * 2 ** 20),
        cost_estimate=pl.CostEstimate(flops=2 * 10 ** 9, bytes_accessed=6 * 2 ** 20, transcendentals=0),
        name="pack",
    )(spot, *pieces, *operands)
    return (got[0], got[1], got[2]) if pieces else (got[0], None, got[1])


def pass_kernel(given, spot_ref, *refs):
    received_ref, crossed_ref, low_ref = refs[:3]
    outs, sems = refs[given["inputs"]:-1], refs[-1]
    here = spot_ref[0]
    sides, groups = given["sides"], given["groups"]
    inner = jnp.logical_and(here > 0, here < sides - 1)
    low_at, low_count = given["low"], given["count"]
    copies = []
    if given["cross"]:
        copies.append((None, pltpu.make_async_copy(received_ref.at[0:3 * groups], outs[0], sems.at[0])))
    if given["back"]:
        copies.append((inner, pltpu.make_async_copy(crossed_ref.at[0:2 * groups], outs[-1], sems.at[1])))
    if low_count:
        copies.append(
            (
                jnp.logical_not(inner),
                pltpu.make_async_copy(
                    low_ref.at[low_at:low_at + low_count], outs[-1].at[0:low_count], sems.at[2]
                ),
            )
        )
    for act in ("start", "wait"):
        for where, copy in copies:
            if where is None:
                getattr(copy, act)()
            else:
                pl.when(where)(getattr(copy, act))


def pass_on(spot, received, crossed, low, deps, given, plane):
    groups = given["groups"]
    given = dict(given, back=crossed is not None, inputs=3 + len(deps))
    out = []
    if given["cross"]:
        out.append(jax.ShapeDtypeStruct((3 * groups,) + plane, jnp.bfloat16))
    if given["back"]:
        out.append(jax.ShapeDtypeStruct((2 * groups,) + plane, jnp.bfloat16))
    anywhere = pl.BlockSpec(memory_space=pl.ANY)
    operands = [received, crossed if crossed is not None else low, low] + list(deps)
    return pl.pallas_call(
        functools.partial(pass_kernel, given),
        out_shape=out,
        in_specs=[pl.BlockSpec(memory_space=pltpu.SMEM)] + [anywhere] * len(operands),
        out_specs=[pl.BlockSpec(memory_space=pltpu.VMEM)] * len(out),
        scratch_shapes=[pltpu.SemaphoreType.DMA((3,))],
        compiler_params=pltpu.CompilerParams(vmem_limit_bytes=32 * 2 ** 20),
        cost_estimate=pl.CostEstimate(flops=0, bytes_accessed=4 * 2 ** 20, transcendentals=0),
        name="pass_on",
    )(spot, *operands)


def fetch(src, dst, sem):
    pltpu.make_async_copy(src, dst, sem).start()


def expand(source, step, group, groups, tables, spread):
    sides, _, plane, rows, _ = source.shape
    kinds = source.shape[1] // groups
    half = (group + 1) // 2
    mains = (plane - half) // group
    windows = spread.shape[1]
    for part, (lo, hi) in enumerate(((0, half), (half, group))):
        if lo == hi:
            continue
        count = hi - lo
        spans = [(main * group + lo, main * group + hi) for main in range(mains)]
        spans.append((mains * group, mains * group + count))
        wide = jnp.concatenate(
            [
                jnp.concatenate(
                    [
                        source[:, kind * groups + step, first:stop].reshape(sides * count * rows, LANES)
                        for first, stop in spans
                    ],
                    axis=1,
                )
                for kind in range(kinds)
            ],
            axis=0,
        )
        for slot, table in enumerate(tables):
            got = jnp.dot(wide, table[part], preferred_element_type=jnp.float32).astype(jnp.bfloat16)
            got = got.reshape(kinds, sides, count, rows, windows * LANES)
            for kind in range(kinds):
                for k in range(count):
                    for a in range(windows):
                        spread[slot + kind, a, :, (lo + k) * LANES:(lo + k + 1) * LANES] = got[
                            kind, :, k, :, a * LANES:(a + 1) * LANES
                        ].reshape(sides * rows, LANES)


def table_kernel(rest, table_ref, *refs):
    out_ref = refs[-1]
    total = table_ref.shape[0]
    mains = total - rest
    out_ref[...] = jnp.zeros_like(out_ref)
    for part in range(2):
        out_ref[part, 0:mains] = table_ref[0:mains]
        out_ref[part, mains + part * rest:mains + (part + 1) * rest] = table_ref[mains:total]


def make_table(table, deps, rest):
    total, lanes = table.shape
    vmem = pl.BlockSpec(memory_space=pltpu.VMEM)
    return pl.pallas_call(
        functools.partial(table_kernel, rest),
        out_shape=jax.ShapeDtypeStruct((2, total - rest + LANES, lanes), table.dtype),
        in_specs=[vmem] + [pl.BlockSpec(memory_space=pl.ANY)] * len(deps),
        out_specs=vmem,
        name="make_table",
    )(table, *deps)


def low_kernel(one_ref, two_ref, out_ref):
    group, slab, lanes = one_ref.shape
    out_ref[...] = jnp.zeros_like(out_ref)
    for k in range(group):
        for half, ref in enumerate((one_ref, two_ref)):
            out_ref[k * LANES:k * LANES + slab, half * lanes:(half + 1) * lanes] = ref[k]


def make_lows(one, two, group):
    depth, slab, lanes = one.shape
    block = pl.BlockSpec((group, slab, lanes), lambda g: (g, 0, 0))
    return pl.pallas_call(
        low_kernel,
        out_shape=jax.ShapeDtypeStruct((depth * LANES, 2 * lanes), one.dtype),
        grid=(depth // group,),
        in_specs=[block, block],
        out_specs=pl.BlockSpec((group * LANES, 2 * lanes), lambda g: (g, 0)),
        compiler_params=pltpu.CompilerParams(vmem_limit_bytes=32 * 2 ** 20),
        name="make_lows",
    )(one, two)


def planes_kernel(spans, depth, tiles, *refs):
    parts = refs[:len(spans)]
    out_ref, held, sems = refs[-3:]
    copies = [
        pltpu.make_async_copy(ref.at[first:first + size], held.at[at:at + size], sems.at[i])
        for i, (ref, (at, first, size)) in enumerate(zip(parts, spans))
    ]
    for copy in copies:
        copy.start()
    out_ref[...] = jnp.zeros_like(out_ref)
    for copy in copies:
        copy.wait()
    planes, rows = held.shape[1], held.shape[2]

    def one(k, _):
        for i in range(tiles[0]):
            for j in range(tiles[1]):
                plane = (k * tiles[0] + i) * tiles[1] + j
                out_ref[
                    pl.ds(pl.multiple_of(k * LANES + i * rows, rows), rows), j * LANES:(j + 1) * LANES
                ] = held[plane // planes, plane % planes]
        return 0

    lax.fori_loop(0, depth, one, 0)


def low_of_planes(parts, deps, units, depth, tiles):
    spans = [(at, first, size) for at, _, first, size in parts]
    shape = parts[0][1].shape[1:]
    anywhere = pl.BlockSpec(memory_space=pl.ANY)
    return pl.pallas_call(
        functools.partial(planes_kernel, spans, depth, tiles),
        out_shape=jax.ShapeDtypeStruct((depth * LANES, tiles[1] * LANES), jnp.bfloat16),
        in_specs=[anywhere] * (len(parts) + len(deps)),
        out_specs=pl.BlockSpec(memory_space=pltpu.VMEM),
        scratch_shapes=[
            pltpu.VMEM((units,) + shape, jnp.bfloat16),
            pltpu.SemaphoreType.DMA((len(parts),)),
        ],
        compiler_params=pltpu.CompilerParams(vmem_limit_bytes=40 * 2 ** 20),
        name="low_of_planes",
    )(*[got for _, got, _, _ in parts], *deps)


def join_kernel(count, *refs):
    outs = refs[-count:]
    for i in range(count):
        outs[i][...] = (refs[2 * i][...].astype(jnp.float32) + refs[2 * i + 1][...].astype(jnp.float32)).astype(
            outs[i].dtype
        )


def join(pairs, deps):
    vmem = pl.BlockSpec(memory_space=pltpu.VMEM)
    types = [jnp.float32] + [jnp.bfloat16] * (len(pairs) - 1)
    return pl.pallas_call(
        functools.partial(join_kernel, len(pairs)),
        out_shape=[jax.ShapeDtypeStruct(a.shape, kind) for (a, _), kind in zip(pairs, types)],
        in_specs=[vmem] * (2 * len(pairs)) + [pl.BlockSpec(memory_space=pl.ANY)] * len(deps),
        out_specs=[vmem] * len(pairs),
        compiler_params=pltpu.CompilerParams(vmem_limit_bytes=32 * 2 ** 20),
        name="join",
    )(*[x for pair in pairs for x in pair], *deps)


def even_kernel(sides, group, groups, use_ends, use_inner, starts, spot_ref, *refs):
    views = [ref.at[at:at + 2 * groups] for ref, at in zip(refs[:2 * sides], starts)]
    inner_blocks, end_blocks = views[:sides], views[sides:]
    tables, low_ref = refs[2 * sides:2 * sides + 2]
    total, even, spread, sems = refs[-4:]
    here = spot_ref[0]
    step = pl.program_id(0)
    inner = jnp.logical_and(here > 0, here < sides - 1)
    work = jnp.logical_or(jnp.logical_and(inner, use_inner), jnp.logical_and(jnp.logical_not(inner), use_ends))

    @pl.when(work)
    def _():
        @pl.when(step == 0)
        def _():
            @pl.when(inner)
            def _():
                for at, turn in enumerate((0, 1, 3, 2)):
                    fetch(inner_blocks[at], even.at[here ^ turn], sems.at[at])

            @pl.when(jnp.logical_not(inner))
            def _():
                for at, turn in enumerate((0, 1, 2, 3)):
                    fetch(end_blocks[at], even.at[here ^ turn], sems.at[at])

            total[...] = jnp.zeros_like(total)
            for at in range(sides):
                pltpu.make_async_copy(inner_blocks[at], even.at[at], sems.at[at]).wait()

        expand(even, step, group, groups, (tables,), spread)
        count = spread.shape[1] * spread.shape[2]
        full = total.shape[2]
        both = spread[...].reshape(2, count, group * LANES)
        got = jnp.dot(both[0], low_ref[...], preferred_element_type=jnp.float32)
        total[0] += got[:, :full]
        total[1] += got[:, full:] + jnp.dot(both[1], low_ref[:, :full], preferred_element_type=jnp.float32)

    @pl.when(jnp.logical_and(step == 0, jnp.logical_not(work)))
    def _():
        total[...] = jnp.zeros_like(total)


def even_product(spot, inner_blocks, end_blocks, deps, table, low, sides, group, groups):
    some = inner_blocks or end_blocks
    use_inner, use_ends = inner_blocks is not None, end_blocks is not None
    blocks = (inner_blocks or some) + (end_blocks or some)
    starts = [at for _, at in blocks]
    _, planes, rows, _ = some[0][0].shape
    windows = table.shape[2] // LANES
    full = low.shape[-1] // 2
    count = windows * sides * rows
    whole = lambda arr: pl.BlockSpec(arr.shape, lambda g, s: (0,) * len(arr.shape))
    part = pl.BlockSpec((group * LANES, 2 * full), lambda g, s: (g, 0))
    out = jax.ShapeDtypeStruct((2, count, full), jnp.float32)
    depth = groups * group
    flops = 2 * count * depth * LANES * 3 * full + 4 * sides * rows * depth * 3 * LANES * windows * LANES
    return pl.pallas_call(
        functools.partial(even_kernel, sides, group, groups, use_ends, use_inner, starts),
        out_shape=out,
        grid_spec=pltpu.PrefetchScalarGridSpec(
            num_scalar_prefetch=1,
            grid=(groups,),
            in_specs=[pl.BlockSpec(memory_space=pl.ANY)] * (2 * sides)
            + [whole(table), part]
            + [pl.BlockSpec(memory_space=pl.ANY)] * len(deps),
            out_specs=whole(out),
            scratch_shapes=[
                pltpu.VMEM((sides, 2 * groups, planes, rows, LANES), jnp.bfloat16),
                pltpu.VMEM((2, windows, sides * rows, group * LANES), jnp.bfloat16),
                pltpu.SemaphoreType.DMA((sides,)),
            ],
        ),
        compiler_params=pltpu.CompilerParams(vmem_limit_bytes=56 * 2 ** 20),
        cost_estimate=pl.CostEstimate(flops=flops, bytes_accessed=20 * 2 ** 20, transcendentals=0),
        name="even_product",
    )(spot, *[ref for ref, _ in blocks], table, low, *deps)


def odd_kernel(sides, group, groups, outs, starts, spot_ref, *refs):
    blocks = [ref.at[at:at + groups] for ref, at in zip(refs[:sides], starts)]
    inner_part, end_part = refs[sides:sides + 2]
    tables, next_tables, low_ref, next_low_ref = refs[sides + 2:sides + 6]
    out_refs = refs[-4 - outs:-4]
    odd, spread, total, sems = refs[-4:]
    here, role = spot_ref[0], spot_ref[1]
    step, last = pl.program_id(0), pl.num_programs(0) - 1
    inner = jnp.logical_and(here > 0, here < sides - 1)

    @pl.when(step == 0)
    def _():
        @pl.when(inner)
        def _():
            fetch(inner_part, total, sems.at[sides])
            for at, turn in enumerate((0, 1, 3, 2)):
                fetch(blocks[at], odd.at[here ^ turn], sems.at[at])
            for at in range(sides):
                pltpu.make_async_copy(blocks[at], odd.at[at], sems.at[at]).wait()

        @pl.when(jnp.logical_not(inner))
        def _():
            fetch(end_part, total, sems.at[sides])

        pltpu.make_async_copy(inner_part, total, sems.at[sides]).wait()

    @pl.when(inner)
    def _():
        expand(odd, step, group, groups, (tables, next_tables), spread)
        count = spread.shape[1] * spread.shape[2]
        rows = spread[...].reshape(2, count, group * LANES)
        got = jnp.dot(rows[0], low_ref[...], preferred_element_type=jnp.float32)
        total[1] += got + jnp.dot(rows[1], next_low_ref[...], preferred_element_type=jnp.float32)

    @pl.when(step == last)
    def _():
        for offset in range(outs):
            which = offset ^ role
            value = total[which // 2]
            width = value.shape[1] // 2
            value = jnp.where(which % 2 == 1, value[:, width:], value[:, :width])
            out_refs[offset][...] = value.reshape(out_refs[offset].shape).astype(jnp.bfloat16)


def odd_product(spot, blocks, inner_part, end_part, deps, tables, lows, sides, group, groups, outs):
    starts = [at for _, at in blocks]
    _, planes, rows, _ = blocks[0][0].shape
    table, next_table = tables
    low, next_low = lows
    windows = table.shape[2] // LANES
    full = low.shape[-1]
    count = windows * sides * rows
    whole = lambda arr: pl.BlockSpec(arr.shape, lambda g, s: (0,) * len(arr.shape))
    part = pl.BlockSpec((group * LANES, full), lambda g, s: (g, 0))
    out = [jax.ShapeDtypeStruct((windows, sides * rows, full // 2), jnp.bfloat16)] * outs
    depth = groups * group
    flops = 2 * count * depth * LANES * 2 * full + 4 * sides * rows * depth * 3 * LANES * windows * LANES
    return pl.pallas_call(
        functools.partial(odd_kernel, sides, group, groups, outs, starts),
        out_shape=out,
        grid_spec=pltpu.PrefetchScalarGridSpec(
            num_scalar_prefetch=1,
            grid=(groups,),
            in_specs=[pl.BlockSpec(memory_space=pl.ANY)] * (sides + 2)
            + [whole(table), whole(next_table), part, part]
            + [pl.BlockSpec(memory_space=pl.ANY)] * len(deps),
            out_specs=[whole(o) for o in out],
            scratch_shapes=[
                pltpu.VMEM((sides, groups, planes, rows, LANES), jnp.bfloat16),
                pltpu.VMEM((2, windows, sides * rows, group * LANES), jnp.bfloat16),
                pltpu.VMEM((2, count, full), jnp.float32),
                pltpu.SemaphoreType.DMA((sides + 1,)),
            ],
        ),
        compiler_params=pltpu.CompilerParams(vmem_limit_bytes=56 * 2 ** 20),
        cost_estimate=pl.CostEstimate(flops=flops, bytes_accessed=20 * 2 ** 20, transcendentals=0),
        name="odd_product",
    )(spot, *[ref for ref, _ in blocks], inner_part, end_part, table, next_table, low, next_low, *deps)


def on_device(sizes, tops, bottoms, left_iso, right_iso):
    roles, contrs, sides = sizes
    role = lax.axis_index("role")
    here = lax.axis_index("horiz")
    kinds, depth_all, rows_all, width = tops.shape
    depth = depth_all // roles
    group = group_size(depth)
    groups = depth // group
    share = right_iso.shape[0]
    chunks = split_sizes(rows_all, share)
    unit = share // chunks
    rows = rows_all // chunks
    windows = left_iso.shape[1]
    slab = left_iso.shape[2]
    downs, full = bottoms.shape[3], bottoms.shape[4]
    spot = jnp.stack([here, role]).astype(jnp.int32)

    cut = tops.reshape(kinds, depth_all, contrs, chunks, unit, width)

    def exchange(t, place):
        pieces = []
        for s in range(roles):
            piece = lax.dynamic_slice(
                cut, (0, (place ^ s) * depth, 0, t, 0, 0), (kinds, depth, contrs, 1, unit, width)
            ).reshape(kinds, depth, rows, width)
            if s:
                piece = lax.ppermute(piece, "role", [(j, j ^ s) for j in range(roles)])
            pieces.append(piece)
        return pieces

    def lower(kind, place):
        low = lax.dynamic_slice(
            bottoms, (kind, place * depth, 0, 0, 0), (1, depth, slab, downs, full)
        )
        return low.reshape(depth, slab, downs * full)

    pairs = [(z, z ^ 1) for z in range(sides)]
    hand = [(z, z ^ 1) for z in (0, sides - 1)]
    cross = [(z, z ^ 3) for z in range(1, sides - 1)]
    move = lambda value, perm: lax.ppermute(value, "horiz", perm)

    pieces = {0: exchange(0, role)}
    left_all = jnp.concatenate(
        [lax.dynamic_slice_in_dim(left_iso, (role ^ s) * width, width, 0) for s in range(roles)], axis=0
    )
    total = left_all.shape[0]
    mains = total // LANES
    rest = total - mains * LANES
    plane = (mains * group + (group + 1) // 2, rows, LANES)

    def table(flat_left):
        wide = flat_left.reshape(total, windows, slab)
        return jnp.pad(wide, ((0, 0), (0, 0), (0, LANES - slab))).reshape(total, windows * LANES)

    flat_left = left_all.reshape(total, windows * slab)
    middle = lower(1, role) * jnp.asarray(2, bottoms.dtype)
    tiles = (slab // rows, downs * full // LANES)
    count = depth * tiles[0] * tiles[1]
    units = -(-count // plane[0])
    carried = middle.reshape(depth, tiles[0], rows, tiles[1], LANES).transpose(0, 1, 3, 2, 4)
    carried = carried.reshape(count, rows, LANES)
    carried = jnp.pad(carried, ((0, units * plane[0] - count), (0, 0), (0, 0)))
    carried = carried.reshape((units,) + plane)
    taken = 0

    def take(most):
        nonlocal taken
        at, size = taken, min(most, units - taken)
        taken += size
        return at, size

    own, sent, straight, turned, last = {}, {}, {}, {}, {}
    sums, shares, reduced = {}, {}, {}
    parts = []
    near_low = None
    done = None

    def send_core(t):
        stages[t] = [lax.ppermute(shares[t][s], "role", [(j, j ^ 1) for j in range(roles)]) for s in (1, 3)]

    def join_core(t, deps):
        kept, give = join([(shares[t][0], stages[t][0]), (shares[t][2], stages[t][1])], deps)
        stages[t] = [kept, lax.ppermute(give, "role", [(j, j ^ 2) for j in range(roles)])]
        return kept

    def join_chip(t, deps):
        summed = join([tuple(stages[t])], deps)[0]
        size, step = sides * contrs, contrs // 2
        stages[t] = halve(summed.reshape(windows, size, unit, full), size, step) + (size // 2, step // 2)
        return summed

    def halve(summed, size, step):
        bit = (lax.axis_index("contr") // step) % 2
        keep = lax.dynamic_slice_in_dim(summed, bit * (size // 2), size // 2, 1)
        give = lax.dynamic_slice_in_dim(summed, (1 - bit) * (size // 2), size // 2, 1).astype(jnp.bfloat16)
        return keep, lax.ppermute(give, "contr", [(j, j ^ step) for j in range(contrs)])

    def join_contr(t, deps):
        keep, got, size, step = stages[t]
        summed = join([(keep, got)], deps)[0]
        while step:
            summed = join([halve(summed, size, step)], [])[0]
            size, step = size // 2, step // 2
        reduced[t] = summed
        return summed

    stages, extra = {}, []
    for r in range(chunks + 3):
        if r <= chunks:
            fresh = r < chunks
            base = 3 * groups if fresh else 0
            most = {0: 2, 1: 3}.get(r, 1) * groups if fresh else 0
            at, size = take(most)
            length = max(base + size, 4 * groups) if fresh else 2 * groups
            given = dict(
                sides=sides, groups=groups, back=2 * groups if fresh else 0, kind=base, low=at, count=size
            )
            deps = [sent[r - 1]] if r else []
            deps += [sums[r - 1]] if r - 1 in sums else []
            out, mine, mark = pack(
                spot, pieces.pop(r) if fresh else [], straight.get(r - 1), carried, deps + extra, given,
                group, plane, length,
            )
            extra = []
            sent[r] = move(out, pairs)
            if size:
                parts.append((at, sent[r], base, size))
            if fresh:
                own[r] = mine
                straight[r] = move(mine, cross)
            done = out
            for t in {0: (1, 2), 1: (3,), 2: (4,)}.get(r, (r + 2,)):
                if t < chunks:
                    pieces[t] = exchange(t, mark[1])
            if r == 0:
                late = mark[1]
                first_table = make_table(table(flat_left), [out], rest)
                low = make_lows(lower(0, late), lower(2, late), group)
                near_left = move(flat_left, hand)
                extra = [low, first_table]
            if r == 1:
                near_table = make_table(table(near_left), [out], rest)
                middle_low = low_of_planes([(0, carried, 0, units)], [out], units, depth, tiles)
                extra = [near_table, middle_low]
        t = r - 4
        if 0 <= t < chunks:
            if near_low is None:
                near_low = low_of_planes(sorted(parts, key=lambda p: p[0]), [done], units, depth, tiles)
            blocks = [(own[t], 2 * groups), (sent[t], 2 * groups), (straight[t], 2 * groups), (turned[t + 1], 2 * groups)]
            shares[t] = odd_product(
                spot, blocks, sums[t + 2], sums[t + 3], [done] + extra, (first_table, near_table),
                (middle_low, near_low), sides, group, groups, roles,
            )
            done = shares[t][0]
            extra = []
            send_core(t)
            if t - 1 in stages:
                extra.append(join_chip(t - 1, [done]))
        if 1 <= r <= chunks + 1:
            at, size = take(2 * groups) if 2 <= r else (0, 0)
            given = dict(sides=sides, groups=groups, cross=r <= chunks, low=at, count=size)
            deps = [done] + ([last[r - 1]] if r - 1 in last else [])
            outs = pass_on(spot, sent[r - 1], turned.get(r - 1), carried, deps + extra, given, plane)
            extra = []
            if r <= chunks:
                turned[r] = move(outs[0], cross)
            if r - 1 in turned:
                last[r] = move(outs[-1], pairs)
                if size:
                    parts.append((at, last[r], 0, size))
            done = outs[0]
        if r >= 2:
            t = r - 2
            inner_blocks = end_blocks = None
            if t < chunks:
                inner_blocks = [(own[t], 0), (sent[t], 0), (straight[t], 0), (turned[t + 1], 0)]
            t = r - 3
            if 0 <= t:
                end_blocks = [
                    (own[t], 0), (sent[t], 0), (sent[t + 1], 2 * groups if t + 1 < chunks else 0), (last[t + 2], 0)
                ]
            sums[r] = even_product(
                spot, inner_blocks, end_blocks, [done] + extra, first_table, low, sides, group, groups
            )
            done = sums[r]
            extra = []
            if r - 4 in shares:
                extra.append(join_core(r - 4, [done]))
            if r - 5 in shares:
                extra.append(join_contr(r - 5, [done]))
    t = chunks - 1
    blocks = [(own[t], 2 * groups), (sent[t], 2 * groups), (straight[t], 2 * groups), (turned[t + 1], 2 * groups)]
    shares[t] = odd_product(
        spot, blocks, sums[t + 2], sums[t + 3], [done] + extra, (first_table, near_table),
        (middle_low, near_low), sides, group, groups, roles,
    )
    send_core(t)
    join_chip(t - 1, [shares[t][0]])
    join_core(t, [])
    join_contr(t - 1, [])
    join_chip(t, [])
    join_contr(t, [])

    summed = jnp.concatenate([reduced[t] for t in range(chunks)], axis=2)
    mine = lax.dynamic_slice_in_dim(summed, here, 1, 1)
    for s in range(1, sides):
        give = lax.dynamic_slice_in_dim(summed, here ^ s, 1, 1).astype(jnp.bfloat16)
        got = lax.ppermute(give, "horiz", [(z, z ^ s) for z in range(sides)])
        mine = mine + got.astype(jnp.float32)
    mine = mine.reshape(windows, share, full).astype(jnp.bfloat16)
    projected = jnp.einsum("aur,urb->ab", mine, right_iso, preferred_element_type=jnp.float32)
    projected = projected * jnp.where(role >= downs, 0.25, 1.0)
    for axis, size in (("contr", contrs), ("horiz", sides)):
        s = 1
        while s < size:
            projected = projected + lax.ppermute(projected, axis, [(j, j ^ s) for j in range(size)])
            s *= 2
    found = [projected] + [
        lax.ppermute(projected, "role", [(j, j ^ s) for j in range(roles)]) for s in range(1, roles)
    ]
    found = jnp.stack(found)
    order = [lax.dynamic_index_in_dim(found, q ^ role, 0, keepdims=False) for q in range(roles)]
    return jnp.stack(order).reshape(roles // downs, downs, windows, -1)


def solution(mesh):
    placed = (
        P(None, "contr", "horiz", "role"),
        P(None, "contr", "horiz", None, None),
        P(None, None, "horiz"),
        P(("contr", "horiz"), None, None),
    )
    sizes = tuple(mesh.shape[axis] for axis in ("role", "contr", "horiz"))
    body = functools.partial(on_device, sizes)
    return jax.shard_map(body, mesh=mesh, in_specs=placed, out_specs=P(), check_vma=False)
```

```python
import functools

import jax
import jax.numpy as jnp
from jax import lax
from jax.experimental import pallas as pl
from jax.experimental.pallas import tpu as pltpu
from jax.sharding import PartitionSpec as P

LANES = 128
ROWS = 16
VMEM_BYTES = 60 * 2 ** 20


def split_sizes(total, count):
    best = 1
    for n in range(1, count + 1):
        if count % n == 0 and total % n == 0 and (total // n) % ROWS == 0:
            best = n
    return best


def group_size(depth):
    best = depth
    for size in range(2, 11, 2):
        if depth % size == 0:
            best = size
    return best


def pack_kernel(group, parts, given, spot_ref, *refs):
    pieces, crossed_ref, low_ref = refs[:parts], refs[parts], refs[parts + 1]
    sent_ref, own_ref, mark_ref, sem = refs[-4:] if parts else (refs[-3], None, refs[-2], refs[-1])
    here = spot_ref[0]
    sides = given["sides"]
    inner = jnp.logical_and(here > 0, here < sides - 1)
    groups, back_at, low_at, low_count, kind_at = (
        given["groups"], given["back"], given["low"], given["count"], given["kind"]
    )
    mark_ref[0] = spot_ref[0]
    mark_ref[1] = spot_ref[1]

    def back():
        return pltpu.make_async_copy(
            crossed_ref.at[0:2 * groups], sent_ref.at[back_at:back_at + 2 * groups], sem
        )

    def lower():
        return pltpu.make_async_copy(
            low_ref.at[low_at:low_at + low_count], sent_ref.at[kind_at:kind_at + low_count], sem
        )

    if given["has_back"]:
        @pl.when(inner)
        def _():
            back().start()
    if low_count:
        @pl.when(jnp.logical_not(inner))
        def _():
            lower().start()

    if parts:
        kinds, depth, rows, width = pieces[0].shape
        total = width * parts
        mains = total // LANES
        rest = total - mains * LANES
        half = (group + 1) // 2

        def place(slot, shift):
            shape = (width, (mains + 1) * LANES)
            target = slot * width + lax.broadcasted_iota(jnp.int32, shape, 0)
            target = jnp.where(target >= mains * LANES, target + shift, target)
            hit = lax.broadcasted_iota(jnp.int32, shape, 1) == target
            return jnp.where(hit, 1.0, 0.0).astype(jnp.bfloat16)

        tables = [[place(s, shift) for s in range(parts)] for shift in (0, rest)]
        for kind in range(kinds):
            base = (0, 2, 1)[kind] * groups

            def put(lo, hi, value):
                value = value.astype(jnp.bfloat16)
                own_ref[base:base + groups, lo:hi] = value
                if kind != 1:
                    sent_ref[base:base + groups, lo:hi] = value
                else:
                    @pl.when(jnp.logical_not(inner))
                    def _():
                        sent_ref[base:base + groups, lo:hi] = value

            tails = []
            for part, (lo, hi) in enumerate(((0, half), (half, group))):
                if lo == hi:
                    continue
                got = 0.0
                for slot, ref in enumerate(pieces):
                    block = ref[kind].reshape(groups, group, rows, width)[:, lo:hi]
                    got = got + jnp.dot(
                        block.reshape(groups * (hi - lo) * rows, width),
                        tables[part][slot],
                        preferred_element_type=jnp.float32,
                    )
                got = got.reshape(groups, hi - lo, rows, (mains + 1) * LANES)
                for main in range(mains):
                    put(main * group + lo, main * group + hi, got[..., main * LANES:(main + 1) * LANES])
                tails.append(got[..., mains * LANES:])
            start = mains * group
            first = tails[0]
            if len(tails) == 1:
                put(start, start + half, first)
            else:
                both = tails[1].shape[1]
                put(start, start + both, first[:, :both] + tails[1])
                if both < half:
                    put(start + both, start + half, first[:, both:])

    if given["has_back"]:
        @pl.when(inner)
        def _():
            back().wait()
    if low_count:
        @pl.when(jnp.logical_not(inner))
        def _():
            lower().wait()


def pack(spot, pieces, crossed, low, deps, given, group, plane, length):
    has_back = crossed is not None
    pieces, turn = pieces
    given = dict(given, has_back=has_back)
    groups = given["groups"]
    out = [jax.ShapeDtypeStruct((length,) + plane, jnp.bfloat16)]
    specs = [pl.BlockSpec(memory_space=pltpu.VMEM)]
    if pieces:
        out.append(jax.ShapeDtypeStruct((3 * groups,) + plane, jnp.bfloat16))
        specs.append(pl.BlockSpec(memory_space=pltpu.VMEM))
    out.append(jax.ShapeDtypeStruct((2,), jnp.int32))
    specs.append(pl.BlockSpec(memory_space=pltpu.SMEM))
    anywhere = pl.BlockSpec(memory_space=pl.ANY)
    operands = [crossed if has_back else low, low] + list(deps)
    got = pl.pallas_call(
        functools.partial(pack_kernel, group, len(pieces), given),
        out_shape=out,
        grid=(1,),
        in_specs=[pl.BlockSpec(memory_space=pltpu.SMEM)]
        + [pl.BlockSpec((None,) + piece.shape[1:], lambda g: (turn, 0, 0, 0, 0)) for piece in pieces]
        + [anywhere] * len(operands),
        out_specs=specs,
        scratch_shapes=[pltpu.SemaphoreType.DMA],
        compiler_params=pltpu.CompilerParams(vmem_limit_bytes=VMEM_BYTES),
        cost_estimate=pl.CostEstimate(flops=2 * 10 ** 9, bytes_accessed=6 * 2 ** 20, transcendentals=0),
        name="pack",
    )(spot, *pieces, *operands)
    return (got[0], got[1], got[2]) if pieces else (got[0], None, got[1])


def pass_kernel(given, spot_ref, *refs):
    received_ref, crossed_ref, low_ref = refs[:3]
    outs, sems = refs[given["inputs"]:-1], refs[-1]
    here = spot_ref[0]
    sides, groups = given["sides"], given["groups"]
    inner = jnp.logical_and(here > 0, here < sides - 1)
    low_at, low_count = given["low"], given["count"]
    copies = []
    if given["cross"]:
        copies.append((None, pltpu.make_async_copy(received_ref.at[0:3 * groups], outs[0], sems.at[0])))
    if given["back"]:
        copies.append((inner, pltpu.make_async_copy(crossed_ref.at[0:2 * groups], outs[-1], sems.at[1])))
    if low_count:
        copies.append(
            (
                jnp.logical_not(inner),
                pltpu.make_async_copy(
                    low_ref.at[low_at:low_at + low_count], outs[-1].at[0:low_count], sems.at[2]
                ),
            )
        )
    for act in ("start", "wait"):
        for where, copy in copies:
            if where is None:
                getattr(copy, act)()
            else:
                pl.when(where)(getattr(copy, act))


def pass_on(spot, received, crossed, low, deps, given, plane):
    groups = given["groups"]
    given = dict(given, back=crossed is not None, inputs=3 + len(deps))
    out = []
    if given["cross"]:
        out.append(jax.ShapeDtypeStruct((3 * groups,) + plane, jnp.bfloat16))
    if given["back"]:
        out.append(jax.ShapeDtypeStruct((2 * groups,) + plane, jnp.bfloat16))
    anywhere = pl.BlockSpec(memory_space=pl.ANY)
    operands = [received, crossed if crossed is not None else low, low] + list(deps)
    return pl.pallas_call(
        functools.partial(pass_kernel, given),
        out_shape=out,
        in_specs=[pl.BlockSpec(memory_space=pltpu.SMEM)] + [anywhere] * len(operands),
        out_specs=[pl.BlockSpec(memory_space=pltpu.VMEM)] * len(out),
        scratch_shapes=[pltpu.SemaphoreType.DMA((3,))],
        compiler_params=pltpu.CompilerParams(vmem_limit_bytes=VMEM_BYTES),
        cost_estimate=pl.CostEstimate(flops=0, bytes_accessed=4 * 2 ** 20, transcendentals=0),
        name="pass_on",
    )(spot, *operands)


def fetch(src, dst, sem):
    pltpu.make_async_copy(src, dst, sem).start()


def expand(source, step, group, groups, tables, spread):
    sides, _, plane, rows, _ = source.shape
    kinds = source.shape[1] // groups
    half = (group + 1) // 2
    mains = (plane - half) // group
    windows = spread.shape[1]
    for part, (lo, hi) in enumerate(((0, half), (half, group))):
        if lo == hi:
            continue
        count = hi - lo
        spans = [(main * group + lo, main * group + hi) for main in range(mains)]
        spans.append((mains * group, mains * group + count))
        wide = jnp.concatenate(
            [
                jnp.concatenate(
                    [
                        source[:, kind * groups + step, first:stop].reshape(sides * count * rows, LANES)
                        for first, stop in spans
                    ],
                    axis=1,
                )
                for kind in range(kinds)
            ],
            axis=0,
        )
        for slot, table in enumerate(tables):
            got = jnp.dot(wide, table[part], preferred_element_type=jnp.float32).astype(jnp.bfloat16)
            got = got.reshape(kinds, sides, count, rows, windows * LANES)
            for kind in range(kinds):
                for k in range(count):
                    for a in range(windows):
                        spread[slot + kind, a, :, (lo + k) * LANES:(lo + k + 1) * LANES] = got[
                            kind, :, k, :, a * LANES:(a + 1) * LANES
                        ].reshape(sides * rows, LANES)


def table_kernel(rest, table_ref, *refs):
    out_ref = refs[-1]
    total = table_ref.shape[0]
    mains = total - rest
    out_ref[...] = jnp.zeros_like(out_ref)
    for part in range(2):
        out_ref[part, 0:mains] = table_ref[0:mains]
        out_ref[part, mains + part * rest:mains + (part + 1) * rest] = table_ref[mains:total]


def make_table(table, deps, rest):
    total, lanes = table.shape
    vmem = pl.BlockSpec(memory_space=pltpu.VMEM)
    return pl.pallas_call(
        functools.partial(table_kernel, rest),
        out_shape=jax.ShapeDtypeStruct((2, total - rest + LANES, lanes), table.dtype),
        in_specs=[vmem] + [pl.BlockSpec(memory_space=pl.ANY)] * len(deps),
        out_specs=vmem,
        compiler_params=pltpu.CompilerParams(vmem_limit_bytes=VMEM_BYTES),
        name="make_table",
    )(table, *deps)


def low_kernel(*refs):
    parts, out_ref = refs[:-1], refs[-1]
    group, slab, lanes = parts[0].shape
    out_ref[...] = jnp.zeros_like(out_ref)
    for k in range(group):
        for at, ref in enumerate(parts):
            out_ref[k * LANES:k * LANES + slab, at * lanes:(at + 1) * lanes] = ref[k]


def make_lows(parts, group):
    depth, slab, lanes = parts[0].shape
    block = pl.BlockSpec((group, slab, lanes), lambda g: (g, 0, 0))
    return pl.pallas_call(
        low_kernel,
        out_shape=jax.ShapeDtypeStruct((depth * LANES, len(parts) * lanes), parts[0].dtype),
        grid=(depth // group,),
        in_specs=[block] * len(parts),
        out_specs=pl.BlockSpec((group * LANES, len(parts) * lanes), lambda g: (g, 0)),
        compiler_params=pltpu.CompilerParams(vmem_limit_bytes=VMEM_BYTES),
        name="make_lows",
    )(*parts)


def split_kernel(tiles, low_ref, out_ref):
    group, rows = low_ref.shape[0], out_ref.shape[1]
    for k in range(group):
        for i in range(tiles[0]):
            for j in range(tiles[1]):
                out_ref[(k * tiles[0] + i) * tiles[1] + j] = low_ref[
                    k, i * rows:(i + 1) * rows, j * LANES:(j + 1) * LANES
                ]


def make_planes(low, group, tiles, rows, planes):
    depth, slab, lanes = low.shape
    each = group * tiles[0] * tiles[1]
    return pl.pallas_call(
        functools.partial(split_kernel, tiles),
        out_shape=jax.ShapeDtypeStruct((planes, rows, LANES), low.dtype),
        grid=(depth // group,),
        in_specs=[pl.BlockSpec((group, slab, lanes), lambda g: (g, 0, 0))],
        out_specs=pl.BlockSpec((each, rows, LANES), lambda g: (g, 0, 0)),
        compiler_params=pltpu.CompilerParams(vmem_limit_bytes=VMEM_BYTES),
        name="make_planes",
    )(low)


def planes_kernel(spans, group, groups, tiles, *refs):
    parts = refs[:len(spans)]
    out_ref, held, sems = refs[-3:]
    step = pl.program_id(0)

    @pl.when(step == 0)
    def _():
        copies = [
            pltpu.make_async_copy(ref.at[first:first + size], held.at[at:at + size], sems.at[i])
            for i, (ref, (at, first, size)) in enumerate(zip(parts, spans))
        ]
        for copy in copies:
            copy.start()
        for copy in copies:
            copy.wait()

    out_ref[...] = jnp.zeros_like(out_ref)
    planes, rows = held.shape[1], held.shape[2]
    each = group * tiles[0] * tiles[1]
    for k in range(group):
        for i in range(tiles[0]):
            for j in range(tiles[1]):
                at = (k * tiles[0] + i) * tiles[1] + j
                if groups == 1:
                    plane = held[at // planes, at % planes]
                elif each % planes == 0:
                    plane = held[step * (each // planes) + at // planes, at % planes]
                else:
                    plane = held[(step * each + at) // planes, (step * each + at) % planes]
                out_ref[k * LANES + i * rows:k * LANES + (i + 1) * rows, j * LANES:(j + 1) * LANES] = plane


def low_of_planes(parts, deps, units, group, groups, tiles):
    spans = [(at, first, size) for at, _, first, size in parts]
    shape = parts[0][1].shape[1:]
    anywhere = pl.BlockSpec(memory_space=pl.ANY)
    return pl.pallas_call(
        functools.partial(planes_kernel, spans, group, groups, tiles),
        out_shape=jax.ShapeDtypeStruct((groups * group * LANES, tiles[1] * LANES), jnp.bfloat16),
        grid=(groups,),
        in_specs=[anywhere] * (len(parts) + len(deps)),
        out_specs=pl.BlockSpec((group * LANES, tiles[1] * LANES), lambda g: (g, 0)),
        scratch_shapes=[
            pltpu.VMEM((units,) + shape, jnp.bfloat16),
            pltpu.SemaphoreType.DMA((len(parts),)),
        ],
        compiler_params=pltpu.CompilerParams(vmem_limit_bytes=VMEM_BYTES),
        name="low_of_planes",
    )(*[got for _, got, _, _ in parts], *deps)


def join_kernel(count, *refs):
    outs = refs[-count:]
    for i in range(count):
        outs[i][...] = (refs[2 * i][...].astype(jnp.float32) + refs[2 * i + 1][...].astype(jnp.float32)).astype(
            outs[i].dtype
        )


def join(pairs, deps):
    vmem = pl.BlockSpec(memory_space=pltpu.VMEM)
    types = [jnp.float32] + [jnp.bfloat16] * (len(pairs) - 1)
    return pl.pallas_call(
        functools.partial(join_kernel, len(pairs)),
        out_shape=[jax.ShapeDtypeStruct(a.shape, kind) for (a, _), kind in zip(pairs, types)],
        in_specs=[vmem] * (2 * len(pairs)) + [pl.BlockSpec(memory_space=pl.ANY)] * len(deps),
        out_specs=[vmem] * len(pairs),
        compiler_params=pltpu.CompilerParams(vmem_limit_bytes=VMEM_BYTES),
        name="join",
    )(*[x for pair in pairs for x in pair], *deps)


def even_kernel(sides, group, groups, use_ends, use_inner, starts, spot_ref, *refs):
    views = [ref.at[at:at + 2 * groups] for ref, at in zip(refs[:2 * sides], starts)]
    inner_blocks, end_blocks = views[:sides], views[sides:]
    tables, low_ref = refs[2 * sides:2 * sides + 2]
    total, even, spread, sems = refs[-4:]
    here = spot_ref[0]
    step = pl.program_id(0)
    inner = jnp.logical_and(here > 0, here < sides - 1)
    work = jnp.logical_or(jnp.logical_and(inner, use_inner), jnp.logical_and(jnp.logical_not(inner), use_ends))

    @pl.when(work)
    def _():
        @pl.when(step == 0)
        def _():
            @pl.when(inner)
            def _():
                for at, turn in enumerate((0, 1, 3, 2)):
                    fetch(inner_blocks[at], even.at[here ^ turn], sems.at[at])

            @pl.when(jnp.logical_not(inner))
            def _():
                for at, turn in enumerate((0, 1, 2, 3)):
                    fetch(end_blocks[at], even.at[here ^ turn], sems.at[at])

            total[...] = jnp.zeros_like(total)
            for at in range(sides):
                pltpu.make_async_copy(inner_blocks[at], even.at[at], sems.at[at]).wait()

        expand(even, step, group, groups, (tables,), spread)
        count = spread.shape[1] * spread.shape[2]
        full = total.shape[2]
        both = spread[...].reshape(2, count, group * LANES)
        got = jnp.dot(both[0], low_ref[...], preferred_element_type=jnp.float32)
        total[0] += got[:, :full]
        total[1] += got[:, full:] + jnp.dot(both[1], low_ref[:, :full], preferred_element_type=jnp.float32)

    @pl.when(jnp.logical_and(step == 0, jnp.logical_not(work)))
    def _():
        total[...] = jnp.zeros_like(total)


def even_product(spot, inner_blocks, end_blocks, deps, table, low, sides, group, groups):
    some = inner_blocks or end_blocks
    use_inner, use_ends = inner_blocks is not None, end_blocks is not None
    blocks = (inner_blocks or some) + (end_blocks or some)
    starts = [at for _, at in blocks]
    _, planes, rows, _ = some[0][0].shape
    windows = table.shape[2] // LANES
    full = low.shape[-1] // 2
    count = windows * sides * rows
    whole = lambda arr: pl.BlockSpec(arr.shape, lambda g, s: (0,) * len(arr.shape))

    def busy(spot_ref):
        end = jnp.logical_or(spot_ref[0] == 0, spot_ref[0] == sides - 1)
        return jnp.where(jnp.where(end, use_ends, use_inner), 1, 0)

    part = pl.BlockSpec((group * LANES, 2 * full), lambda g, s: (g * busy(s), 0))
    out = jax.ShapeDtypeStruct((2, count, full), jnp.float32)
    depth = groups * group
    flops = 2 * count * depth * LANES * 3 * full + 4 * sides * rows * depth * 3 * LANES * windows * LANES
    return pl.pallas_call(
        functools.partial(even_kernel, sides, group, groups, use_ends, use_inner, starts),
        out_shape=out,
        grid_spec=pltpu.PrefetchScalarGridSpec(
            num_scalar_prefetch=1,
            grid=(groups,),
            in_specs=[pl.BlockSpec(memory_space=pl.ANY)] * (2 * sides)
            + [whole(table), part]
            + [pl.BlockSpec(memory_space=pl.ANY)] * len(deps),
            out_specs=whole(out),
            scratch_shapes=[
                pltpu.VMEM((sides, 2 * groups, planes, rows, LANES), jnp.bfloat16),
                pltpu.VMEM((2, windows, sides * rows, group * LANES), jnp.bfloat16),
                pltpu.SemaphoreType.DMA((sides,)),
            ],
        ),
        compiler_params=pltpu.CompilerParams(vmem_limit_bytes=VMEM_BYTES),
        cost_estimate=pl.CostEstimate(flops=flops, bytes_accessed=20 * 2 ** 20, transcendentals=0),
        name="even_product",
    )(spot, *[ref for ref, _ in blocks], table, low, *deps)


def odd_kernel(sides, group, groups, outs, starts, spot_ref, *refs):
    blocks = [ref.at[at:at + groups] for ref, at in zip(refs[:sides], starts)]
    inner_part, end_part = refs[sides:sides + 2]
    tables, next_tables, low_ref, next_low_ref = refs[sides + 2:sides + 6]
    out_refs = refs[-4 - outs:-4]
    odd, spread, total, sems = refs[-4:]
    here, role = spot_ref[0], spot_ref[1]
    step, last = pl.program_id(0), pl.num_programs(0) - 1
    inner = jnp.logical_and(here > 0, here < sides - 1)

    @pl.when(step == 0)
    def _():
        @pl.when(inner)
        def _():
            fetch(inner_part, total, sems.at[sides])
            for at, turn in enumerate((0, 1, 3, 2)):
                fetch(blocks[at], odd.at[here ^ turn], sems.at[at])
            for at in range(sides):
                pltpu.make_async_copy(blocks[at], odd.at[at], sems.at[at]).wait()

        @pl.when(jnp.logical_not(inner))
        def _():
            fetch(end_part, total, sems.at[sides])

        pltpu.make_async_copy(inner_part, total, sems.at[sides]).wait()

    @pl.when(inner)
    def _():
        expand(odd, step, group, groups, (tables, next_tables), spread)
        count = spread.shape[1] * spread.shape[2]
        rows = spread[...].reshape(2, count, group * LANES)
        total[1] += jnp.dot(rows[0], low_ref[...], preferred_element_type=jnp.float32)
        total[1] += jnp.dot(rows[1], next_low_ref[...], preferred_element_type=jnp.float32)

    @pl.when(step == last)
    def _():
        for offset in range(outs):
            which = offset ^ role
            value = total[which // 2]
            width = value.shape[1] // 2
            value = jnp.where(which % 2 == 1, value[:, width:], value[:, :width])
            out_refs[offset][...] = value.reshape(out_refs[offset].shape).astype(jnp.bfloat16)


def odd_product(spot, blocks, inner_part, end_part, deps, tables, lows, sides, group, groups, outs):
    starts = [at for _, at in blocks]
    _, planes, rows, _ = blocks[0][0].shape
    table, next_table = tables
    low, next_low = lows
    windows = table.shape[2] // LANES
    full = low.shape[-1]
    count = windows * sides * rows
    whole = lambda arr: pl.BlockSpec(arr.shape, lambda g, s: (0,) * len(arr.shape))

    def busy(spot_ref):
        return jnp.where(jnp.logical_or(spot_ref[0] == 0, spot_ref[0] == sides - 1), 0, 1)

    part = pl.BlockSpec((group * LANES, full), lambda g, s: (g * busy(s), 0))
    out = [jax.ShapeDtypeStruct((windows, sides * rows, full // 2), jnp.bfloat16)] * outs
    depth = groups * group
    flops = 2 * count * depth * LANES * 2 * full + 4 * sides * rows * depth * 3 * LANES * windows * LANES
    return pl.pallas_call(
        functools.partial(odd_kernel, sides, group, groups, outs, starts),
        out_shape=out,
        grid_spec=pltpu.PrefetchScalarGridSpec(
            num_scalar_prefetch=1,
            grid=(groups,),
            in_specs=[pl.BlockSpec(memory_space=pl.ANY)] * (sides + 2)
            + [whole(table), whole(next_table), part, part]
            + [pl.BlockSpec(memory_space=pl.ANY)] * len(deps),
            out_specs=[whole(o) for o in out],
            scratch_shapes=[
                pltpu.VMEM((sides, groups, planes, rows, LANES), jnp.bfloat16),
                pltpu.VMEM((2, windows, sides * rows, group * LANES), jnp.bfloat16),
                pltpu.VMEM((2, count, full), jnp.float32),
                pltpu.SemaphoreType.DMA((sides + 1,)),
            ],
        ),
        compiler_params=pltpu.CompilerParams(vmem_limit_bytes=VMEM_BYTES),
        cost_estimate=pl.CostEstimate(flops=flops, bytes_accessed=20 * 2 ** 20, transcendentals=0),
        name="odd_product",
    )(spot, *[ref for ref, _ in blocks], inner_part, end_part, table, next_table, low, next_low, *deps)


def on_device(sizes, tops, bottoms, left_iso, right_iso):
    roles, contrs, sides = sizes
    role = lax.axis_index("role")
    here = lax.axis_index("horiz")
    kinds, depth_all, rows_all, width = tops.shape
    depth = depth_all // roles
    group = group_size(depth)
    groups = depth // group
    share = right_iso.shape[0]
    chunks = split_sizes(rows_all, share)
    unit = share // chunks
    rows = rows_all // chunks
    windows = left_iso.shape[1]
    slab = left_iso.shape[2]
    downs, full = bottoms.shape[3], bottoms.shape[4]
    spot = jnp.stack([here, role]).astype(jnp.int32)

    cut = tops.reshape(kinds, depth_all, contrs, chunks, unit, width)

    def exchange(first, count, place):
        got = []
        for s in range(roles):
            piece = lax.dynamic_slice(
                cut, (0, (place ^ s) * depth, 0, first, 0, 0), (kinds, depth, contrs, count, unit, width)
            ).transpose(3, 0, 1, 2, 4, 5).reshape(count, kinds, depth, rows, width)
            if s:
                piece = lax.ppermute(piece, "role", [(j, j ^ s) for j in range(roles)])
            got.append(piece)
        for t in range(count):
            pieces[first + t] = (got, t)

    def lower(kind, place):
        low = lax.dynamic_slice(
            bottoms, (kind, place * depth, 0, 0, 0), (1, depth, slab, downs, full)
        )
        return low.reshape(depth, slab, downs * full)

    pairs = [(z, z ^ 1) for z in range(sides)]
    hand = [(z, z ^ 1) for z in (0, sides - 1)]
    cross = [(z, z ^ 3) for z in range(1, sides - 1)]
    move = lambda value, perm: lax.ppermute(value, "horiz", perm)

    pieces = {}
    exchange(0, 1, role)
    left_all = jnp.concatenate(
        [lax.dynamic_slice_in_dim(left_iso, (role ^ s) * width, width, 0) for s in range(roles)], axis=0
    )
    total = left_all.shape[0]
    mains = total // LANES
    rest = total - mains * LANES
    plane = (mains * group + (group + 1) // 2, rows, LANES)

    def table(flat_left):
        wide = flat_left.reshape(total, windows, slab)
        return jnp.pad(wide, ((0, 0), (0, 0), (0, LANES - slab))).reshape(total, windows * LANES)

    flat_left = left_all.reshape(total, windows * slab)
    middle = lower(1, role) * jnp.asarray(2, bottoms.dtype)
    tiles = (slab // rows, downs * full // LANES)
    count = depth * tiles[0] * tiles[1]
    units = -(-count // plane[0])
    carried = make_planes(middle, group, tiles, rows, units * plane[0]).reshape((units,) + plane)
    taken = 0

    def take(most):
        nonlocal taken
        at, size = taken, min(most, units - taken)
        taken += size
        return at, size

    own, sent, straight, turned, last = {}, {}, {}, {}, {}
    sums, shares, reduced = {}, {}, {}
    parts = []
    near_low = None
    done = None

    def send_core(t):
        stages[t] = [lax.ppermute(shares[t][s], "role", [(j, j ^ 1) for j in range(roles)]) for s in (1, 3)]

    def join_core(t, deps):
        kept, give = join([(shares[t][0], stages[t][0]), (shares[t][2], stages[t][1])], deps)
        stages[t] = [kept, lax.ppermute(give, "role", [(j, j ^ 2) for j in range(roles)])]
        return kept

    def join_chip(t, deps):
        summed = join([tuple(stages[t])], deps)[0]
        size, step = sides * contrs, contrs // 2
        stages[t] = halve(summed.reshape(windows, size, unit, full), size, step) + (size // 2, step // 2)
        return summed

    def halve(summed, size, step):
        bit = (lax.axis_index("contr") // step) % 2
        keep = lax.dynamic_slice_in_dim(summed, bit * (size // 2), size // 2, 1)
        give = lax.dynamic_slice_in_dim(summed, (1 - bit) * (size // 2), size // 2, 1).astype(jnp.bfloat16)
        return keep, lax.ppermute(give, "contr", [(j, j ^ step) for j in range(contrs)])

    def join_contr(t, deps):
        keep, got, size, step = stages[t]
        summed = join([(keep, got)], deps)[0]
        while step:
            summed = join([halve(summed, size, step)], [])[0]
            size, step = size // 2, step // 2
        reduced[t] = summed
        return summed

    stages, extra = {}, []
    for r in range(chunks + 3):
        if r <= chunks:
            fresh = r < chunks
            base = 3 * groups if fresh else 0
            most = {0: 2, 1: 3}.get(r, 1) * groups if fresh else 0
            at, size = take(most)
            length = max(base + size, 4 * groups) if fresh else 2 * groups
            given = dict(
                sides=sides, groups=groups, back=2 * groups if fresh else 0, kind=base, low=at, count=size
            )
            deps = [sent[r - 1]] if r else []
            deps += [sums[r - 1]] if r - 1 in sums else []
            out, mine, mark = pack(
                spot, pieces.pop(r) if fresh else ([], 0), straight.get(r - 1), carried, deps + extra, given,
                group, plane, length,
            )
            extra = []
            sent[r] = move(out, pairs)
            if size:
                parts.append((at, sent[r], base, size))
            if fresh:
                own[r] = mine
                straight[r] = move(mine, cross)
            done = out
            if 2 * r + 1 < chunks:
                exchange(2 * r + 1, min(2, chunks - 2 * r - 1), mark[1])
            if r == 0:
                late = mark[1]
                first_table = make_table(table(flat_left), [out], rest)
                low = make_lows([lower(0, late), lower(2, late)], group)
                near_left = move(flat_left, hand)
        t = r - 4
        if 0 <= t < chunks:
            if near_low is None:
                near_low = low_of_planes(
                    sorted(parts, key=lambda p: p[0]), [done], units, group, groups, tiles
                )
                near_table = make_table(table(near_left), [done], rest)
            blocks = [(own[t], 2 * groups), (sent[t], 2 * groups), (straight[t], 2 * groups), (turned[t + 1], 2 * groups)]
            shares[t] = odd_product(
                spot, blocks, sums[t + 2], sums[t + 3], [done] + extra, (first_table, near_table),
                (middle_low, near_low), sides, group, groups, roles,
            )
            done = shares[t][0]
            extra = []
            send_core(t)
            if t - 1 in stages:
                extra.append(join_chip(t - 1, [done]))
        if 1 <= r <= chunks + 1:
            at, size = take(2 * groups) if 2 <= r else (0, 0)
            given = dict(sides=sides, groups=groups, cross=r <= chunks, low=at, count=size)
            deps = [done] + ([last[r - 1]] if r - 1 in last else [])
            outs = pass_on(spot, sent[r - 1], turned.get(r - 1), carried, deps + extra, given, plane)
            extra = []
            if r <= chunks:
                turned[r] = move(outs[0], cross)
            if r - 1 in turned:
                last[r] = move(outs[-1], pairs)
                if size:
                    parts.append((at, last[r], 0, size))
            done = outs[0]
        if r == 1:
            extra = [low, first_table]
        if r == 2:
            middle_low = make_lows([middle], group)
        if r >= 2:
            t = r - 2
            inner_blocks = end_blocks = None
            if t < chunks:
                inner_blocks = [(own[t], 0), (sent[t], 0), (straight[t], 0), (turned[t + 1], 0)]
            t = r - 3
            if 0 <= t:
                end_blocks = [
                    (own[t], 0), (sent[t], 0), (sent[t + 1], 2 * groups if t + 1 < chunks else 0), (last[t + 2], 0)
                ]
            sums[r] = even_product(
                spot, inner_blocks, end_blocks, [done] + extra, first_table, low, sides, group, groups
            )
            done = sums[r]
            extra = []
            if r - 4 in shares:
                extra.append(join_core(r - 4, [done]))
            if r - 5 in shares:
                extra.append(join_contr(r - 5, [done]))
    t = chunks - 1
    blocks = [(own[t], 2 * groups), (sent[t], 2 * groups), (straight[t], 2 * groups), (turned[t + 1], 2 * groups)]
    shares[t] = odd_product(
        spot, blocks, sums[t + 2], sums[t + 3], [done] + extra, (first_table, near_table),
        (middle_low, near_low), sides, group, groups, roles,
    )
    send_core(t)
    join_chip(t - 1, [shares[t][0]])
    join_core(t, [])
    join_contr(t - 1, [])
    join_chip(t, [])
    join_contr(t, [])

    summed = jnp.concatenate([reduced[t] for t in range(chunks)], axis=2)
    mine = lax.dynamic_slice_in_dim(summed, here, 1, 1)
    for s in range(1, sides):
        give = lax.dynamic_slice_in_dim(summed, here ^ s, 1, 1).astype(jnp.bfloat16)
        got = lax.ppermute(give, "horiz", [(z, z ^ s) for z in range(sides)])
        mine = mine + got.astype(jnp.float32)
    mine = mine.reshape(windows, share, full).astype(jnp.bfloat16)
    projected = jnp.einsum("aur,urb->ab", mine, right_iso, preferred_element_type=jnp.float32)
    projected = projected * jnp.where(role >= downs, 0.25, 1.0)
    for axis, size in (("contr", contrs), ("horiz", sides)):
        s = 1
        while s < size:
            projected = projected + lax.ppermute(projected, axis, [(j, j ^ s) for j in range(size)])
            s *= 2
    found = [projected] + [
        lax.ppermute(projected, "role", [(j, j ^ s) for j in range(roles)]) for s in range(1, roles)
    ]
    found = jnp.stack(found)
    order = [lax.dynamic_index_in_dim(found, q ^ role, 0, keepdims=False) for q in range(roles)]
    return jnp.stack(order).reshape(roles // downs, downs, windows, -1)


def solution(mesh):
    placed = (
        P(None, "contr", "horiz", "role"),
        P(None, "contr", "horiz", None, None),
        P(None, None, "horiz"),
        P(("contr", "horiz"), None, None),
    )
    sizes = tuple(mesh.shape[axis] for axis in ("role", "contr", "horiz"))
    body = functools.partial(on_device, sizes)
    return jax.shard_map(body, mesh=mesh, in_specs=placed, out_specs=P(), check_vma=False)
```

```python
import functools

import jax
import jax.numpy as jnp
from jax import lax
from jax.experimental import pallas as pl
from jax.experimental.pallas import tpu as pltpu
from jax.sharding import PartitionSpec as P

LANES = 128
ROWS = 16
VMEM_BYTES = 60 * 2 ** 20


def split_sizes(total, count):
    best = 1
    for n in range(1, count + 1):
        if count % n == 0 and total % n == 0 and (total // n) % ROWS == 0:
            best = n
    return best


def group_size(depth):
    best = depth
    for size in range(2, 21, 2):
        if depth % size == 0:
            best = size
    return best


def row_of(k, slab):
    each = 2 * LANES // slab
    return k // each * 2 * LANES + k % each * slab


def rows_of(group, slab):
    return -(-(row_of(group - 1, slab) + slab) // LANES) * LANES


def pack_kernel(group, parts, given, spot_ref, *refs):
    pieces, crossed_ref, low_ref = refs[:parts], refs[parts], refs[parts + 1]
    sent_ref, own_ref, mark_ref, sem = refs[-4:] if parts else (refs[-3], None, refs[-2], refs[-1])
    here = spot_ref[0]
    sides = given["sides"]
    inner = jnp.logical_and(here > 0, here < sides - 1)
    groups, back_at, low_at, low_count, kind_at = (
        given["groups"], given["back"], given["low"], given["count"], given["kind"]
    )
    mark_ref[0] = spot_ref[0]
    mark_ref[1] = spot_ref[1]

    def back():
        return pltpu.make_async_copy(
            crossed_ref.at[0:2 * groups], sent_ref.at[back_at:back_at + 2 * groups], sem
        )

    def lower():
        return pltpu.make_async_copy(
            low_ref.at[low_at:low_at + low_count], sent_ref.at[kind_at:kind_at + low_count], sem
        )

    if given["has_back"]:
        @pl.when(inner)
        def _():
            back().start()
    if low_count:
        @pl.when(jnp.logical_not(inner))
        def _():
            lower().start()

    if parts:
        kinds, depth, rows, width = pieces[0].shape
        total = width * parts
        mains = total // LANES
        rest = total - mains * LANES
        half = (group + 1) // 2

        def place(slot, shift):
            shape = (width, (mains + 1) * LANES)
            target = slot * width + lax.broadcasted_iota(jnp.int32, shape, 0)
            target = jnp.where(target >= mains * LANES, target + shift, target)
            hit = lax.broadcasted_iota(jnp.int32, shape, 1) == target
            return jnp.where(hit, 1.0, 0.0).astype(jnp.bfloat16)

        tables = [[place(s, shift) for s in range(parts)] for shift in (0, rest)]
        for kind in range(kinds):
            base = (0, 2, 1)[kind] * groups

            def put(lo, hi, value):
                value = value.astype(jnp.bfloat16)
                own_ref[base:base + groups, lo:hi] = value
                if kind != 1:
                    sent_ref[base:base + groups, lo:hi] = value
                else:
                    @pl.when(jnp.logical_not(inner))
                    def _():
                        sent_ref[base:base + groups, lo:hi] = value

            tails = []
            for part, (lo, hi) in enumerate(((0, half), (half, group))):
                if lo == hi:
                    continue
                got = 0.0
                for slot, ref in enumerate(pieces):
                    block = ref[kind].reshape(groups, group, rows, width)[:, lo:hi]
                    got = got + jnp.dot(
                        block.reshape(groups * (hi - lo) * rows, width),
                        tables[part][slot],
                        preferred_element_type=jnp.float32,
                    )
                got = got.reshape(groups, hi - lo, rows, (mains + 1) * LANES)
                for main in range(mains):
                    put(main * group + lo, main * group + hi, got[..., main * LANES:(main + 1) * LANES])
                tails.append(got[..., mains * LANES:])
            start = mains * group
            first = tails[0]
            if len(tails) == 1:
                put(start, start + half, first)
            else:
                both = tails[1].shape[1]
                put(start, start + both, first[:, :both] + tails[1])
                if both < half:
                    put(start + both, start + half, first[:, both:])

    if given["has_back"]:
        @pl.when(inner)
        def _():
            back().wait()
    if low_count:
        @pl.when(jnp.logical_not(inner))
        def _():
            lower().wait()


def pack(spot, pieces, crossed, low, deps, given, group, plane, length):
    has_back = crossed is not None
    pieces, turn = pieces
    given = dict(given, has_back=has_back)
    groups = given["groups"]
    out = [jax.ShapeDtypeStruct((length,) + plane, jnp.bfloat16)]
    specs = [pl.BlockSpec(memory_space=pltpu.VMEM)]
    if pieces:
        out.append(jax.ShapeDtypeStruct((3 * groups,) + plane, jnp.bfloat16))
        specs.append(pl.BlockSpec(memory_space=pltpu.VMEM))
    out.append(jax.ShapeDtypeStruct((2,), jnp.int32))
    specs.append(pl.BlockSpec(memory_space=pltpu.SMEM))
    anywhere = pl.BlockSpec(memory_space=pl.ANY)
    operands = [crossed if has_back else low, low] + list(deps)
    got = pl.pallas_call(
        functools.partial(pack_kernel, group, len(pieces), given),
        out_shape=out,
        grid=(1,),
        in_specs=[pl.BlockSpec(memory_space=pltpu.SMEM)]
        + [pl.BlockSpec((None,) + piece.shape[1:], lambda g: (turn, 0, 0, 0, 0)) for piece in pieces]
        + [anywhere] * len(operands),
        out_specs=specs,
        scratch_shapes=[pltpu.SemaphoreType.DMA],
        compiler_params=pltpu.CompilerParams(vmem_limit_bytes=VMEM_BYTES),
        cost_estimate=pl.CostEstimate(flops=2 * 10 ** 9, bytes_accessed=6 * 2 ** 20, transcendentals=0),
        name="pack",
    )(spot, *pieces, *operands)
    return (got[0], got[1], got[2]) if pieces else (got[0], None, got[1])


def pass_kernel(given, spot_ref, *refs):
    received_ref, crossed_ref, low_ref = refs[:3]
    outs, sems = refs[given["inputs"]:-1], refs[-1]
    here = spot_ref[0]
    sides, groups = given["sides"], given["groups"]
    inner = jnp.logical_and(here > 0, here < sides - 1)
    low_at, low_count = given["low"], given["count"]
    copies = []
    if given["cross"]:
        copies.append((None, pltpu.make_async_copy(received_ref.at[0:3 * groups], outs[0], sems.at[0])))
    if given["back"]:
        copies.append((inner, pltpu.make_async_copy(crossed_ref.at[0:2 * groups], outs[-1], sems.at[1])))
    if low_count:
        copies.append(
            (
                jnp.logical_not(inner),
                pltpu.make_async_copy(
                    low_ref.at[low_at:low_at + low_count], outs[-1].at[0:low_count], sems.at[2]
                ),
            )
        )
    for act in ("start", "wait"):
        for where, copy in copies:
            if where is None:
                getattr(copy, act)()
            else:
                pl.when(where)(getattr(copy, act))


def pass_on(spot, received, crossed, low, deps, given, plane):
    groups = given["groups"]
    given = dict(given, back=crossed is not None, inputs=3 + len(deps))
    out = []
    if given["cross"]:
        out.append(jax.ShapeDtypeStruct((3 * groups,) + plane, jnp.bfloat16))
    if given["back"]:
        out.append(jax.ShapeDtypeStruct((2 * groups,) + plane, jnp.bfloat16))
    anywhere = pl.BlockSpec(memory_space=pl.ANY)
    operands = [received, crossed if crossed is not None else low, low] + list(deps)
    return pl.pallas_call(
        functools.partial(pass_kernel, given),
        out_shape=out,
        in_specs=[pl.BlockSpec(memory_space=pltpu.SMEM)] + [anywhere] * len(operands),
        out_specs=[pl.BlockSpec(memory_space=pltpu.VMEM)] * len(out),
        scratch_shapes=[pltpu.SemaphoreType.DMA((3,))],
        compiler_params=pltpu.CompilerParams(vmem_limit_bytes=VMEM_BYTES),
        cost_estimate=pl.CostEstimate(flops=0, bytes_accessed=4 * 2 ** 20, transcendentals=0),
        name="pass_on",
    )(spot, *operands)


def fetch(src, dst, sem):
    pltpu.make_async_copy(src, dst, sem).start()


def expand(source, step, group, groups, tables, spread, slab):
    sides, _, plane, rows, _ = source.shape
    kinds = source.shape[1] // groups
    half = (group + 1) // 2
    mains = (plane - half) // group
    windows = spread.shape[1]
    each = tables[0].shape[0]
    rest = tables[0].shape[1] - mains * LANES - LANES // 2
    lane = lax.broadcasted_iota(jnp.int32, (sides * rows, LANES), 1)
    keeps = [jnp.where(side, 1.0, 0.0).astype(jnp.bfloat16) for side in (lane < rest, lane >= rest)]

    def row(kind, k):
        def block(at):
            return source[:, kind * groups + step, at].reshape(sides * rows, LANES)

        last = block(mains * group + (k if k < half else k - half)) * keeps[0 if k < half else 1]
        return jnp.concatenate([block(main * group + k) for main in range(mains)] + [last], axis=1)

    wides = []
    for turn in range(min(each, group)):
        wides.append(
            jnp.concatenate([row(kind, k) for kind in range(kinds) for k in range(turn, group, each)], axis=0)
        )
    for slot, table in enumerate(tables):
        got = [
            jnp.dot(wide, table[turn], preferred_element_type=jnp.float32).reshape(
                kinds, -1, sides * rows, windows * LANES
            )
            for turn, wide in enumerate(wides)
        ]
        for kind in range(kinds):
            for first in range(0, group, each):
                members = range(first, min(first + each, group))
                for a in range(windows):
                    window = slice(a * LANES, (a + 1) * LANES)
                    for tile in range(2):
                        value = None
                        for k in members:
                            start = (k - first) * slab - tile * LANES
                            if start + slab <= 0 or start >= LANES:
                                continue
                            mine = got[k - first][kind, k // each, :, window]
                            value = mine if value is None else jnp.where(lane >= start, mine, value)
                        if value is not None:
                            at = first // each * 2 * LANES + tile * LANES
                            spread[slot + kind, a, :, at:at + LANES] = value.astype(jnp.bfloat16)


def table_kernel(windows, slab, left_ref, *refs):
    out_ref = refs[-1]
    total, lanes = left_ref.shape
    rest = LANES // 2
    mains = total - rest
    shape = (lanes, windows * LANES)
    source = lax.broadcasted_iota(jnp.int32, shape, 0)
    target = lax.broadcasted_iota(jnp.int32, shape, 1)
    for turn in range(out_ref.shape[0]):
        column = (source // slab) * LANES + (source % slab + turn * slab) % LANES
        select = jnp.where(column == target, 1.0, 0.0).astype(jnp.bfloat16)
        got = jnp.dot(left_ref[...], select, preferred_element_type=jnp.float32).astype(jnp.bfloat16)
        out_ref[turn, 0:total] = got
        out_ref[turn, total:total + rest] = got[mains:total]


def make_table(left, deps, windows, slab):
    total, lanes = left.shape
    vmem = pl.BlockSpec(memory_space=pltpu.VMEM)
    return pl.pallas_call(
        functools.partial(table_kernel, windows, slab),
        out_shape=jax.ShapeDtypeStruct((2 * LANES // slab, total + LANES // 2, windows * LANES), left.dtype),
        in_specs=[vmem] + [pl.BlockSpec(memory_space=pl.ANY)] * len(deps),
        out_specs=vmem,
        compiler_params=pltpu.CompilerParams(vmem_limit_bytes=VMEM_BYTES),
        name="make_table",
    )(left, *deps)


def low_kernel(*refs):
    parts, out_ref = refs[:-1], refs[-1]
    group, slab, lanes = parts[0].shape
    out_ref[...] = jnp.zeros_like(out_ref)
    for k in range(group):
        for at, ref in enumerate(parts):
            row = row_of(k, slab)
            out_ref[row:row + slab, at * lanes:(at + 1) * lanes] = ref[k]


def make_lows(parts, group):
    depth, slab, lanes = parts[0].shape
    block = pl.BlockSpec((group, slab, lanes), lambda g: (g, 0, 0))
    return pl.pallas_call(
        low_kernel,
        out_shape=jax.ShapeDtypeStruct((depth // group * rows_of(group, slab), len(parts) * lanes), parts[0].dtype),
        grid=(depth // group,),
        in_specs=[block] * len(parts),
        out_specs=pl.BlockSpec((rows_of(group, slab), len(parts) * lanes), lambda g: (g, 0)),
        compiler_params=pltpu.CompilerParams(vmem_limit_bytes=VMEM_BYTES),
        name="make_lows",
    )(*parts)


def split_kernel(tiles, low_ref, out_ref):
    group, rows = low_ref.shape[0], out_ref.shape[1]
    for k in range(group):
        for i in range(tiles[0]):
            for j in range(tiles[1]):
                out_ref[(k * tiles[0] + i) * tiles[1] + j] = low_ref[
                    k, i * rows:(i + 1) * rows, j * LANES:(j + 1) * LANES
                ]


def make_planes(low, group, tiles, rows, planes):
    depth, slab, lanes = low.shape
    each = group * tiles[0] * tiles[1]
    return pl.pallas_call(
        functools.partial(split_kernel, tiles),
        out_shape=jax.ShapeDtypeStruct((planes, rows, LANES), low.dtype),
        grid=(depth // group,),
        in_specs=[pl.BlockSpec((group, slab, lanes), lambda g: (g, 0, 0))],
        out_specs=pl.BlockSpec((each, rows, LANES), lambda g: (g, 0, 0)),
        compiler_params=pltpu.CompilerParams(vmem_limit_bytes=VMEM_BYTES),
        name="make_planes",
    )(low)


def planes_kernel(spans, group, groups, tiles, *refs):
    parts = refs[:len(spans)]
    out_ref, held, sems = refs[-3:]
    step = pl.program_id(0)

    @pl.when(step == 0)
    def _():
        copies = [
            pltpu.make_async_copy(ref.at[first:first + size], held.at[at:at + size], sems.at[i])
            for i, (ref, (at, first, size)) in enumerate(zip(parts, spans))
        ]
        for copy in copies:
            copy.start()
        for copy in copies:
            copy.wait()

    out_ref[...] = jnp.zeros_like(out_ref)
    planes, rows = held.shape[1], held.shape[2]
    each = group * tiles[0] * tiles[1]
    for k in range(group):
        for i in range(tiles[0]):
            for j in range(tiles[1]):
                at = (k * tiles[0] + i) * tiles[1] + j
                if groups == 1:
                    plane = held[at // planes, at % planes]
                elif each % planes == 0:
                    plane = held[step * (each // planes) + at // planes, at % planes]
                else:
                    plane = held[(step * each + at) // planes, (step * each + at) % planes]
                row = row_of(k, tiles[0] * rows) + i * rows
                out_ref[row:row + rows, j * LANES:(j + 1) * LANES] = plane


def low_of_planes(parts, deps, units, group, groups, tiles):
    spans = [(at, first, size) for at, _, first, size in parts]
    shape = parts[0][1].shape[1:]
    height = rows_of(group, tiles[0] * shape[1])
    anywhere = pl.BlockSpec(memory_space=pl.ANY)
    return pl.pallas_call(
        functools.partial(planes_kernel, spans, group, groups, tiles),
        out_shape=jax.ShapeDtypeStruct((groups * height, tiles[1] * LANES), jnp.bfloat16),
        grid=(groups,),
        in_specs=[anywhere] * (len(parts) + len(deps)),
        out_specs=pl.BlockSpec((height, tiles[1] * LANES), lambda g: (g, 0)),
        scratch_shapes=[
            pltpu.VMEM((units,) + shape, jnp.bfloat16),
            pltpu.SemaphoreType.DMA((len(parts),)),
        ],
        compiler_params=pltpu.CompilerParams(vmem_limit_bytes=VMEM_BYTES),
        name="low_of_planes",
    )(*[got for _, got, _, _ in parts], *deps)


def join_kernel(count, *refs):
    outs = refs[-count:]
    for i in range(count):
        outs[i][...] = (refs[2 * i][...].astype(jnp.float32) + refs[2 * i + 1][...].astype(jnp.float32)).astype(
            outs[i].dtype
        )


def join(pairs, deps):
    vmem = pl.BlockSpec(memory_space=pltpu.VMEM)
    types = [jnp.float32] + [jnp.bfloat16] * (len(pairs) - 1)
    return pl.pallas_call(
        functools.partial(join_kernel, len(pairs)),
        out_shape=[jax.ShapeDtypeStruct(a.shape, kind) for (a, _), kind in zip(pairs, types)],
        in_specs=[vmem] * (2 * len(pairs)) + [pl.BlockSpec(memory_space=pl.ANY)] * len(deps),
        out_specs=[vmem] * len(pairs),
        compiler_params=pltpu.CompilerParams(vmem_limit_bytes=VMEM_BYTES),
        name="join",
    )(*[x for pair in pairs for x in pair], *deps)


def even_kernel(sides, group, groups, slab, use_ends, use_inner, starts, spot_ref, *refs):
    views = [ref.at[at:at + 2 * groups] for ref, at in zip(refs[:2 * sides], starts)]
    inner_blocks, end_blocks = views[:sides], views[sides:]
    tables, low_ref = refs[2 * sides:2 * sides + 2]
    total, even, spread, sems = refs[-4:]
    here = spot_ref[0]
    step = pl.program_id(0)
    inner = jnp.logical_and(here > 0, here < sides - 1)
    work = jnp.logical_or(jnp.logical_and(inner, use_inner), jnp.logical_and(jnp.logical_not(inner), use_ends))

    @pl.when(work)
    def _():
        @pl.when(step == 0)
        def _():
            @pl.when(inner)
            def _():
                for at, turn in enumerate((0, 1, 3, 2)):
                    fetch(inner_blocks[at], even.at[here ^ turn], sems.at[at])

            @pl.when(jnp.logical_not(inner))
            def _():
                for at, turn in enumerate((0, 1, 2, 3)):
                    fetch(end_blocks[at], even.at[here ^ turn], sems.at[at])

            total[...] = jnp.zeros_like(total)
            for at in range(sides):
                pltpu.make_async_copy(inner_blocks[at], even.at[at], sems.at[at]).wait()

        expand(even, step, group, groups, (tables,), spread, slab)
        count = spread.shape[1] * spread.shape[2]
        full = total.shape[2]
        one = spread[0].reshape(count, spread.shape[3])
        two = spread[1].reshape(count, spread.shape[3])
        got = jnp.dot(one, low_ref[...], preferred_element_type=jnp.float32)
        total[0] += got[:, :full]
        total[1] += got[:, full:] + jnp.dot(two, low_ref[:, :full], preferred_element_type=jnp.float32)

    @pl.when(jnp.logical_and(step == 0, jnp.logical_not(work)))
    def _():
        total[...] = jnp.zeros_like(total)


def even_product(spot, inner_blocks, end_blocks, deps, table, low, sides, group, groups, slab):
    some = inner_blocks or end_blocks
    use_inner, use_ends = inner_blocks is not None, end_blocks is not None
    blocks = (inner_blocks or some) + (end_blocks or some)
    starts = [at for _, at in blocks]
    _, planes, rows, _ = some[0][0].shape
    height = rows_of(group, slab)
    windows = table.shape[2] // LANES
    full = low.shape[-1] // 2
    count = windows * sides * rows
    whole = lambda arr, **mode: pl.BlockSpec(arr.shape, lambda g, s: (0,) * len(arr.shape), **mode)
    once = dict(pipeline_mode=pl.Buffered(1))

    def busy(spot_ref):
        end = jnp.logical_or(spot_ref[0] == 0, spot_ref[0] == sides - 1)
        return jnp.where(jnp.where(end, use_ends, use_inner), 1, 0)

    part = pl.BlockSpec((height, 2 * full), lambda g, s: (g * busy(s), 0))
    out = jax.ShapeDtypeStruct((2, count, full), jnp.float32)
    flops = 2 * count * groups * height * 3 * full + 4 * sides * rows * groups * group * 3 * LANES * windows * LANES
    return pl.pallas_call(
        functools.partial(even_kernel, sides, group, groups, slab, use_ends, use_inner, starts),
        out_shape=out,
        grid_spec=pltpu.PrefetchScalarGridSpec(
            num_scalar_prefetch=1,
            grid=(groups,),
            in_specs=[pl.BlockSpec(memory_space=pl.ANY)] * (2 * sides)
            + [whole(table, **once), part]
            + [pl.BlockSpec(memory_space=pl.ANY)] * len(deps),
            out_specs=whole(out),
            scratch_shapes=[
                pltpu.VMEM((sides, 2 * groups, planes, rows, LANES), jnp.bfloat16),
                pltpu.VMEM((2, windows, sides * rows, height), jnp.bfloat16),
                pltpu.SemaphoreType.DMA((sides,)),
            ],
        ),
        compiler_params=pltpu.CompilerParams(vmem_limit_bytes=VMEM_BYTES),
        cost_estimate=pl.CostEstimate(flops=flops, bytes_accessed=20 * 2 ** 20, transcendentals=0),
        name="even_product",
    )(spot, *[ref for ref, _ in blocks], table, low, *deps)


def odd_kernel(sides, group, groups, slab, outs, starts, spot_ref, *refs):
    blocks = [ref.at[at:at + groups] for ref, at in zip(refs[:sides], starts)]
    inner_part, end_part = refs[sides:sides + 2]
    tables, next_tables, low_ref, next_low_ref = refs[sides + 2:sides + 6]
    out_refs = refs[-4 - outs:-4]
    odd, spread, total, sems = refs[-4:]
    here, role = spot_ref[0], spot_ref[1]
    step, last = pl.program_id(0), pl.num_programs(0) - 1
    inner = jnp.logical_and(here > 0, here < sides - 1)

    @pl.when(step == 0)
    def _():
        @pl.when(inner)
        def _():
            fetch(inner_part, total, sems.at[sides])
            for at, turn in enumerate((0, 1, 3, 2)):
                fetch(blocks[at], odd.at[here ^ turn], sems.at[at])
            for at in range(sides):
                pltpu.make_async_copy(blocks[at], odd.at[at], sems.at[at]).wait()

        @pl.when(jnp.logical_not(inner))
        def _():
            fetch(end_part, total, sems.at[sides])

        pltpu.make_async_copy(inner_part, total, sems.at[sides]).wait()

    @pl.when(inner)
    def _():
        expand(odd, step, group, groups, (tables, next_tables), spread, slab)
        count = spread.shape[1] * spread.shape[2]
        one = spread[0].reshape(count, spread.shape[3])
        two = spread[1].reshape(count, spread.shape[3])
        total[1] += jnp.dot(one, low_ref[...], preferred_element_type=jnp.float32)
        total[1] += jnp.dot(two, next_low_ref[...], preferred_element_type=jnp.float32)

    @pl.when(step == last)
    def _():
        for offset in range(outs):
            which = offset ^ role
            value = total[which // 2]
            width = value.shape[1] // 2
            value = jnp.where(which % 2 == 1, value[:, width:], value[:, :width])
            out_refs[offset][...] = value.reshape(out_refs[offset].shape).astype(jnp.bfloat16)


def odd_product(spot, blocks, inner_part, end_part, deps, tables, lows, sides, group, groups, slab, outs):
    starts = [at for _, at in blocks]
    _, planes, rows, _ = blocks[0][0].shape
    table, next_table = tables
    low, next_low = lows
    height = rows_of(group, slab)
    windows = table.shape[2] // LANES
    full = low.shape[-1]
    count = windows * sides * rows
    whole = lambda arr, **mode: pl.BlockSpec(arr.shape, lambda g, s: (0,) * len(arr.shape), **mode)
    once = dict(pipeline_mode=pl.Buffered(1))

    def busy(spot_ref):
        return jnp.where(jnp.logical_or(spot_ref[0] == 0, spot_ref[0] == sides - 1), 0, 1)

    part = pl.BlockSpec((height, full), lambda g, s: (g * busy(s), 0))
    out = [jax.ShapeDtypeStruct((windows, sides * rows, full // 2), jnp.bfloat16)] * outs
    flops = 2 * count * groups * height * 2 * full + 4 * sides * rows * groups * group * 3 * LANES * windows * LANES
    return pl.pallas_call(
        functools.partial(odd_kernel, sides, group, groups, slab, outs, starts),
        out_shape=out,
        grid_spec=pltpu.PrefetchScalarGridSpec(
            num_scalar_prefetch=1,
            grid=(groups,),
            in_specs=[pl.BlockSpec(memory_space=pl.ANY)] * (sides + 2)
            + [whole(table, **once), whole(next_table, **once), part, part]
            + [pl.BlockSpec(memory_space=pl.ANY)] * len(deps),
            out_specs=[whole(o) for o in out],
            scratch_shapes=[
                pltpu.VMEM((sides, groups, planes, rows, LANES), jnp.bfloat16),
                pltpu.VMEM((2, windows, sides * rows, height), jnp.bfloat16),
                pltpu.VMEM((2, count, full), jnp.float32),
                pltpu.SemaphoreType.DMA((sides + 1,)),
            ],
        ),
        compiler_params=pltpu.CompilerParams(vmem_limit_bytes=VMEM_BYTES),
        cost_estimate=pl.CostEstimate(flops=flops, bytes_accessed=20 * 2 ** 20, transcendentals=0),
        name="odd_product",
    )(spot, *[ref for ref, _ in blocks], inner_part, end_part, table, next_table, low, next_low, *deps)


def on_device(sizes, tops, bottoms, left_iso, right_iso):
    roles, contrs, sides = sizes
    role = lax.axis_index("role")
    here = lax.axis_index("horiz")
    kinds, depth_all, rows_all, width = tops.shape
    depth = depth_all // roles
    group = group_size(depth)
    groups = depth // group
    share = right_iso.shape[0]
    chunks = split_sizes(rows_all, share)
    unit = share // chunks
    rows = rows_all // chunks
    windows = left_iso.shape[1]
    slab = left_iso.shape[2]
    downs, full = bottoms.shape[3], bottoms.shape[4]
    spot = jnp.stack([here, role]).astype(jnp.int32)

    cut = tops.reshape(kinds, depth_all, contrs, chunks, unit, width)

    def exchange(first, count, place):
        got = []
        for s in range(roles):
            piece = lax.dynamic_slice(
                cut, (0, (place ^ s) * depth, 0, first, 0, 0), (kinds, depth, contrs, count, unit, width)
            ).transpose(3, 0, 1, 2, 4, 5).reshape(count, kinds, depth, rows, width)
            if s:
                piece = lax.ppermute(piece, "role", [(j, j ^ s) for j in range(roles)])
            got.append(piece)
        for t in range(count):
            pieces[first + t] = (got, t)

    def lower(kind, place):
        low = lax.dynamic_slice(
            bottoms, (kind, place * depth, 0, 0, 0), (1, depth, slab, downs, full)
        )
        return low.reshape(depth, slab, downs * full)

    pairs = [(z, z ^ 1) for z in range(sides)]
    hand = [(z, z ^ 1) for z in (0, sides - 1)]
    cross = [(z, z ^ 3) for z in range(1, sides - 1)]
    move = lambda value, perm: lax.ppermute(value, "horiz", perm)

    pieces = {}
    exchange(0, 1, role)
    left_all = jnp.concatenate(
        [lax.dynamic_slice_in_dim(left_iso, (role ^ s) * width, width, 0) for s in range(roles)], axis=0
    )
    total = left_all.shape[0]
    mains = total // LANES
    plane = (mains * group + (group + 1) // 2, rows, LANES)

    flat_left = left_all.reshape(total, windows * slab)
    middle = lower(1, role) * jnp.asarray(2, bottoms.dtype)
    tiles = (slab // rows, downs * full // LANES)
    count = depth * tiles[0] * tiles[1]
    units = -(-count // plane[0])
    carried = make_planes(middle, group, tiles, rows, units * plane[0]).reshape((units,) + plane)
    taken = 0

    def take(most):
        nonlocal taken
        at, size = taken, min(most, units - taken)
        taken += size
        return at, size

    own, sent, straight, turned, last = {}, {}, {}, {}, {}
    sums, shares, reduced = {}, {}, {}
    parts = []
    near_low = None
    done = None

    def send_core(t):
        stages[t] = [lax.ppermute(shares[t][s], "role", [(j, j ^ 1) for j in range(roles)]) for s in (1, 3)]

    def join_core(t, deps):
        kept, give = join([(shares[t][0], stages[t][0]), (shares[t][2], stages[t][1])], deps)
        stages[t] = [kept, lax.ppermute(give, "role", [(j, j ^ 2) for j in range(roles)])]
        return kept

    def join_chip(t, deps):
        summed = join([tuple(stages[t])], deps)[0]
        size, step = sides * contrs, contrs // 2
        stages[t] = halve(summed.reshape(windows, size, unit, full), size, step) + (size // 2, step // 2)
        return summed

    def halve(summed, size, step):
        bit = (lax.axis_index("contr") // step) % 2
        keep = lax.dynamic_slice_in_dim(summed, bit * (size // 2), size // 2, 1)
        give = lax.dynamic_slice_in_dim(summed, (1 - bit) * (size // 2), size // 2, 1).astype(jnp.bfloat16)
        return keep, lax.ppermute(give, "contr", [(j, j ^ step) for j in range(contrs)])

    def join_contr(t, deps):
        keep, got, size, step = stages[t]
        summed = join([(keep, got)], deps)[0]
        while step:
            summed = join([halve(summed, size, step)], [])[0]
            size, step = size // 2, step // 2
        reduced[t] = summed
        return summed

    stages, extra = {}, []
    for r in range(chunks + 3):
        if r <= chunks:
            fresh = r < chunks
            base = 3 * groups if fresh else 0
            most = {0: 2, 1: 3}.get(r, 1) * groups if fresh else 0
            at, size = take(most)
            length = max(base + size, 4 * groups) if fresh else 2 * groups
            given = dict(
                sides=sides, groups=groups, back=2 * groups if fresh else 0, kind=base, low=at, count=size
            )
            deps = [sent[r - 1]] if r else []
            deps += [sums[r - 1]] if r - 1 in sums else []
            out, mine, mark = pack(
                spot, pieces.pop(r) if fresh else ([], 0), straight.get(r - 1), carried, deps + extra, given,
                group, plane, length,
            )
            extra = []
            sent[r] = move(out, pairs)
            if size:
                parts.append((at, sent[r], base, size))
            if fresh:
                own[r] = mine
                straight[r] = move(mine, cross)
            done = out
            for first, size in {0: ((1, 1), (2, 1)), 1: ((3, chunks - 3),)}.get(r, ()):
                if size > 0 and first < chunks:
                    exchange(first, size, mark[1])
            if r == 0:
                late = mark[1]
                near_left = move(flat_left, hand)
                outer = [lower(0, late), lower(2, late)]
                extra = list(outer)
        t = r - 4
        if 0 <= t < chunks:
            if near_low is None:
                near_low = low_of_planes(
                    sorted(parts, key=lambda p: p[0]), [done], units, group, groups, tiles
                )
            blocks = [(own[t], 2 * groups), (sent[t], 2 * groups), (straight[t], 2 * groups), (turned[t + 1], 2 * groups)]
            shares[t] = odd_product(
                spot, blocks, sums[t + 2], sums[t + 3], [done] + extra, (first_table, near_table),
                (middle_low, near_low), sides, group, groups, slab, roles,
            )
            done = shares[t][0]
            extra = []
            send_core(t)
            if t - 1 in stages:
                extra.append(join_chip(t - 1, [done]))
        if 1 <= r <= chunks + 1:
            at, size = take(2 * groups) if 2 <= r else (0, 0)
            given = dict(sides=sides, groups=groups, cross=r <= chunks, low=at, count=size)
            deps = [done] + ([last[r - 1]] if r - 1 in last else [])
            outs = pass_on(spot, sent[r - 1], turned.get(r - 1), carried, deps + extra, given, plane)
            extra = []
            if r <= chunks:
                turned[r] = move(outs[0], cross)
            if r - 1 in turned:
                last[r] = move(outs[-1], pairs)
                if size:
                    parts.append((at, last[r], 0, size))
            done = outs[0]
        if r == 1:
            first_table = make_table(flat_left, [done], windows, slab)
            low = make_lows(outer, group)
            extra = [low, first_table]
        if r == 2:
            middle_low = make_lows([middle], group)
        if r >= 2:
            t = r - 2
            inner_blocks = end_blocks = None
            if t < chunks:
                inner_blocks = [(own[t], 0), (sent[t], 0), (straight[t], 0), (turned[t + 1], 0)]
            t = r - 3
            if 0 <= t:
                end_blocks = [
                    (own[t], 0), (sent[t], 0), (sent[t + 1], 2 * groups if t + 1 < chunks else 0), (last[t + 2], 0)
                ]
            sums[r] = even_product(
                spot, inner_blocks, end_blocks, [done] + extra, first_table, low, sides, group, groups, slab
            )
            done = sums[r]
            extra = []
            if r == 3:
                near_table = make_table(near_left, [], windows, slab)
                extra.append(near_table)
            if r - 4 in shares:
                extra.append(join_core(r - 4, [done]))
            if r - 5 in shares:
                extra.append(join_contr(r - 5, [done]))
    t = chunks - 1
    blocks = [(own[t], 2 * groups), (sent[t], 2 * groups), (straight[t], 2 * groups), (turned[t + 1], 2 * groups)]
    shares[t] = odd_product(
        spot, blocks, sums[t + 2], sums[t + 3], [done] + extra, (first_table, near_table),
        (middle_low, near_low), sides, group, groups, slab, roles,
    )
    send_core(t)
    join_chip(t - 1, [shares[t][0]])
    join_core(t, [])
    join_contr(t - 1, [])
    join_chip(t, [])
    join_contr(t, [])

    summed = jnp.concatenate([reduced[t] for t in range(chunks)], axis=2)
    mine = lax.dynamic_slice_in_dim(summed, here, 1, 1)
    for s in range(1, sides):
        give = lax.dynamic_slice_in_dim(summed, here ^ s, 1, 1).astype(jnp.bfloat16)
        got = lax.ppermute(give, "horiz", [(z, z ^ s) for z in range(sides)])
        mine = mine + got.astype(jnp.float32)
    mine = mine.reshape(windows, share, full).astype(jnp.bfloat16)
    projected = jnp.einsum("aur,urb->ab", mine, right_iso, preferred_element_type=jnp.float32)
    projected = projected * jnp.where(role >= downs, 0.25, 1.0)
    for axis, size in (("contr", contrs), ("horiz", sides)):
        s = 1
        while s < size:
            projected = projected + lax.ppermute(projected, axis, [(j, j ^ s) for j in range(size)])
            s *= 2
    found = [projected] + [
        lax.ppermute(projected, "role", [(j, j ^ s) for j in range(roles)]) for s in range(1, roles)
    ]
    found = jnp.stack(found)
    order = [lax.dynamic_index_in_dim(found, q ^ role, 0, keepdims=False) for q in range(roles)]
    return jnp.stack(order).reshape(roles // downs, downs, windows, -1)


def solution(mesh):
    placed = (
        P(None, "contr", "horiz", "role"),
        P(None, "contr", "horiz", None, None),
        P(None, None, "horiz"),
        P(("contr", "horiz"), None, None),
    )
    sizes = tuple(mesh.shape[axis] for axis in ("role", "contr", "horiz"))
    body = functools.partial(on_device, sizes)
    return jax.shard_map(body, mesh=mesh, in_specs=placed, out_specs=P(), check_vma=False)
```

```python
import functools

import jax
import jax.numpy as jnp
from jax import lax
from jax.experimental import pallas as pl
from jax.experimental.pallas import tpu as pltpu
from jax.sharding import PartitionSpec as P

LANES = 128
ROWS = 16
VMEM_BYTES = 60 * 2 ** 20


def split_sizes(total, count):
    best = 1
    for n in range(1, count + 1):
        if count % n == 0 and total % n == 0 and (total // n) % ROWS == 0:
            best = n
    return best


def group_size(depth):
    best = depth
    for size in range(2, 21, 2):
        if depth % size == 0:
            best = size
    return best


def row_of(k, slab):
    each = 2 * LANES // slab
    return k // each * 2 * LANES + k % each * slab


def rows_of(group, slab):
    return -(-(row_of(group - 1, slab) + slab) // LANES) * LANES


def pack_kernel(group, parts, given, spot_ref, *refs):
    pieces, crossed_ref, low_ref = refs[:parts], refs[parts], refs[parts + 1]
    sent_ref, own_ref, mark_ref, sem = refs[-4:] if parts else (refs[-3], None, refs[-2], refs[-1])
    here = spot_ref[0]
    sides = given["sides"]
    inner = jnp.logical_and(here > 0, here < sides - 1)
    groups, back_at, low_at, low_count, kind_at = (
        given["groups"], given["back"], given["low"], given["count"], given["kind"]
    )
    mark_ref[0] = spot_ref[0]
    mark_ref[1] = spot_ref[1]

    def back():
        return pltpu.make_async_copy(
            crossed_ref.at[0:2 * groups], sent_ref.at[back_at:back_at + 2 * groups], sem
        )

    def lower():
        return pltpu.make_async_copy(
            low_ref.at[low_at:low_at + low_count], sent_ref.at[kind_at:kind_at + low_count], sem
        )

    if given["has_back"]:
        @pl.when(inner)
        def _():
            back().start()
    if low_count:
        @pl.when(jnp.logical_not(inner))
        def _():
            lower().start()

    if parts:
        kinds, depth, rows, width = pieces[0].shape
        total = width * parts
        mains = total // LANES
        rest = total - mains * LANES
        half = (group + 1) // 2

        def place(slot, shift):
            shape = (width, (mains + 1) * LANES)
            target = slot * width + lax.broadcasted_iota(jnp.int32, shape, 0)
            target = jnp.where(target >= mains * LANES, target + shift, target)
            hit = lax.broadcasted_iota(jnp.int32, shape, 1) == target
            return jnp.where(hit, 1.0, 0.0).astype(jnp.bfloat16)

        tables = [[place(s, shift) for s in range(parts)] for shift in (0, rest)]
        for kind in range(kinds):
            base = (0, 2, 1)[kind] * groups

            def put(lo, hi, value):
                value = value.astype(jnp.bfloat16)
                own_ref[base:base + groups, lo:hi] = value
                if kind != 1:
                    sent_ref[base:base + groups, lo:hi] = value
                else:
                    @pl.when(jnp.logical_not(inner))
                    def _():
                        sent_ref[base:base + groups, lo:hi] = value

            tails = []
            for part, (lo, hi) in enumerate(((0, half), (half, group))):
                if lo == hi:
                    continue
                got = 0.0
                for slot, ref in enumerate(pieces):
                    block = ref[kind].reshape(groups, group, rows, width)[:, lo:hi]
                    got = got + jnp.dot(
                        block.reshape(groups * (hi - lo) * rows, width),
                        tables[part][slot],
                        preferred_element_type=jnp.float32,
                    )
                got = got.reshape(groups, hi - lo, rows, (mains + 1) * LANES)
                for main in range(mains):
                    put(main * group + lo, main * group + hi, got[..., main * LANES:(main + 1) * LANES])
                tails.append(got[..., mains * LANES:])
            start = mains * group
            first = tails[0]
            if len(tails) == 1:
                put(start, start + half, first)
            else:
                both = tails[1].shape[1]
                put(start, start + both, first[:, :both] + tails[1])
                if both < half:
                    put(start + both, start + half, first[:, both:])

    if given["has_back"]:
        @pl.when(inner)
        def _():
            back().wait()
    if low_count:
        @pl.when(jnp.logical_not(inner))
        def _():
            lower().wait()


def pack(spot, pieces, crossed, low, deps, given, group, plane, length):
    has_back = crossed is not None
    pieces, turn = pieces
    given = dict(given, has_back=has_back)
    groups = given["groups"]
    out = [jax.ShapeDtypeStruct((length,) + plane, jnp.bfloat16)]
    specs = [pl.BlockSpec(memory_space=pltpu.VMEM)]
    if pieces:
        out.append(jax.ShapeDtypeStruct((3 * groups,) + plane, jnp.bfloat16))
        specs.append(pl.BlockSpec(memory_space=pltpu.VMEM))
    out.append(jax.ShapeDtypeStruct((2,), jnp.int32))
    specs.append(pl.BlockSpec(memory_space=pltpu.SMEM))
    anywhere = pl.BlockSpec(memory_space=pl.ANY)
    operands = [crossed if has_back else low, low] + list(deps)
    got = pl.pallas_call(
        functools.partial(pack_kernel, group, len(pieces), given),
        out_shape=out,
        grid=(1,),
        in_specs=[pl.BlockSpec(memory_space=pltpu.SMEM)]
        + [pl.BlockSpec((None,) + piece.shape[1:], lambda g: (turn, 0, 0, 0, 0)) for piece in pieces]
        + [anywhere] * len(operands),
        out_specs=specs,
        scratch_shapes=[pltpu.SemaphoreType.DMA],
        compiler_params=pltpu.CompilerParams(vmem_limit_bytes=VMEM_BYTES),
        cost_estimate=pl.CostEstimate(flops=2 * 10 ** 9, bytes_accessed=6 * 2 ** 20, transcendentals=0),
        name="pack",
    )(spot, *pieces, *operands)
    return (got[0], got[1], got[2]) if pieces else (got[0], None, got[1])


def pass_kernel(given, spot_ref, *refs):
    received_ref, crossed_ref, low_ref = refs[:3]
    outs, sems = refs[given["inputs"]:-1], refs[-1]
    here = spot_ref[0]
    sides, groups = given["sides"], given["groups"]
    inner = jnp.logical_and(here > 0, here < sides - 1)
    low_at, low_count = given["low"], given["count"]
    copies = []
    if given["cross"]:
        copies.append((None, pltpu.make_async_copy(received_ref.at[0:3 * groups], outs[0], sems.at[0])))
    if given["back"]:
        copies.append((inner, pltpu.make_async_copy(crossed_ref.at[0:2 * groups], outs[-1], sems.at[1])))
    if low_count:
        copies.append(
            (
                jnp.logical_not(inner),
                pltpu.make_async_copy(
                    low_ref.at[low_at:low_at + low_count], outs[-1].at[0:low_count], sems.at[2]
                ),
            )
        )
    for act in ("start", "wait"):
        for where, copy in copies:
            if where is None:
                getattr(copy, act)()
            else:
                pl.when(where)(getattr(copy, act))


def pass_on(spot, received, crossed, low, deps, given, plane):
    groups = given["groups"]
    given = dict(given, back=crossed is not None, inputs=3 + len(deps))
    out = []
    if given["cross"]:
        out.append(jax.ShapeDtypeStruct((3 * groups,) + plane, jnp.bfloat16))
    if given["back"]:
        out.append(jax.ShapeDtypeStruct((2 * groups,) + plane, jnp.bfloat16))
    anywhere = pl.BlockSpec(memory_space=pl.ANY)
    operands = [received, crossed if crossed is not None else low, low] + list(deps)
    return pl.pallas_call(
        functools.partial(pass_kernel, given),
        out_shape=out,
        in_specs=[pl.BlockSpec(memory_space=pltpu.SMEM)] + [anywhere] * len(operands),
        out_specs=[pl.BlockSpec(memory_space=pltpu.VMEM)] * len(out),
        scratch_shapes=[pltpu.SemaphoreType.DMA((3,))],
        compiler_params=pltpu.CompilerParams(vmem_limit_bytes=VMEM_BYTES),
        cost_estimate=pl.CostEstimate(flops=0, bytes_accessed=4 * 2 ** 20, transcendentals=0),
        name="pass_on",
    )(spot, *operands)


def fetch(src, dst, sem):
    pltpu.make_async_copy(src, dst, sem).start()


def expand(source, step, group, groups, tables, spread, slab):
    sides, _, plane, rows, _ = source.shape
    kinds = source.shape[1] // groups
    half = (group + 1) // 2
    mains = (plane - half) // group
    windows = spread.shape[1]
    each = tables[0].shape[0]
    rest = tables[0].shape[1] - mains * LANES - LANES // 2
    lane = lax.broadcasted_iota(jnp.int32, (sides * rows, LANES), 1)
    keeps = [jnp.where(side, 1.0, 0.0).astype(jnp.bfloat16) for side in (lane < rest, lane >= rest)]

    def row(kind, k):
        def block(at):
            return source[:, kind * groups + step, at].reshape(sides * rows, LANES)

        last = block(mains * group + (k if k < half else k - half)) * keeps[0 if k < half else 1]
        return jnp.concatenate([block(main * group + k) for main in range(mains)] + [last], axis=1)

    wides = []
    for turn in range(min(each, group)):
        wides.append(
            jnp.concatenate([row(kind, k) for kind in range(kinds) for k in range(turn, group, each)], axis=0)
        )
    for slot, table in enumerate(tables):
        got = [
            jnp.dot(wide, table[turn], preferred_element_type=jnp.float32).reshape(
                kinds, -1, sides * rows, windows * LANES
            )
            for turn, wide in enumerate(wides)
        ]
        for kind in range(kinds):
            for first in range(0, group, each):
                members = range(first, min(first + each, group))
                for a in range(windows):
                    window = slice(a * LANES, (a + 1) * LANES)
                    for tile in range(2):
                        value = None
                        for k in members:
                            start = (k - first) * slab - tile * LANES
                            if start + slab <= 0 or start >= LANES:
                                continue
                            mine = got[k - first][kind, k // each, :, window]
                            value = mine if value is None else jnp.where(lane >= start, mine, value)
                        if value is not None:
                            at = first // each * 2 * LANES + tile * LANES
                            spread[slot + kind, a, :, at:at + LANES] = value.astype(jnp.bfloat16)


def table_kernel(windows, slab, left_ref, *refs):
    out_ref = refs[-1]
    total, lanes = left_ref.shape
    rest = LANES // 2
    mains = total - rest
    shape = (lanes, windows * LANES)
    source = lax.broadcasted_iota(jnp.int32, shape, 0)
    target = lax.broadcasted_iota(jnp.int32, shape, 1)
    for turn in range(out_ref.shape[0]):
        column = (source // slab) * LANES + (source % slab + turn * slab) % LANES
        select = jnp.where(column == target, 1.0, 0.0).astype(jnp.bfloat16)
        got = jnp.dot(left_ref[...], select, preferred_element_type=jnp.float32).astype(jnp.bfloat16)
        out_ref[turn, 0:total] = got
        out_ref[turn, total:total + rest] = got[mains:total]


def make_table(left, deps, windows, slab):
    total, lanes = left.shape
    vmem = pl.BlockSpec(memory_space=pltpu.VMEM)
    return pl.pallas_call(
        functools.partial(table_kernel, windows, slab),
        out_shape=jax.ShapeDtypeStruct((2 * LANES // slab, total + LANES // 2, windows * LANES), left.dtype),
        in_specs=[vmem] + [pl.BlockSpec(memory_space=pl.ANY)] * len(deps),
        out_specs=vmem,
        compiler_params=pltpu.CompilerParams(vmem_limit_bytes=VMEM_BYTES),
        name="make_table",
    )(left, *deps)


def low_kernel(*refs):
    parts, out_ref = refs[:-1], refs[-1]
    group, slab, lanes = parts[0].shape
    out_ref[...] = jnp.zeros_like(out_ref)
    for k in range(group):
        for at, ref in enumerate(parts):
            row = row_of(k, slab)
            out_ref[row:row + slab, at * lanes:(at + 1) * lanes] = ref[k]


def make_lows(parts, group):
    depth, slab, lanes = parts[0].shape
    block = pl.BlockSpec((group, slab, lanes), lambda g: (g, 0, 0))
    return pl.pallas_call(
        low_kernel,
        out_shape=jax.ShapeDtypeStruct((depth // group * rows_of(group, slab), len(parts) * lanes), parts[0].dtype),
        grid=(depth // group,),
        in_specs=[block] * len(parts),
        out_specs=pl.BlockSpec((rows_of(group, slab), len(parts) * lanes), lambda g: (g, 0)),
        compiler_params=pltpu.CompilerParams(vmem_limit_bytes=VMEM_BYTES),
        name="make_lows",
    )(*parts)


def split_kernel(tiles, low_ref, out_ref):
    group, rows = low_ref.shape[0], out_ref.shape[1]
    for k in range(group):
        for i in range(tiles[0]):
            for j in range(tiles[1]):
                out_ref[(k * tiles[0] + i) * tiles[1] + j] = low_ref[
                    k, i * rows:(i + 1) * rows, j * LANES:(j + 1) * LANES
                ]


def make_planes(low, group, tiles, rows, planes):
    depth, slab, lanes = low.shape
    each = group * tiles[0] * tiles[1]
    return pl.pallas_call(
        functools.partial(split_kernel, tiles),
        out_shape=jax.ShapeDtypeStruct((planes, rows, LANES), low.dtype),
        grid=(depth // group,),
        in_specs=[pl.BlockSpec((group, slab, lanes), lambda g: (g, 0, 0))],
        out_specs=pl.BlockSpec((each, rows, LANES), lambda g: (g, 0, 0)),
        compiler_params=pltpu.CompilerParams(vmem_limit_bytes=VMEM_BYTES),
        name="make_planes",
    )(low)


def planes_kernel(spans, group, groups, tiles, *refs):
    parts = refs[:len(spans)]
    out_ref, held, sems = refs[-3:]
    step = pl.program_id(0)

    @pl.when(step == 0)
    def _():
        copies = [
            pltpu.make_async_copy(ref.at[first:first + size], held.at[at:at + size], sems.at[i])
            for i, (ref, (at, first, size)) in enumerate(zip(parts, spans))
        ]
        for copy in copies:
            copy.start()
        for copy in copies:
            copy.wait()

    out_ref[...] = jnp.zeros_like(out_ref)
    planes, rows = held.shape[1], held.shape[2]
    each = group * tiles[0] * tiles[1]
    for k in range(group):
        for i in range(tiles[0]):
            for j in range(tiles[1]):
                at = (k * tiles[0] + i) * tiles[1] + j
                if groups == 1:
                    plane = held[at // planes, at % planes]
                elif each % planes == 0:
                    plane = held[step * (each // planes) + at // planes, at % planes]
                else:
                    plane = held[(step * each + at) // planes, (step * each + at) % planes]
                row = row_of(k, tiles[0] * rows) + i * rows
                out_ref[row:row + rows, j * LANES:(j + 1) * LANES] = plane


def low_of_planes(parts, deps, units, group, groups, tiles):
    spans = [(at, first, size) for at, _, first, size in parts]
    shape = parts[0][1].shape[1:]
    height = rows_of(group, tiles[0] * shape[1])
    anywhere = pl.BlockSpec(memory_space=pl.ANY)
    return pl.pallas_call(
        functools.partial(planes_kernel, spans, group, groups, tiles),
        out_shape=jax.ShapeDtypeStruct((groups * height, tiles[1] * LANES), jnp.bfloat16),
        grid=(groups,),
        in_specs=[anywhere] * (len(parts) + len(deps)),
        out_specs=pl.BlockSpec((height, tiles[1] * LANES), lambda g: (g, 0)),
        scratch_shapes=[
            pltpu.VMEM((units,) + shape, jnp.bfloat16),
            pltpu.SemaphoreType.DMA((len(parts),)),
        ],
        compiler_params=pltpu.CompilerParams(vmem_limit_bytes=VMEM_BYTES),
        name="low_of_planes",
    )(*[got for _, got, _, _ in parts], *deps)


def join_kernel(one_ref, two_ref, *refs):
    refs[-1][...] = one_ref[...] + two_ref[...].astype(jnp.float32)


def join(one, two, deps):
    vmem = pl.BlockSpec(memory_space=pltpu.VMEM)
    return pl.pallas_call(
        join_kernel,
        out_shape=jax.ShapeDtypeStruct(one.shape, jnp.float32),
        in_specs=[vmem] * 2 + [pl.BlockSpec(memory_space=pl.ANY)] * len(deps),
        out_specs=vmem,
        compiler_params=pltpu.CompilerParams(vmem_limit_bytes=VMEM_BYTES),
        name="join",
    )(one, two, *deps)


def join_roles_kernel(chunks, pieces, spot_ref, *refs):
    keep_ref, give_ref, held = refs[-3:]
    half = keep_ref.shape[2]
    side = spot_ref[2]
    for t in range(chunks):
        value = refs[t * pieces][...].astype(jnp.float32)
        for i in range(1, pieces):
            value = value + refs[t * pieces + i][...].astype(jnp.float32)
        held[...] = value
        keep_ref[t] = held[:, pl.ds(pl.multiple_of(side * half, half), half)]
        give_ref[t] = held[:, pl.ds(pl.multiple_of((1 - side) * half, half), half)].astype(jnp.bfloat16)


def join_roles(spot, groups, deps):
    windows, rows, full = groups[0][0].shape
    vmem = pl.BlockSpec(memory_space=pltpu.VMEM)
    shape = (len(groups), windows, rows // 2, full)
    return pl.pallas_call(
        functools.partial(join_roles_kernel, len(groups), len(groups[0])),
        out_shape=[jax.ShapeDtypeStruct(shape, jnp.float32), jax.ShapeDtypeStruct(shape, jnp.bfloat16)],
        in_specs=[pl.BlockSpec(memory_space=pltpu.SMEM)]
        + [vmem] * (len(groups) * len(groups[0]))
        + [pl.BlockSpec(memory_space=pl.ANY)] * len(deps),
        out_specs=[vmem] * 2,
        scratch_shapes=[pltpu.VMEM((windows, rows, full), jnp.float32)],
        compiler_params=pltpu.CompilerParams(vmem_limit_bytes=VMEM_BYTES),
        name="join_roles",
    )(spot, *[x for group in groups for x in group], *deps)


def even_kernel(sides, group, groups, slab, use_ends, use_inner, starts, spot_ref, *refs):
    views = [ref.at[at:at + 2 * groups] for ref, at in zip(refs[:2 * sides], starts)]
    inner_blocks, end_blocks = views[:sides], views[sides:]
    tables, low_ref = refs[2 * sides:2 * sides + 2]
    total, even, spread, sems = refs[-4:]
    here = spot_ref[0]
    step = pl.program_id(0)
    inner = jnp.logical_and(here > 0, here < sides - 1)
    work = jnp.logical_or(jnp.logical_and(inner, use_inner), jnp.logical_and(jnp.logical_not(inner), use_ends))

    @pl.when(work)
    def _():
        @pl.when(step == 0)
        def _():
            @pl.when(inner)
            def _():
                for at, turn in enumerate((0, 1, 3, 2)):
                    fetch(inner_blocks[at], even.at[here ^ turn], sems.at[at])

            @pl.when(jnp.logical_not(inner))
            def _():
                for at, turn in enumerate((0, 1, 2, 3)):
                    fetch(end_blocks[at], even.at[here ^ turn], sems.at[at])

            total[...] = jnp.zeros_like(total)
            for at in range(sides):
                pltpu.make_async_copy(inner_blocks[at], even.at[at], sems.at[at]).wait()

        expand(even, step, group, groups, (tables,), spread, slab)
        count = spread.shape[1] * spread.shape[2]
        full = total.shape[2]
        one = spread[0].reshape(count, spread.shape[3])
        two = spread[1].reshape(count, spread.shape[3])
        got = jnp.dot(one, low_ref[...], preferred_element_type=jnp.float32)
        total[0] += got[:, :full]
        total[1] += got[:, full:] + jnp.dot(two, low_ref[:, :full], preferred_element_type=jnp.float32)

    @pl.when(jnp.logical_and(step == 0, jnp.logical_not(work)))
    def _():
        total[...] = jnp.zeros_like(total)


def even_product(spot, inner_blocks, end_blocks, deps, table, low, sides, group, groups, slab):
    some = inner_blocks or end_blocks
    use_inner, use_ends = inner_blocks is not None, end_blocks is not None
    blocks = (inner_blocks or some) + (end_blocks or some)
    starts = [at for _, at in blocks]
    _, planes, rows, _ = some[0][0].shape
    height = rows_of(group, slab)
    windows = table.shape[2] // LANES
    full = low.shape[-1] // 2
    count = windows * sides * rows
    whole = lambda arr, **mode: pl.BlockSpec(arr.shape, lambda g, s: (0,) * len(arr.shape), **mode)
    once = dict(pipeline_mode=pl.Buffered(1))

    def busy(spot_ref):
        end = jnp.logical_or(spot_ref[0] == 0, spot_ref[0] == sides - 1)
        return jnp.where(jnp.where(end, use_ends, use_inner), 1, 0)

    part = pl.BlockSpec((height, 2 * full), lambda g, s: (g * busy(s), 0))
    out = jax.ShapeDtypeStruct((2, count, full), jnp.float32)
    flops = 2 * count * groups * height * 3 * full + 4 * sides * rows * groups * group * 3 * LANES * windows * LANES
    return pl.pallas_call(
        functools.partial(even_kernel, sides, group, groups, slab, use_ends, use_inner, starts),
        out_shape=out,
        grid_spec=pltpu.PrefetchScalarGridSpec(
            num_scalar_prefetch=1,
            grid=(groups,),
            in_specs=[pl.BlockSpec(memory_space=pl.ANY)] * (2 * sides)
            + [whole(table, **once), part]
            + [pl.BlockSpec(memory_space=pl.ANY)] * len(deps),
            out_specs=whole(out),
            scratch_shapes=[
                pltpu.VMEM((sides, 2 * groups, planes, rows, LANES), jnp.bfloat16),
                pltpu.VMEM((2, windows, sides * rows, height), jnp.bfloat16),
                pltpu.SemaphoreType.DMA((sides,)),
            ],
        ),
        compiler_params=pltpu.CompilerParams(vmem_limit_bytes=VMEM_BYTES),
        cost_estimate=pl.CostEstimate(flops=flops, bytes_accessed=20 * 2 ** 20, transcendentals=0),
        name="even_product",
    )(spot, *[ref for ref, _ in blocks], table, low, *deps)


def odd_kernel(sides, group, groups, slab, outs, starts, spot_ref, *refs):
    blocks = [ref.at[at:at + groups] for ref, at in zip(refs[:sides], starts)]
    inner_part, end_part = refs[sides:sides + 2]
    tables, next_tables, low_ref, next_low_ref = refs[sides + 2:sides + 6]
    out_refs = refs[-4 - outs:-4]
    odd, spread, total, sems = refs[-4:]
    here, role = spot_ref[0], spot_ref[1]
    step, last = pl.program_id(0), pl.num_programs(0) - 1
    inner = jnp.logical_and(here > 0, here < sides - 1)

    @pl.when(step == 0)
    def _():
        @pl.when(inner)
        def _():
            fetch(inner_part, total, sems.at[sides])
            for at, turn in enumerate((0, 1, 3, 2)):
                fetch(blocks[at], odd.at[here ^ turn], sems.at[at])
            for at in range(sides):
                pltpu.make_async_copy(blocks[at], odd.at[at], sems.at[at]).wait()

        @pl.when(jnp.logical_not(inner))
        def _():
            fetch(end_part, total, sems.at[sides])

        pltpu.make_async_copy(inner_part, total, sems.at[sides]).wait()

    @pl.when(inner)
    def _():
        expand(odd, step, group, groups, (tables, next_tables), spread, slab)
        count = spread.shape[1] * spread.shape[2]
        one = spread[0].reshape(count, spread.shape[3])
        two = spread[1].reshape(count, spread.shape[3])
        total[1] += jnp.dot(one, low_ref[...], preferred_element_type=jnp.float32)
        total[1] += jnp.dot(two, next_low_ref[...], preferred_element_type=jnp.float32)

    @pl.when(step == last)
    def _():
        for offset in range(outs):
            which = offset ^ role
            value = total[which // 2]
            width = value.shape[1] // 2
            value = jnp.where(which % 2 == 1, value[:, width:], value[:, :width])
            out_refs[offset][...] = value.reshape(out_refs[offset].shape).astype(jnp.bfloat16)


def odd_product(spot, blocks, inner_part, end_part, deps, tables, lows, sides, group, groups, slab, outs):
    starts = [at for _, at in blocks]
    _, planes, rows, _ = blocks[0][0].shape
    table, next_table = tables
    low, next_low = lows
    height = rows_of(group, slab)
    windows = table.shape[2] // LANES
    full = low.shape[-1]
    count = windows * sides * rows
    whole = lambda arr, **mode: pl.BlockSpec(arr.shape, lambda g, s: (0,) * len(arr.shape), **mode)
    once = dict(pipeline_mode=pl.Buffered(1))

    def busy(spot_ref):
        return jnp.where(jnp.logical_or(spot_ref[0] == 0, spot_ref[0] == sides - 1), 0, 1)

    part = pl.BlockSpec((height, full), lambda g, s: (g * busy(s), 0))
    out = [jax.ShapeDtypeStruct((windows, sides * rows, full // 2), jnp.bfloat16)] * outs
    flops = 2 * count * groups * height * 2 * full + 4 * sides * rows * groups * group * 3 * LANES * windows * LANES
    return pl.pallas_call(
        functools.partial(odd_kernel, sides, group, groups, slab, outs, starts),
        out_shape=out,
        grid_spec=pltpu.PrefetchScalarGridSpec(
            num_scalar_prefetch=1,
            grid=(groups,),
            in_specs=[pl.BlockSpec(memory_space=pl.ANY)] * (sides + 2)
            + [whole(table, **once), whole(next_table, **once), part, part]
            + [pl.BlockSpec(memory_space=pl.ANY)] * len(deps),
            out_specs=[whole(o) for o in out],
            scratch_shapes=[
                pltpu.VMEM((sides, groups, planes, rows, LANES), jnp.bfloat16),
                pltpu.VMEM((2, windows, sides * rows, height), jnp.bfloat16),
                pltpu.VMEM((2, count, full), jnp.float32),
                pltpu.SemaphoreType.DMA((sides + 1,)),
            ],
        ),
        compiler_params=pltpu.CompilerParams(vmem_limit_bytes=VMEM_BYTES),
        cost_estimate=pl.CostEstimate(flops=flops, bytes_accessed=20 * 2 ** 20, transcendentals=0),
        name="odd_product",
    )(spot, *[ref for ref, _ in blocks], inner_part, end_part, table, next_table, low, next_low, *deps)


def on_device(sizes, tops, bottoms, left_iso, right_iso):
    roles, contrs, sides = sizes
    role = lax.axis_index("role")
    here = lax.axis_index("horiz")
    kinds, depth_all, rows_all, width = tops.shape
    depth = depth_all // roles
    group = group_size(depth)
    groups = depth // group
    share = right_iso.shape[0]
    chunks = split_sizes(rows_all, share)
    unit = share // chunks
    rows = rows_all // chunks
    windows = left_iso.shape[1]
    slab = left_iso.shape[2]
    downs, full = bottoms.shape[3], bottoms.shape[4]
    step = max(contrs // 2, 1)
    spot = jnp.stack([here, role, lax.axis_index("contr") // step]).astype(jnp.int32)

    cut = tops.reshape(kinds, depth_all, contrs, chunks, unit, width)

    def exchange(first, count, place):
        got = []
        for s in range(roles):
            piece = lax.dynamic_slice(
                cut, (0, (place ^ s) * depth, 0, first, 0, 0), (kinds, depth, contrs, count, unit, width)
            ).transpose(3, 0, 1, 2, 4, 5).reshape(count, kinds, depth, rows, width)
            if s:
                piece = lax.ppermute(piece, "role", [(j, j ^ s) for j in range(roles)])
            got.append(piece)
        for t in range(count):
            pieces[first + t] = (got, t)

    def lower(kind, place):
        low = lax.dynamic_slice(
            bottoms, (kind, place * depth, 0, 0, 0), (1, depth, slab, downs, full)
        )
        return low.reshape(depth, slab, downs * full)

    pairs = [(z, z ^ 1) for z in range(sides)]
    hand = [(z, z ^ 1) for z in (0, sides - 1)]
    cross = [(z, z ^ 3) for z in range(1, sides - 1)]
    move = lambda value, perm: lax.ppermute(value, "horiz", perm)

    pieces = {}
    exchange(0, 1, role)
    total = left_iso.shape[0]
    mains = total // LANES
    plane = (mains * group + (group + 1) // 2, rows, LANES)

    def flat_left(left):
        rows = [lax.dynamic_slice_in_dim(left, (role ^ s) * width, width, 0) for s in range(roles)]
        return jnp.concatenate(rows, axis=0).reshape(total, windows * slab)

    near_left = move(left_iso, hand)
    middle = lower(1, role) * jnp.asarray(2, bottoms.dtype)
    tiles = (slab // rows, downs * full // LANES)
    count = depth * tiles[0] * tiles[1]
    units = -(-count // plane[0])
    carried = make_planes(middle, group, tiles, rows, units * plane[0]).reshape((units,) + plane)
    taken = 0

    def take(most):
        nonlocal taken
        at, size = taken, min(most, units - taken)
        taken += size
        return at, size

    own, sent, straight, turned, last = {}, {}, {}, {}, {}
    sums, shares, reduced = {}, {}, {}
    parts = []
    near_low = None
    done = None

    def send_roles(t):
        stages[t] = [shares[t][0]] + [
            lax.ppermute(shares[t][s], "role", [(j, j ^ s) for j in range(roles)]) for s in range(1, roles)
        ]

    def add_roles(ts, deps):
        step = contrs // 2
        keep, give = join_roles(spot, [stages[t] for t in ts], deps)
        halves[ts] = keep, lax.ppermute(give, "contr", [(j, j ^ step) for j in range(contrs)])
        return keep

    def add_contr(ts, deps):
        summed = join(*halves[ts], deps)
        size, step = sides * contrs // 2, contrs // 4
        summed = summed.reshape(len(ts), windows, size, unit, full)
        while step:
            size //= 2
            bit = (lax.axis_index("contr") // step) % 2
            keep = lax.dynamic_slice_in_dim(summed, bit * size, size, 2)
            give = lax.dynamic_slice_in_dim(summed, (1 - bit) * size, size, 2).astype(jnp.bfloat16)
            got = lax.ppermute(give, "contr", [(j, j ^ step) for j in range(contrs)])
            summed = keep + got.astype(jnp.float32)
            step //= 2
        reduced[ts] = summed
        return summed

    def project(groups):
        summed = jnp.concatenate([reduced[ts] for ts in groups], axis=0)
        first, count = groups[0][0], summed.shape[0]
        mine = lax.dynamic_slice_in_dim(summed, here, 1, 2)
        for s in range(1, sides):
            give = lax.dynamic_slice_in_dim(summed, here ^ s, 1, 2).astype(jnp.bfloat16)
            got = lax.ppermute(give, "horiz", [(z, z ^ s) for z in range(sides)])
            mine = mine + got.astype(jnp.float32)
        mine = mine.reshape(count, windows, unit, full).astype(jnp.bfloat16)
        iso = right_iso[first * unit:(first + count) * unit].reshape(count, unit, full, right_iso.shape[2])
        return jnp.einsum("taur,turb->ab", mine, iso, preferred_element_type=jnp.float32)

    halves = {}
    stages, extra = {}, []
    for r in range(chunks + 3):
        if r <= chunks:
            fresh = r < chunks
            base = 3 * groups if fresh else 0
            most = {0: 3, 1: 2}.get(r, 1) * groups if fresh else 0
            at, size = take(most)
            length = max(base + size, 4 * groups) if fresh else 2 * groups
            given = dict(
                sides=sides, groups=groups, back=2 * groups if fresh else 0, kind=base, low=at, count=size
            )
            deps = [sent[r - 1]] if r else [near_left]
            deps += [sums[r - 1]] if r - 1 in sums else []
            out, mine, mark = pack(
                spot, pieces.pop(r) if fresh else ([], 0), straight.get(r - 1), carried, deps + extra, given,
                group, plane, length,
            )
            extra = []
            sent[r] = move(out, pairs)
            if size:
                parts.append((at, sent[r], base, size))
            if fresh:
                own[r] = mine
                straight[r] = move(mine, cross)
            done = out
            for first, size in {0: ((1, 1), (2, 1)), 1: ((3, chunks - 3),)}.get(r, ()):
                if size > 0 and first < chunks:
                    exchange(first, size, mark[1])
            if r == 0:
                late = mark[1]
                outer = [lower(0, late), lower(2, late)]
                extra = list(outer)
        t = r - 4
        if 0 <= t < chunks:
            if near_low is None:
                near_low = low_of_planes(
                    sorted(parts, key=lambda p: p[0]), [done], units, group, groups, tiles
                )
            blocks = [(own[t], 2 * groups), (sent[t], 2 * groups), (straight[t], 2 * groups), (turned[t + 1], 2 * groups)]
            shares[t] = odd_product(
                spot, blocks, sums[t + 2], sums[t + 3], [done] + extra, (first_table, near_table),
                (middle_low, near_low), sides, group, groups, slab, roles,
            )
            done = shares[t][0]
            extra = []
            send_roles(t)
            if t - 1 in stages:
                extra.append(add_roles((t - 1,), [done]))
        if 1 <= r <= chunks + 1:
            at, size = take(2 * groups) if 2 <= r else (0, 0)
            given = dict(sides=sides, groups=groups, cross=r <= chunks, low=at, count=size)
            deps = [done] + ([last[r - 1]] if r - 1 in last else [])
            outs = pass_on(spot, sent[r - 1], turned.get(r - 1), carried, deps + extra, given, plane)
            extra = []
            if r <= chunks:
                turned[r] = move(outs[0], cross)
            if r - 1 in turned:
                last[r] = move(outs[-1], pairs)
                if size:
                    parts.append((at, last[r], 0, size))
            done = outs[0]
        if r == 1:
            first_table = make_table(flat_left(left_iso), [done], windows, slab)
            low = make_lows(outer, group)
            extra = [low, first_table]
        if r == 2:
            middle_low = make_lows([middle], group)
        if r >= 2:
            t = r - 2
            inner_blocks = end_blocks = None
            if t < chunks:
                inner_blocks = [(own[t], 0), (sent[t], 0), (straight[t], 0), (turned[t + 1], 0)]
            t = r - 3
            if 0 <= t:
                end_blocks = [
                    (own[t], 0), (sent[t], 0), (sent[t + 1], 2 * groups if t + 1 < chunks else 0), (last[t + 2], 0)
                ]
            sums[r] = even_product(
                spot, inner_blocks, end_blocks, [done] + extra, first_table, low, sides, group, groups, slab
            )
            done = sums[r]
            extra = []
            if r == 3:
                near_table = make_table(flat_left(near_left), [done], windows, slab)
                extra.append(near_table)
            if (r - 5,) in halves:
                extra.append(add_contr((r - 5,), [done]))
    t = chunks - 1
    blocks = [(own[t], 2 * groups), (sent[t], 2 * groups), (straight[t], 2 * groups), (turned[t + 1], 2 * groups)]
    shares[t] = odd_product(
        spot, blocks, sums[t + 2], sums[t + 3], [done] + extra, (first_table, near_table),
        (middle_low, near_low), sides, group, groups, slab, roles,
    )
    send_roles(t)
    late = tuple(t for t in range(chunks) if (t,) not in halves)
    done = [(t,) for t in range(chunks) if (t,) in halves]
    projected = project(done) if done else 0.0
    add_roles(late, [])
    add_contr(late, [])
    projected = projected + project([late])
    projected = projected * jnp.where(role >= downs, 0.25, 1.0)
    for axis, size in (("contr", contrs), ("horiz", sides)):
        s = 1
        while s < size:
            projected = projected + lax.ppermute(projected, axis, [(j, j ^ s) for j in range(size)])
            s *= 2
    found = [projected] + [
        lax.ppermute(projected, "role", [(j, j ^ s) for j in range(roles)]) for s in range(1, roles)
    ]
    found = jnp.stack(found)
    order = [lax.dynamic_index_in_dim(found, q ^ role, 0, keepdims=False) for q in range(roles)]
    return jnp.stack(order).reshape(roles // downs, downs, windows, -1)


def solution(mesh):
    placed = (
        P(None, "contr", "horiz", "role"),
        P(None, "contr", "horiz", None, None),
        P(None, None, "horiz"),
        P(("contr", "horiz"), None, None),
    )
    sizes = tuple(mesh.shape[axis] for axis in ("role", "contr", "horiz"))
    body = functools.partial(on_device, sizes)
    return jax.shard_map(body, mesh=mesh, in_specs=placed, out_specs=P(), check_vma=False)
```

```python
import functools

import jax
import jax.numpy as jnp
from jax import lax
from jax.experimental import pallas as pl
from jax.experimental.pallas import tpu as pltpu
from jax.sharding import PartitionSpec as P

LANES = 128
ROWS = 16
VMEM_BYTES = 60 * 2 ** 20


def split_sizes(total, count):
    best = 1
    for n in range(1, count + 1):
        if count % n == 0 and total % n == 0 and (total // n) % ROWS == 0:
            best = n
    return best


def group_size(depth):
    best = depth
    for size in range(2, 21, 2):
        if depth % size == 0:
            best = size
    return best


def row_of(k, slab):
    each = 2 * LANES // slab
    return k // each * 2 * LANES + k % each * slab


def rows_of(group, slab):
    return -(-(row_of(group - 1, slab) + slab) // LANES) * LANES


def pack_kernel(group, parts, given, spot_ref, *refs):
    pieces, crossed_ref, low_ref = refs[:parts], refs[parts], refs[parts + 1]
    sent_ref, own_ref, mark_ref, sem = refs[-4:] if parts else (refs[-3], None, refs[-2], refs[-1])
    here = spot_ref[0]
    sides = given["sides"]
    inner = jnp.logical_and(here > 0, here < sides - 1)
    groups, back_at, low_at, low_count, kind_at = (
        given["groups"], given["back"], given["low"], given["count"], given["kind"]
    )
    mark_ref[0] = spot_ref[0]
    mark_ref[1] = spot_ref[1]

    def back():
        return pltpu.make_async_copy(
            crossed_ref.at[0:2 * groups], sent_ref.at[back_at:back_at + 2 * groups], sem
        )

    def lower():
        return pltpu.make_async_copy(
            low_ref.at[low_at:low_at + low_count], sent_ref.at[kind_at:kind_at + low_count], sem
        )

    if given["has_back"]:
        @pl.when(inner)
        def _():
            back().start()
    if low_count:
        @pl.when(jnp.logical_not(inner))
        def _():
            lower().start()

    if parts:
        kinds, depth, rows, width = pieces[0].shape
        total = width * parts
        mains = total // LANES
        rest = total - mains * LANES
        half = (group + 1) // 2

        def place(slot, shift):
            shape = (width, (mains + 1) * LANES)
            target = slot * width + lax.broadcasted_iota(jnp.int32, shape, 0)
            target = jnp.where(target >= mains * LANES, target + shift, target)
            hit = lax.broadcasted_iota(jnp.int32, shape, 1) == target
            return jnp.where(hit, 1.0, 0.0).astype(jnp.bfloat16)

        tables = [[place(s, shift) for s in range(parts)] for shift in (0, rest)]
        for kind in range(kinds):
            base = (0, 2, 1)[kind] * groups

            def put(lo, hi, value):
                value = value.astype(jnp.bfloat16)
                own_ref[base:base + groups, lo:hi] = value
                if kind != 1:
                    sent_ref[base:base + groups, lo:hi] = value
                else:
                    @pl.when(jnp.logical_not(inner))
                    def _():
                        sent_ref[base:base + groups, lo:hi] = value

            tails = []
            for part, (lo, hi) in enumerate(((0, half), (half, group))):
                if lo == hi:
                    continue
                got = 0.0
                for slot, ref in enumerate(pieces):
                    block = ref[kind].reshape(groups, group, rows, width)[:, lo:hi]
                    got = got + jnp.dot(
                        block.reshape(groups * (hi - lo) * rows, width),
                        tables[part][slot],
                        preferred_element_type=jnp.float32,
                    )
                got = got.reshape(groups, hi - lo, rows, (mains + 1) * LANES)
                for main in range(mains):
                    put(main * group + lo, main * group + hi, got[..., main * LANES:(main + 1) * LANES])
                tails.append(got[..., mains * LANES:])
            start = mains * group
            first = tails[0]
            if len(tails) == 1:
                put(start, start + half, first)
            else:
                both = tails[1].shape[1]
                put(start, start + both, first[:, :both] + tails[1])
                if both < half:
                    put(start + both, start + half, first[:, both:])

    if given["has_back"]:
        @pl.when(inner)
        def _():
            back().wait()
    if low_count:
        @pl.when(jnp.logical_not(inner))
        def _():
            lower().wait()


def pack(spot, pieces, crossed, low, deps, given, group, plane, length):
    has_back = crossed is not None
    pieces, turn = pieces
    given = dict(given, has_back=has_back)
    groups = given["groups"]
    out = [jax.ShapeDtypeStruct((length,) + plane, jnp.bfloat16)]
    specs = [pl.BlockSpec(memory_space=pltpu.VMEM)]
    if pieces:
        out.append(jax.ShapeDtypeStruct((3 * groups,) + plane, jnp.bfloat16))
        specs.append(pl.BlockSpec(memory_space=pltpu.VMEM))
    out.append(jax.ShapeDtypeStruct((2,), jnp.int32))
    specs.append(pl.BlockSpec(memory_space=pltpu.SMEM))
    anywhere = pl.BlockSpec(memory_space=pl.ANY)
    some = crossed if has_back else pieces[0]
    operands = [some, some if low is None else low] + list(deps)
    got = pl.pallas_call(
        functools.partial(pack_kernel, group, len(pieces), given),
        out_shape=out,
        grid=(1,),
        in_specs=[pl.BlockSpec(memory_space=pltpu.SMEM)]
        + [pl.BlockSpec((None,) + piece.shape[1:], lambda g: (turn, 0, 0, 0, 0)) for piece in pieces]
        + [anywhere] * len(operands),
        out_specs=specs,
        scratch_shapes=[pltpu.SemaphoreType.DMA],
        compiler_params=pltpu.CompilerParams(vmem_limit_bytes=VMEM_BYTES),
        cost_estimate=pl.CostEstimate(flops=2 * 10 ** 9, bytes_accessed=6 * 2 ** 20, transcendentals=0),
        name="pack",
    )(spot, *pieces, *operands)
    return (got[0], got[1], got[2]) if pieces else (got[0], None, got[1])


def pass_kernel(given, spot_ref, *refs):
    received_ref, crossed_ref, low_ref = refs[:3]
    outs, sems = refs[given["inputs"]:-1], refs[-1]
    here = spot_ref[0]
    sides, groups = given["sides"], given["groups"]
    inner = jnp.logical_and(here > 0, here < sides - 1)
    low_at, low_count = given["low"], given["count"]
    copies = []
    if given["cross"]:
        copies.append((None, pltpu.make_async_copy(received_ref.at[0:3 * groups], outs[0], sems.at[0])))
    if given["back"]:
        copies.append((inner, pltpu.make_async_copy(crossed_ref.at[0:2 * groups], outs[-1], sems.at[1])))
    if low_count:
        copies.append(
            (
                jnp.logical_not(inner),
                pltpu.make_async_copy(
                    low_ref.at[low_at:low_at + low_count], outs[-1].at[0:low_count], sems.at[2]
                ),
            )
        )
    for act in ("start", "wait"):
        for where, copy in copies:
            if where is None:
                getattr(copy, act)()
            else:
                pl.when(where)(getattr(copy, act))


def pass_on(spot, received, crossed, low, deps, given, plane):
    groups = given["groups"]
    given = dict(given, back=crossed is not None, inputs=3 + len(deps))
    out = []
    if given["cross"]:
        out.append(jax.ShapeDtypeStruct((3 * groups,) + plane, jnp.bfloat16))
    if given["back"]:
        out.append(jax.ShapeDtypeStruct((2 * groups,) + plane, jnp.bfloat16))
    anywhere = pl.BlockSpec(memory_space=pl.ANY)
    operands = [received, crossed if crossed is not None else low, low] + list(deps)
    return pl.pallas_call(
        functools.partial(pass_kernel, given),
        out_shape=out,
        in_specs=[pl.BlockSpec(memory_space=pltpu.SMEM)] + [anywhere] * len(operands),
        out_specs=[pl.BlockSpec(memory_space=pltpu.VMEM)] * len(out),
        scratch_shapes=[pltpu.SemaphoreType.DMA((3,))],
        compiler_params=pltpu.CompilerParams(vmem_limit_bytes=VMEM_BYTES),
        cost_estimate=pl.CostEstimate(flops=0, bytes_accessed=4 * 2 ** 20, transcendentals=0),
        name="pass_on",
    )(spot, *operands)


def fetch(src, dst, sem):
    pltpu.make_async_copy(src, dst, sem).start()


def expand(source, step, group, groups, tables, spread, slab):
    sides, _, plane, rows, _ = source.shape
    kinds = source.shape[1] // groups
    half = (group + 1) // 2
    mains = (plane - half) // group
    windows = spread.shape[1]
    each = tables[0].shape[0]
    rest = tables[0].shape[1] - mains * LANES - LANES // 2
    lane = lax.broadcasted_iota(jnp.int32, (sides * rows, LANES), 1)
    keeps = [jnp.where(side, 1.0, 0.0).astype(jnp.bfloat16) for side in (lane < rest, lane >= rest)]

    def row(kind, k):
        def block(at):
            return source[:, kind * groups + step, at].reshape(sides * rows, LANES)

        last = block(mains * group + (k if k < half else k - half)) * keeps[0 if k < half else 1]
        return jnp.concatenate([block(main * group + k) for main in range(mains)] + [last], axis=1)

    wides = []
    for turn in range(min(each, group)):
        wides.append(
            jnp.concatenate([row(kind, k) for kind in range(kinds) for k in range(turn, group, each)], axis=0)
        )
    for slot, table in enumerate(tables):
        got = [
            jnp.dot(wide, table[turn], preferred_element_type=jnp.float32).reshape(
                kinds, -1, sides * rows, windows * LANES
            )
            for turn, wide in enumerate(wides)
        ]
        for kind in range(kinds):
            for first in range(0, group, each):
                members = range(first, min(first + each, group))
                for a in range(windows):
                    window = slice(a * LANES, (a + 1) * LANES)
                    for tile in range(2):
                        value = None
                        for k in members:
                            start = (k - first) * slab - tile * LANES
                            if start + slab <= 0 or start >= LANES:
                                continue
                            mine = got[k - first][kind, k // each, :, window]
                            value = mine if value is None else jnp.where(lane >= start, mine, value)
                        if value is not None:
                            at = first // each * 2 * LANES + tile * LANES
                            spread[slot + kind, a, :, at:at + LANES] = value.astype(jnp.bfloat16)


def table_kernel(windows, slab, left_ref, *refs):
    out_ref = refs[-1]
    total, lanes = left_ref.shape
    rest = LANES // 2
    mains = total - rest
    shape = (lanes, windows * LANES)
    source = lax.broadcasted_iota(jnp.int32, shape, 0)
    target = lax.broadcasted_iota(jnp.int32, shape, 1)
    for turn in range(out_ref.shape[0]):
        column = (source // slab) * LANES + (source % slab + turn * slab) % LANES
        select = jnp.where(column == target, 1.0, 0.0).astype(jnp.bfloat16)
        got = jnp.dot(left_ref[...], select, preferred_element_type=jnp.float32).astype(jnp.bfloat16)
        out_ref[turn, 0:total] = got
        out_ref[turn, total:total + rest] = got[mains:total]


def make_table(left, deps, windows, slab):
    total, lanes = left.shape
    vmem = pl.BlockSpec(memory_space=pltpu.VMEM)
    return pl.pallas_call(
        functools.partial(table_kernel, windows, slab),
        out_shape=jax.ShapeDtypeStruct((2 * LANES // slab, total + LANES // 2, windows * LANES), left.dtype),
        in_specs=[vmem] + [pl.BlockSpec(memory_space=pl.ANY)] * len(deps),
        out_specs=vmem,
        compiler_params=pltpu.CompilerParams(vmem_limit_bytes=VMEM_BYTES),
        name="make_table",
    )(left, *deps)


def low_kernel(*refs):
    parts, out_ref = refs[:-1], refs[-1]
    group, slab, lanes = parts[0].shape
    out_ref[...] = jnp.zeros_like(out_ref)
    for k in range(group):
        for at, ref in enumerate(parts):
            row = row_of(k, slab)
            out_ref[row:row + slab, at * lanes:(at + 1) * lanes] = ref[k]


def make_lows(parts, group):
    depth, slab, lanes = parts[0].shape
    block = pl.BlockSpec((group, slab, lanes), lambda g: (g, 0, 0))
    return pl.pallas_call(
        low_kernel,
        out_shape=jax.ShapeDtypeStruct((depth // group * rows_of(group, slab), len(parts) * lanes), parts[0].dtype),
        grid=(depth // group,),
        in_specs=[block] * len(parts),
        out_specs=pl.BlockSpec((rows_of(group, slab), len(parts) * lanes), lambda g: (g, 0)),
        compiler_params=pltpu.CompilerParams(vmem_limit_bytes=VMEM_BYTES),
        name="make_lows",
    )(*parts)


def split_kernel(tiles, low_ref, out_ref):
    group, rows = low_ref.shape[0], out_ref.shape[1]
    for k in range(group):
        for i in range(tiles[0]):
            for j in range(tiles[1]):
                out_ref[(k * tiles[0] + i) * tiles[1] + j] = low_ref[
                    k, i * rows:(i + 1) * rows, j * LANES:(j + 1) * LANES
                ]


def make_planes(low, group, tiles, rows, planes):
    depth, slab, lanes = low.shape
    each = group * tiles[0] * tiles[1]
    return pl.pallas_call(
        functools.partial(split_kernel, tiles),
        out_shape=jax.ShapeDtypeStruct((planes, rows, LANES), low.dtype),
        grid=(depth // group,),
        in_specs=[pl.BlockSpec((group, slab, lanes), lambda g: (g, 0, 0))],
        out_specs=pl.BlockSpec((each, rows, LANES), lambda g: (g, 0, 0)),
        compiler_params=pltpu.CompilerParams(vmem_limit_bytes=VMEM_BYTES),
        name="make_planes",
    )(low)


def planes_kernel(spans, group, groups, tiles, *refs):
    parts = refs[:len(spans)]
    out_ref, held, sems = refs[-3:]
    step = pl.program_id(0)

    @pl.when(step == 0)
    def _():
        copies = [
            pltpu.make_async_copy(ref.at[first:first + size], held.at[at:at + size], sems.at[i])
            for i, (ref, (at, first, size)) in enumerate(zip(parts, spans))
        ]
        for copy in copies:
            copy.start()
        for copy in copies:
            copy.wait()

    out_ref[...] = jnp.zeros_like(out_ref)
    planes, rows = held.shape[1], held.shape[2]
    each = group * tiles[0] * tiles[1]
    for k in range(group):
        for i in range(tiles[0]):
            for j in range(tiles[1]):
                at = (k * tiles[0] + i) * tiles[1] + j
                if groups == 1:
                    plane = held[at // planes, at % planes]
                elif each % planes == 0:
                    plane = held[step * (each // planes) + at // planes, at % planes]
                else:
                    plane = held[(step * each + at) // planes, (step * each + at) % planes]
                row = row_of(k, tiles[0] * rows) + i * rows
                out_ref[row:row + rows, j * LANES:(j + 1) * LANES] = plane


def low_of_planes(parts, deps, units, group, groups, tiles):
    spans = [(at, first, size) for at, _, first, size in parts]
    shape = parts[0][1].shape[1:]
    height = rows_of(group, tiles[0] * shape[1])
    anywhere = pl.BlockSpec(memory_space=pl.ANY)
    return pl.pallas_call(
        functools.partial(planes_kernel, spans, group, groups, tiles),
        out_shape=jax.ShapeDtypeStruct((groups * height, tiles[1] * LANES), jnp.bfloat16),
        grid=(groups,),
        in_specs=[anywhere] * (len(parts) + len(deps)),
        out_specs=pl.BlockSpec((height, tiles[1] * LANES), lambda g: (g, 0)),
        scratch_shapes=[
            pltpu.VMEM((units,) + shape, jnp.bfloat16),
            pltpu.SemaphoreType.DMA((len(parts),)),
        ],
        compiler_params=pltpu.CompilerParams(vmem_limit_bytes=VMEM_BYTES),
        name="low_of_planes",
    )(*[got for _, got, _, _ in parts], *deps)


def join_kernel(one_ref, two_ref, *refs):
    refs[-1][...] = one_ref[...] + two_ref[...].astype(jnp.float32)


def join(one, two, deps):
    vmem = pl.BlockSpec(memory_space=pltpu.VMEM)
    return pl.pallas_call(
        join_kernel,
        out_shape=jax.ShapeDtypeStruct(one.shape, jnp.float32),
        in_specs=[vmem] * 2 + [pl.BlockSpec(memory_space=pl.ANY)] * len(deps),
        out_specs=vmem,
        compiler_params=pltpu.CompilerParams(vmem_limit_bytes=VMEM_BYTES),
        name="join",
    )(one, two, *deps)


def join_roles_kernel(counts, spot_ref, *refs):
    keep_ref, give_ref, held = refs[-3:]
    half = keep_ref.shape[2]
    side = spot_ref[2]
    for t, count in enumerate(counts):
        at = sum(counts[:t])
        value = refs[at][...].astype(jnp.float32)
        for i in range(1, count):
            value = value + refs[at + i][...].astype(jnp.float32)
        held[...] = value
        keep_ref[t] = held[:, pl.ds(pl.multiple_of(side * half, half), half)]
        give_ref[t] = held[:, pl.ds(pl.multiple_of((1 - side) * half, half), half)].astype(jnp.bfloat16)


def join_roles(spot, groups, deps):
    windows, rows, full = groups[0][0].shape
    vmem = pl.BlockSpec(memory_space=pltpu.VMEM)
    shape = (len(groups), windows, rows // 2, full)
    return pl.pallas_call(
        functools.partial(join_roles_kernel, [len(group) for group in groups]),
        out_shape=[jax.ShapeDtypeStruct(shape, jnp.float32), jax.ShapeDtypeStruct(shape, jnp.bfloat16)],
        in_specs=[pl.BlockSpec(memory_space=pltpu.SMEM)]
        + [vmem] * sum(len(group) for group in groups)
        + [pl.BlockSpec(memory_space=pl.ANY)] * len(deps),
        out_specs=[vmem] * 2,
        scratch_shapes=[pltpu.VMEM((windows, rows, full), jnp.float32)],
        compiler_params=pltpu.CompilerParams(vmem_limit_bytes=VMEM_BYTES),
        name="join_roles",
    )(spot, *[x for group in groups for x in group], *deps)


def even_kernel(sides, group, groups, slab, use_ends, use_inner, starts, spot_ref, *refs):
    views = [ref.at[at:at + 2 * groups] for ref, at in zip(refs[:2 * sides], starts)]
    inner_blocks, end_blocks = views[:sides], views[sides:]
    tables, low_ref = refs[2 * sides:2 * sides + 2]
    total, even, spread, sems = refs[-4:]
    here = spot_ref[0]
    step = pl.program_id(0)
    inner = jnp.logical_and(here > 0, here < sides - 1)
    work = jnp.logical_or(jnp.logical_and(inner, use_inner), jnp.logical_and(jnp.logical_not(inner), use_ends))

    @pl.when(work)
    def _():
        @pl.when(step == 0)
        def _():
            @pl.when(inner)
            def _():
                for at, turn in enumerate((0, 1, 3, 2)):
                    fetch(inner_blocks[at], even.at[here ^ turn], sems.at[at])

            @pl.when(jnp.logical_not(inner))
            def _():
                for at, turn in enumerate((0, 1, 2, 3)):
                    fetch(end_blocks[at], even.at[here ^ turn], sems.at[at])

            total[...] = jnp.zeros_like(total)
            for at in range(sides):
                pltpu.make_async_copy(inner_blocks[at], even.at[at], sems.at[at]).wait()

        expand(even, step, group, groups, (tables,), spread, slab)
        count = spread.shape[1] * spread.shape[2]
        full = total.shape[2]
        one = spread[0].reshape(count, spread.shape[3])
        two = spread[1].reshape(count, spread.shape[3])
        got = jnp.dot(one, low_ref[...], preferred_element_type=jnp.float32)
        total[0] += got[:, :full]
        total[1] += got[:, full:] + jnp.dot(two, low_ref[:, :full], preferred_element_type=jnp.float32)

    @pl.when(jnp.logical_and(step == 0, jnp.logical_not(work)))
    def _():
        total[...] = jnp.zeros_like(total)


def even_product(spot, inner_blocks, end_blocks, deps, table, low, sides, group, groups, slab):
    some = inner_blocks or end_blocks
    use_inner, use_ends = inner_blocks is not None, end_blocks is not None
    blocks = (inner_blocks or some) + (end_blocks or some)
    starts = [at for _, at in blocks]
    _, planes, rows, _ = some[0][0].shape
    height = rows_of(group, slab)
    windows = table.shape[2] // LANES
    full = low.shape[-1] // 2
    count = windows * sides * rows
    whole = lambda arr, **mode: pl.BlockSpec(arr.shape, lambda g, s: (0,) * len(arr.shape), **mode)
    once = dict(pipeline_mode=pl.Buffered(1))

    def busy(spot_ref):
        end = jnp.logical_or(spot_ref[0] == 0, spot_ref[0] == sides - 1)
        return jnp.where(jnp.where(end, use_ends, use_inner), 1, 0)

    part = pl.BlockSpec((height, 2 * full), lambda g, s: (g * busy(s), 0))
    out = jax.ShapeDtypeStruct((2, count, full), jnp.float32)
    flops = 2 * count * groups * height * 3 * full + 4 * sides * rows * groups * group * 3 * LANES * windows * LANES
    return pl.pallas_call(
        functools.partial(even_kernel, sides, group, groups, slab, use_ends, use_inner, starts),
        out_shape=out,
        grid_spec=pltpu.PrefetchScalarGridSpec(
            num_scalar_prefetch=1,
            grid=(groups,),
            in_specs=[pl.BlockSpec(memory_space=pl.ANY)] * (2 * sides)
            + [whole(table, **once), part]
            + [pl.BlockSpec(memory_space=pl.ANY)] * len(deps),
            out_specs=whole(out),
            scratch_shapes=[
                pltpu.VMEM((sides, 2 * groups, planes, rows, LANES), jnp.bfloat16),
                pltpu.VMEM((2, windows, sides * rows, height), jnp.bfloat16),
                pltpu.SemaphoreType.DMA((sides,)),
            ],
        ),
        compiler_params=pltpu.CompilerParams(vmem_limit_bytes=VMEM_BYTES),
        cost_estimate=pl.CostEstimate(flops=flops, bytes_accessed=20 * 2 ** 20, transcendentals=0),
        name="even_product",
    )(spot, *[ref for ref, _ in blocks], table, low, *deps)


def odd_kernel(sides, group, groups, slab, outs, starts, spot_ref, *refs):
    blocks = [ref.at[at:at + groups] for ref, at in zip(refs[:sides], starts)]
    inner_part, end_part = refs[sides:sides + 2]
    tables, next_tables, low_ref, next_low_ref = refs[sides + 2:sides + 6]
    out_refs = refs[-4 - outs:-4]
    odd, spread, total, sems = refs[-4:]
    here, role = spot_ref[0], spot_ref[1]
    step, last = pl.program_id(0), pl.num_programs(0) - 1
    inner = jnp.logical_and(here > 0, here < sides - 1)

    @pl.when(step == 0)
    def _():
        @pl.when(inner)
        def _():
            fetch(inner_part, total, sems.at[sides])
            for at, turn in enumerate((0, 1, 3, 2)):
                fetch(blocks[at], odd.at[here ^ turn], sems.at[at])
            for at in range(sides):
                pltpu.make_async_copy(blocks[at], odd.at[at], sems.at[at]).wait()

        @pl.when(jnp.logical_not(inner))
        def _():
            fetch(end_part, total, sems.at[sides])

        pltpu.make_async_copy(inner_part, total, sems.at[sides]).wait()

    @pl.when(inner)
    def _():
        expand(odd, step, group, groups, (tables, next_tables), spread, slab)
        count = spread.shape[1] * spread.shape[2]
        one = spread[0].reshape(count, spread.shape[3])
        two = spread[1].reshape(count, spread.shape[3])
        total[1] += jnp.dot(one, low_ref[...], preferred_element_type=jnp.float32)
        total[1] += jnp.dot(two, next_low_ref[...], preferred_element_type=jnp.float32)

    @pl.when(step == last)
    def _():
        for offset in range(outs):
            which = offset ^ role
            value = total[which // 2]
            width = value.shape[1] // 2
            value = jnp.where(which % 2 == 1, value[:, width:], value[:, :width])
            out_refs[offset][...] = value.reshape(out_refs[offset].shape).astype(jnp.bfloat16)


def odd_product(spot, blocks, inner_part, end_part, deps, tables, lows, sides, group, groups, slab, outs):
    starts = [at for _, at in blocks]
    _, planes, rows, _ = blocks[0][0].shape
    table, next_table = tables
    low, next_low = lows
    height = rows_of(group, slab)
    windows = table.shape[2] // LANES
    full = low.shape[-1]
    count = windows * sides * rows
    whole = lambda arr, **mode: pl.BlockSpec(arr.shape, lambda g, s: (0,) * len(arr.shape), **mode)
    once = dict(pipeline_mode=pl.Buffered(1))

    def busy(spot_ref):
        return jnp.where(jnp.logical_or(spot_ref[0] == 0, spot_ref[0] == sides - 1), 0, 1)

    part = pl.BlockSpec((height, full), lambda g, s: (g * busy(s), 0))
    out = [jax.ShapeDtypeStruct((windows, sides * rows, full // 2), jnp.bfloat16)] * outs
    flops = 2 * count * groups * height * 2 * full + 4 * sides * rows * groups * group * 3 * LANES * windows * LANES
    return pl.pallas_call(
        functools.partial(odd_kernel, sides, group, groups, slab, outs, starts),
        out_shape=out,
        grid_spec=pltpu.PrefetchScalarGridSpec(
            num_scalar_prefetch=1,
            grid=(groups,),
            in_specs=[pl.BlockSpec(memory_space=pl.ANY)] * (sides + 2)
            + [whole(table, **once), whole(next_table, **once), part, part]
            + [pl.BlockSpec(memory_space=pl.ANY)] * len(deps),
            out_specs=[whole(o) for o in out],
            scratch_shapes=[
                pltpu.VMEM((sides, groups, planes, rows, LANES), jnp.bfloat16),
                pltpu.VMEM((2, windows, sides * rows, height), jnp.bfloat16),
                pltpu.VMEM((2, count, full), jnp.float32),
                pltpu.SemaphoreType.DMA((sides + 1,)),
            ],
        ),
        compiler_params=pltpu.CompilerParams(vmem_limit_bytes=VMEM_BYTES),
        cost_estimate=pl.CostEstimate(flops=flops, bytes_accessed=20 * 2 ** 20, transcendentals=0),
        name="odd_product",
    )(spot, *[ref for ref, _ in blocks], inner_part, end_part, table, next_table, low, next_low, *deps)


def on_device(sizes, tops, bottoms, left_iso, right_iso):
    roles, contrs, sides = sizes
    role = lax.axis_index("role")
    here = lax.axis_index("horiz")
    kinds, depth_all, rows_all, width = tops.shape
    depth = depth_all // roles
    group = group_size(depth)
    groups = depth // group
    share = right_iso.shape[0]
    chunks = split_sizes(rows_all, share)
    unit = share // chunks
    rows = rows_all // chunks
    windows = left_iso.shape[1]
    slab = left_iso.shape[2]
    downs, full = bottoms.shape[3], bottoms.shape[4]
    step = max(contrs // 2, 1)
    spot = jnp.stack([here, role, lax.axis_index("contr") // step]).astype(jnp.int32)

    cut = tops.reshape(kinds, depth_all, contrs, chunks, unit, width)

    def exchange(first, count, place):
        got = []
        for s in range(roles):
            piece = lax.dynamic_slice(
                cut, (0, (place ^ s) * depth, 0, first, 0, 0), (kinds, depth, contrs, count, unit, width)
            ).transpose(3, 0, 1, 2, 4, 5).reshape(count, kinds, depth, rows, width)
            if s:
                piece = lax.ppermute(piece, "role", [(j, j ^ s) for j in range(roles)])
            got.append(piece)
        for t in range(count):
            pieces[first + t] = (got, t)

    def lower(kind, place):
        low = lax.dynamic_slice(
            bottoms, (kind, place * depth, 0, 0, 0), (1, depth, slab, downs, full)
        )
        return low.reshape(depth, slab, downs * full)

    pairs = [(z, z ^ 1) for z in range(sides)]
    hand = [(z, z ^ 1) for z in (0, sides - 1)]
    cross = [(z, z ^ 3) for z in range(1, sides - 1)]
    move = lambda value, perm: lax.ppermute(value, "horiz", perm)

    pieces = {}
    exchange(0, 1, role)
    total = left_iso.shape[0]
    mains = total // LANES
    plane = (mains * group + (group + 1) // 2, rows, LANES)

    def flat_left(left):
        rows = [lax.dynamic_slice_in_dim(left, (role ^ s) * width, width, 0) for s in range(roles)]
        return jnp.concatenate(rows, axis=0).reshape(total, windows * slab)

    near_left = move(left_iso, hand)
    tiles = (slab // rows, downs * full // LANES)
    units = -(-(depth * tiles[0] * tiles[1]) // plane[0])
    carried = None
    taken = 0

    def take(most):
        nonlocal taken
        at, size = taken, min(most, units - taken)
        taken += size
        return at, size

    own, sent, straight, turned, last = {}, {}, {}, {}, {}
    sums, shares, reduced = {}, {}, {}
    parts = []
    near_low = None
    done = None

    def send_roles(t):
        stages[t] = [shares[t][0]] + [
            lax.ppermute(shares[t][s], "role", [(j, j ^ s) for j in range(roles)]) for s in range(1, roles)
        ]

    def add_roles(ts, deps):
        step = contrs // 2
        keep, give = join_roles(spot, [stages[t] for t in ts], deps)
        halves[ts] = keep, lax.ppermute(give, "contr", [(j, j ^ step) for j in range(contrs)])
        return keep

    def add_contr(ts, deps):
        summed = join(*halves[ts], deps)
        size, step = sides * contrs // 2, contrs // 4
        summed = summed.reshape(len(ts), windows, size, unit, full)
        while step:
            size //= 2
            bit = (lax.axis_index("contr") // step) % 2
            keep = lax.dynamic_slice_in_dim(summed, bit * size, size, 2)
            give = lax.dynamic_slice_in_dim(summed, (1 - bit) * size, size, 2).astype(jnp.bfloat16)
            got = lax.ppermute(give, "contr", [(j, j ^ step) for j in range(contrs)])
            summed = keep + got.astype(jnp.float32)
            step //= 2
        reduced[ts] = summed
        return summed

    def project(groups):
        summed = jnp.concatenate([reduced[ts] for ts in groups], axis=0)
        first, count = groups[0][0], summed.shape[0]
        mine = lax.dynamic_slice_in_dim(summed, here, 1, 2)
        for s in range(1, sides):
            give = lax.dynamic_slice_in_dim(summed, here ^ s, 1, 2).astype(jnp.bfloat16)
            got = lax.ppermute(give, "horiz", [(z, z ^ s) for z in range(sides)])
            mine = mine + got.astype(jnp.float32)
        mine = mine.reshape(count, windows, unit, full).astype(jnp.bfloat16)
        iso = right_iso[first * unit:(first + count) * unit].reshape(count, unit, full, right_iso.shape[2])
        return jnp.einsum("taur,turb->ab", mine, iso, preferred_element_type=jnp.float32)

    halves = {}
    stages, extra = {}, []
    for r in range(chunks + 3):
        if r <= chunks:
            fresh = r < chunks
            base = 3 * groups if fresh else 0
            most = {0: 0, 1: 4, 3: 3}.get(r, 1) * groups if fresh else 0
            at, size = take(most)
            length = max(base + size, 4 * groups if r else 0) if fresh else 2 * groups
            given = dict(
                sides=sides, groups=groups, back=2 * groups if fresh else 0, kind=base, low=at, count=size
            )
            deps = [sent[r - 1]] if r else [near_left]
            deps += [sums[r - 1]] if r - 1 in sums else []
            deps += [turned[2], last[2]] if r == 3 else []
            deps += [got for later in pieces.values() for got in later[0]] if r == 2 else []
            out, mine, mark = pack(
                spot, pieces.pop(r) if fresh else ([], 0), straight.get(r - 1), carried, deps + extra, given,
                group, plane, length,
            )
            extra = []
            sent[r] = move(out, pairs)
            if size:
                parts.append((at, sent[r], base, size))
            if fresh:
                own[r] = mine
                straight[r] = move(mine, cross)
            done = out
            for first, size in {0: ((1, 1), (2, chunks - 2))}.get(r, ()):
                if size > 0 and first < chunks:
                    exchange(first, size, mark[1])
            if r == 0:
                late = mark[1]
                middle = lower(1, late) * jnp.asarray(2, bottoms.dtype)
                carried = make_planes(middle, group, tiles, rows, units * plane[0]).reshape((units,) + plane)
                outer = [lower(0, late), lower(2, late)]
        t = r - 4
        if 0 <= t < chunks:
            if near_low is None:
                near_low = low_of_planes(
                    sorted(parts, key=lambda p: p[0]), [done], units, group, groups, tiles
                )
            blocks = [(own[t], 2 * groups), (sent[t], 2 * groups), (straight[t], 2 * groups), (turned[t + 1], 2 * groups)]
            shares[t] = odd_product(
                spot, blocks, sums[t + 2], sums[t + 3], [done] + extra, (first_table, near_table),
                (middle_low, near_low), sides, group, groups, slab, roles,
            )
            done = shares[t][0]
            extra = []
            send_roles(t)
            if t - 1 in stages:
                extra.append(add_roles((t - 1,), [done]))
        if 1 <= r <= chunks + 1:
            at, size = take(2 * groups) if 2 <= r else (0, 0)
            given = dict(sides=sides, groups=groups, cross=r <= chunks, low=at, count=size)
            deps = [done] + ([last[r - 1]] if r - 1 in last else [])
            outs = pass_on(spot, sent[r - 1], turned.get(r - 1), carried, deps + extra, given, plane)
            extra = []
            if r <= chunks:
                turned[r] = move(outs[0], cross)
            if r - 1 in turned:
                last[r] = move(outs[-1], pairs)
                if size:
                    parts.append((at, last[r], 0, size))
            done = outs[0]
        if r == 1:
            first_table = make_table(flat_left(left_iso), [done], windows, slab)
            low = make_lows(outer, group)
            extra = [low, first_table]
        if r == 2:
            middle_low = make_lows([middle], group)
        if r >= 2:
            t = r - 2
            inner_blocks = end_blocks = None
            if t < chunks:
                inner_blocks = [(own[t], 0), (sent[t], 0), (straight[t], 0), (turned[t + 1], 0)]
            t = r - 3
            if 0 <= t:
                end_blocks = [
                    (own[t], 0), (sent[t], 0), (sent[t + 1], 2 * groups if t + 1 < chunks else 0), (last[t + 2], 0)
                ]
            sums[r] = even_product(
                spot, inner_blocks, end_blocks, [done] + extra, first_table, low, sides, group, groups, slab
            )
            done = sums[r]
            extra = []
            if r == 3:
                near_table = make_table(flat_left(near_left), [done], windows, slab)
                extra.append(near_table)
            if (r - 5,) in halves:
                extra.append(add_contr((r - 5,), [done]))
    t = chunks - 1
    blocks = [(own[t], 2 * groups), (sent[t], 2 * groups), (straight[t], 2 * groups), (turned[t + 1], 2 * groups)]
    shares[t] = odd_product(
        spot, blocks, sums[t + 2], sums[t + 3], [done] + extra, (first_table, near_table),
        (middle_low, near_low), sides, group, groups, slab, roles,
    )
    ones = [lax.ppermute(shares[t][s], "role", [(j, j ^ 1) for j in range(roles)]) for s in (1, 3)]
    kept = shares[t][0].astype(jnp.float32) + ones[0].astype(jnp.float32)
    give = (shares[t][2].astype(jnp.float32) + ones[1].astype(jnp.float32)).astype(jnp.bfloat16)
    stages[t] = [kept, lax.ppermute(give, "role", [(j, j ^ 2) for j in range(roles)])]
    late = tuple(t for t in range(chunks) if (t,) not in halves)
    done = [(t,) for t in range(chunks) if (t,) in halves]
    projected = project(done) if done else 0.0
    add_roles(late, [])
    add_contr(late, [])
    projected = projected + project([late])
    projected = projected * jnp.where(role >= downs, 0.25, 1.0)
    for axis, size in (("contr", contrs), ("horiz", sides)):
        s = 1
        while s < size:
            projected = projected + lax.ppermute(projected, axis, [(j, j ^ s) for j in range(size)])
            s *= 2
    found = [projected] + [
        lax.ppermute(projected, "role", [(j, j ^ s) for j in range(roles)]) for s in range(1, roles)
    ]
    found = jnp.stack(found)
    order = [lax.dynamic_index_in_dim(found, q ^ role, 0, keepdims=False) for q in range(roles)]
    return jnp.stack(order).reshape(roles // downs, downs, windows, -1)


def solution(mesh):
    placed = (
        P(None, "contr", "horiz", "role"),
        P(None, "contr", "horiz", None, None),
        P(None, None, "horiz"),
        P(("contr", "horiz"), None, None),
    )
    sizes = tuple(mesh.shape[axis] for axis in ("role", "contr", "horiz"))
    body = functools.partial(on_device, sizes)
    return jax.shard_map(body, mesh=mesh, in_specs=placed, out_specs=P(), check_vma=False)
```

```python
import functools

import jax
import jax.numpy as jnp
from jax import lax
from jax.experimental import pallas as pl
from jax.experimental.pallas import tpu as pltpu
from jax.sharding import PartitionSpec as P

LANES = 128
ROWS = 16
VMEM_BYTES = 60 * 2 ** 20


def split_sizes(total, count):
    best = 1
    for n in range(1, count + 1):
        if count % n == 0 and total % n == 0 and (total // n) % ROWS == 0:
            best = n
    return best


def group_size(depth):
    best = depth
    for size in range(2, 21, 2):
        if depth % size == 0:
            best = size
    return best


def row_of(k, slab):
    each = 2 * LANES // slab
    return k // each * 2 * LANES + k % each * slab


def rows_of(group, slab):
    return -(-(row_of(group - 1, slab) + slab) // LANES) * LANES


def pack_kernel(group, parts, given, spot_ref, *refs):
    pieces, crossed_ref, low_ref = refs[:parts], refs[parts], refs[parts + 1]
    sent_ref, own_ref, mark_ref, sem = refs[-4:] if parts else (refs[-3], None, refs[-2], refs[-1])
    here = spot_ref[0]
    sides = given["sides"]
    inner = jnp.logical_and(here > 0, here < sides - 1)
    groups, back_at, low_at, low_count, kind_at = (
        given["groups"], given["back"], given["low"], given["count"], given["kind"]
    )
    mark_ref[0] = spot_ref[0]
    mark_ref[1] = spot_ref[1]

    def back():
        return pltpu.make_async_copy(
            crossed_ref.at[0:2 * groups], sent_ref.at[back_at:back_at + 2 * groups], sem
        )

    def lower():
        return pltpu.make_async_copy(
            low_ref.at[low_at:low_at + low_count], sent_ref.at[kind_at:kind_at + low_count], sem
        )

    if given["has_back"]:
        @pl.when(inner)
        def _():
            back().start()
    if low_count:
        @pl.when(jnp.logical_not(inner))
        def _():
            lower().start()

    if parts:
        kinds, depth, rows, width = pieces[0].shape
        total = width * parts
        mains = total // LANES
        rest = total - mains * LANES
        half = (group + 1) // 2

        def place(slot, shift):
            shape = (width, (mains + 1) * LANES)
            target = slot * width + lax.broadcasted_iota(jnp.int32, shape, 0)
            target = jnp.where(target >= mains * LANES, target + shift, target)
            hit = lax.broadcasted_iota(jnp.int32, shape, 1) == target
            return jnp.where(hit, 1.0, 0.0).astype(jnp.bfloat16)

        tables = [[place(s, shift) for s in range(parts)] for shift in (0, rest)]
        for kind in range(kinds):
            base = (0, 2, 1)[kind] * groups

            def put(lo, hi, value):
                value = value.astype(jnp.bfloat16)
                own_ref[base:base + groups, lo:hi] = value
                if kind != 1:
                    sent_ref[base:base + groups, lo:hi] = value
                else:
                    @pl.when(jnp.logical_not(inner))
                    def _():
                        sent_ref[base:base + groups, lo:hi] = value

            tails = []
            for part, (lo, hi) in enumerate(((0, half), (half, group))):
                if lo == hi:
                    continue
                got = 0.0
                for slot, ref in enumerate(pieces):
                    block = ref[kind].reshape(groups, group, rows, width)[:, lo:hi]
                    got = got + jnp.dot(
                        block.reshape(groups * (hi - lo) * rows, width),
                        tables[part][slot],
                        preferred_element_type=jnp.float32,
                    )
                got = got.reshape(groups, hi - lo, rows, (mains + 1) * LANES)
                for main in range(mains):
                    put(main * group + lo, main * group + hi, got[..., main * LANES:(main + 1) * LANES])
                tails.append(got[..., mains * LANES:])
            start = mains * group
            first = tails[0]
            if len(tails) == 1:
                put(start, start + half, first)
            else:
                both = tails[1].shape[1]
                put(start, start + both, first[:, :both] + tails[1])
                if both < half:
                    put(start + both, start + half, first[:, both:])

    if given["has_back"]:
        @pl.when(inner)
        def _():
            back().wait()
    if low_count:
        @pl.when(jnp.logical_not(inner))
        def _():
            lower().wait()


def pack(spot, pieces, crossed, low, deps, given, group, plane, length):
    has_back = crossed is not None
    pieces, turn = pieces
    given = dict(given, has_back=has_back)
    groups = given["groups"]
    out = [jax.ShapeDtypeStruct((length,) + plane, jnp.bfloat16)]
    specs = [pl.BlockSpec(memory_space=pltpu.VMEM)]
    if pieces:
        out.append(jax.ShapeDtypeStruct((3 * groups,) + plane, jnp.bfloat16))
        specs.append(pl.BlockSpec(memory_space=pltpu.VMEM))
    out.append(jax.ShapeDtypeStruct((2,), jnp.int32))
    specs.append(pl.BlockSpec(memory_space=pltpu.SMEM))
    anywhere = pl.BlockSpec(memory_space=pl.ANY)
    operands = [crossed if has_back else low, low] + list(deps)
    got = pl.pallas_call(
        functools.partial(pack_kernel, group, len(pieces), given),
        out_shape=out,
        grid=(1,),
        in_specs=[pl.BlockSpec(memory_space=pltpu.SMEM)]
        + [pl.BlockSpec((None,) + piece.shape[1:], lambda g: (turn, 0, 0, 0, 0)) for piece in pieces]
        + [anywhere] * len(operands),
        out_specs=specs,
        scratch_shapes=[pltpu.SemaphoreType.DMA],
        compiler_params=pltpu.CompilerParams(vmem_limit_bytes=VMEM_BYTES),
        cost_estimate=pl.CostEstimate(flops=2 * 10 ** 9, bytes_accessed=6 * 2 ** 20, transcendentals=0),
        name="pack",
    )(spot, *pieces, *operands)
    return (got[0], got[1], got[2]) if pieces else (got[0], None, got[1])


def pass_kernel(given, spot_ref, *refs):
    received_ref, crossed_ref, low_ref = refs[:3]
    outs, sems = refs[given["inputs"]:-1], refs[-1]
    here = spot_ref[0]
    sides, groups = given["sides"], given["groups"]
    inner = jnp.logical_and(here > 0, here < sides - 1)
    low_at, low_count = given["low"], given["count"]
    copies = []
    if given["cross"]:
        copies.append((None, pltpu.make_async_copy(received_ref.at[0:3 * groups], outs[0], sems.at[0])))
    if given["back"]:
        copies.append((inner, pltpu.make_async_copy(crossed_ref.at[0:2 * groups], outs[-1], sems.at[1])))
    if low_count:
        copies.append(
            (
                jnp.logical_not(inner),
                pltpu.make_async_copy(
                    low_ref.at[low_at:low_at + low_count], outs[-1].at[0:low_count], sems.at[2]
                ),
            )
        )
    for act in ("start", "wait"):
        for where, copy in copies:
            if where is None:
                getattr(copy, act)()
            else:
                pl.when(where)(getattr(copy, act))


def pass_on(spot, received, crossed, low, deps, given, plane):
    groups = given["groups"]
    given = dict(given, back=crossed is not None, inputs=3 + len(deps))
    out = []
    if given["cross"]:
        out.append(jax.ShapeDtypeStruct((3 * groups,) + plane, jnp.bfloat16))
    if given["back"]:
        out.append(jax.ShapeDtypeStruct((2 * groups,) + plane, jnp.bfloat16))
    anywhere = pl.BlockSpec(memory_space=pl.ANY)
    operands = [received, crossed if crossed is not None else low, low] + list(deps)
    return pl.pallas_call(
        functools.partial(pass_kernel, given),
        out_shape=out,
        in_specs=[pl.BlockSpec(memory_space=pltpu.SMEM)] + [anywhere] * len(operands),
        out_specs=[pl.BlockSpec(memory_space=pltpu.VMEM)] * len(out),
        scratch_shapes=[pltpu.SemaphoreType.DMA((3,))],
        compiler_params=pltpu.CompilerParams(vmem_limit_bytes=VMEM_BYTES),
        cost_estimate=pl.CostEstimate(flops=0, bytes_accessed=4 * 2 ** 20, transcendentals=0),
        name="pass_on",
    )(spot, *operands)


def fetch(src, dst, sem):
    pltpu.make_async_copy(src, dst, sem).start()


def expand(source, step, group, groups, tables, spread, slab):
    sides, _, plane, rows, _ = source.shape
    kinds = source.shape[1] // groups
    half = (group + 1) // 2
    mains = (plane - half) // group
    windows = spread.shape[1]
    each = tables[0].shape[0]
    rest = tables[0].shape[1] - mains * LANES - LANES // 2
    lane = lax.broadcasted_iota(jnp.int32, (sides * rows, LANES), 1)
    keeps = [jnp.where(side, 1.0, 0.0).astype(jnp.bfloat16) for side in (lane < rest, lane >= rest)]

    def row(kind, k):
        def block(at):
            return source[:, kind * groups + step, at].reshape(sides * rows, LANES)

        last = block(mains * group + (k if k < half else k - half)) * keeps[0 if k < half else 1]
        return jnp.concatenate([block(main * group + k) for main in range(mains)] + [last], axis=1)

    wides = []
    for turn in range(min(each, group)):
        wides.append(
            jnp.concatenate([row(kind, k) for kind in range(kinds) for k in range(turn, group, each)], axis=0)
        )
    for slot, table in enumerate(tables):
        got = [
            jnp.dot(wide, table[turn], preferred_element_type=jnp.float32).reshape(
                kinds, -1, sides * rows, windows * LANES
            )
            for turn, wide in enumerate(wides)
        ]
        for kind in range(kinds):
            for first in range(0, group, each):
                members = range(first, min(first + each, group))
                for a in range(windows):
                    window = slice(a * LANES, (a + 1) * LANES)
                    for tile in range(2):
                        value = None
                        for k in members:
                            start = (k - first) * slab - tile * LANES
                            if start + slab <= 0 or start >= LANES:
                                continue
                            mine = got[k - first][kind, k // each, :, window]
                            value = mine if value is None else jnp.where(lane >= start, mine, value)
                        if value is not None:
                            at = first // each * 2 * LANES + tile * LANES
                            spread[slot + kind, a, :, at:at + LANES] = value.astype(jnp.bfloat16)


def table_kernel(windows, slab, left_ref, *refs):
    out_ref = refs[-1]
    total, lanes = left_ref.shape
    rest = LANES // 2
    mains = total - rest
    shape = (lanes, windows * LANES)
    source = lax.broadcasted_iota(jnp.int32, shape, 0)
    target = lax.broadcasted_iota(jnp.int32, shape, 1)
    for turn in range(out_ref.shape[0]):
        column = (source // slab) * LANES + (source % slab + turn * slab) % LANES
        select = jnp.where(column == target, 1.0, 0.0).astype(jnp.bfloat16)
        got = jnp.dot(left_ref[...], select, preferred_element_type=jnp.float32).astype(jnp.bfloat16)
        out_ref[turn, 0:total] = got
        out_ref[turn, total:total + rest] = got[mains:total]


def make_table(left, deps, windows, slab):
    total, lanes = left.shape
    vmem = pl.BlockSpec(memory_space=pltpu.VMEM)
    return pl.pallas_call(
        functools.partial(table_kernel, windows, slab),
        out_shape=jax.ShapeDtypeStruct((2 * LANES // slab, total + LANES // 2, windows * LANES), left.dtype),
        in_specs=[vmem] + [pl.BlockSpec(memory_space=pl.ANY)] * len(deps),
        out_specs=vmem,
        compiler_params=pltpu.CompilerParams(vmem_limit_bytes=VMEM_BYTES),
        name="make_table",
    )(left, *deps)


def low_kernel(*refs):
    parts, out_ref = refs[:-1], refs[-1]
    group, slab, lanes = parts[0].shape
    out_ref[...] = jnp.zeros_like(out_ref)
    for k in range(group):
        for at, ref in enumerate(parts):
            row = row_of(k, slab)
            out_ref[row:row + slab, at * lanes:(at + 1) * lanes] = ref[k]


def make_lows(parts, group):
    depth, slab, lanes = parts[0].shape
    block = pl.BlockSpec((group, slab, lanes), lambda g: (g, 0, 0))
    return pl.pallas_call(
        low_kernel,
        out_shape=jax.ShapeDtypeStruct((depth // group * rows_of(group, slab), len(parts) * lanes), parts[0].dtype),
        grid=(depth // group,),
        in_specs=[block] * len(parts),
        out_specs=pl.BlockSpec((rows_of(group, slab), len(parts) * lanes), lambda g: (g, 0)),
        compiler_params=pltpu.CompilerParams(vmem_limit_bytes=VMEM_BYTES),
        name="make_lows",
    )(*parts)


def split_kernel(tiles, low_ref, out_ref):
    group, rows = low_ref.shape[0], out_ref.shape[1]
    for k in range(group):
        for i in range(tiles[0]):
            for j in range(tiles[1]):
                out_ref[(k * tiles[0] + i) * tiles[1] + j] = low_ref[
                    k, i * rows:(i + 1) * rows, j * LANES:(j + 1) * LANES
                ]


def make_planes(low, group, tiles, rows, planes):
    depth, slab, lanes = low.shape
    each = group * tiles[0] * tiles[1]
    return pl.pallas_call(
        functools.partial(split_kernel, tiles),
        out_shape=jax.ShapeDtypeStruct((planes, rows, LANES), low.dtype),
        grid=(depth // group,),
        in_specs=[pl.BlockSpec((group, slab, lanes), lambda g: (g, 0, 0))],
        out_specs=pl.BlockSpec((each, rows, LANES), lambda g: (g, 0, 0)),
        compiler_params=pltpu.CompilerParams(vmem_limit_bytes=VMEM_BYTES),
        name="make_planes",
    )(low)


def planes_kernel(spans, group, groups, tiles, *refs):
    parts = refs[:len(spans)]
    out_ref, held, sems = refs[-3:]
    step = pl.program_id(0)

    @pl.when(step == 0)
    def _():
        copies = [
            pltpu.make_async_copy(ref.at[first:first + size], held.at[at:at + size], sems.at[i])
            for i, (ref, (at, first, size)) in enumerate(zip(parts, spans))
        ]
        for copy in copies:
            copy.start()
        for copy in copies:
            copy.wait()

    out_ref[...] = jnp.zeros_like(out_ref)
    planes, rows = held.shape[1], held.shape[2]
    each = group * tiles[0] * tiles[1]
    for k in range(group):
        for i in range(tiles[0]):
            for j in range(tiles[1]):
                at = (k * tiles[0] + i) * tiles[1] + j
                if groups == 1:
                    plane = held[at // planes, at % planes]
                elif each % planes == 0:
                    plane = held[step * (each // planes) + at // planes, at % planes]
                else:
                    plane = held[(step * each + at) // planes, (step * each + at) % planes]
                row = row_of(k, tiles[0] * rows) + i * rows
                out_ref[row:row + rows, j * LANES:(j + 1) * LANES] = plane


def low_of_planes(parts, deps, units, group, groups, tiles):
    spans = [(at, first, size) for at, _, first, size in parts]
    shape = parts[0][1].shape[1:]
    height = rows_of(group, tiles[0] * shape[1])
    anywhere = pl.BlockSpec(memory_space=pl.ANY)
    return pl.pallas_call(
        functools.partial(planes_kernel, spans, group, groups, tiles),
        out_shape=jax.ShapeDtypeStruct((groups * height, tiles[1] * LANES), jnp.bfloat16),
        grid=(groups,),
        in_specs=[anywhere] * (len(parts) + len(deps)),
        out_specs=pl.BlockSpec((height, tiles[1] * LANES), lambda g: (g, 0)),
        scratch_shapes=[
            pltpu.VMEM((units,) + shape, jnp.bfloat16),
            pltpu.SemaphoreType.DMA((len(parts),)),
        ],
        compiler_params=pltpu.CompilerParams(vmem_limit_bytes=VMEM_BYTES),
        name="low_of_planes",
    )(*[got for _, got, _, _ in parts], *deps)


def join_kernel(one_ref, two_ref, *refs):
    refs[-1][...] = one_ref[...] + two_ref[...].astype(jnp.float32)


def join(one, two, deps):
    vmem = pl.BlockSpec(memory_space=pltpu.VMEM)
    return pl.pallas_call(
        join_kernel,
        out_shape=jax.ShapeDtypeStruct(one.shape, jnp.float32),
        in_specs=[vmem] * 2 + [pl.BlockSpec(memory_space=pl.ANY)] * len(deps),
        out_specs=vmem,
        compiler_params=pltpu.CompilerParams(vmem_limit_bytes=VMEM_BYTES),
        name="join",
    )(one, two, *deps)


def join_roles_kernel(chunks, pieces, spot_ref, *refs):
    keep_ref, give_ref, held = refs[-3:]
    half = keep_ref.shape[2]
    side = spot_ref[2]
    for t in range(chunks):
        value = refs[t * pieces][...].astype(jnp.float32)
        for i in range(1, pieces):
            value = value + refs[t * pieces + i][...].astype(jnp.float32)
        held[...] = value
        keep_ref[t] = held[:, pl.ds(pl.multiple_of(side * half, half), half)]
        give_ref[t] = held[:, pl.ds(pl.multiple_of((1 - side) * half, half), half)].astype(jnp.bfloat16)


def join_roles(spot, groups, deps):
    windows, rows, full = groups[0][0].shape
    vmem = pl.BlockSpec(memory_space=pltpu.VMEM)
    shape = (len(groups), windows, rows // 2, full)
    return pl.pallas_call(
        functools.partial(join_roles_kernel, len(groups), len(groups[0])),
        out_shape=[jax.ShapeDtypeStruct(shape, jnp.float32), jax.ShapeDtypeStruct(shape, jnp.bfloat16)],
        in_specs=[pl.BlockSpec(memory_space=pltpu.SMEM)]
        + [vmem] * (len(groups) * len(groups[0]))
        + [pl.BlockSpec(memory_space=pl.ANY)] * len(deps),
        out_specs=[vmem] * 2,
        scratch_shapes=[pltpu.VMEM((windows, rows, full), jnp.float32)],
        compiler_params=pltpu.CompilerParams(vmem_limit_bytes=VMEM_BYTES),
        name="join_roles",
    )(spot, *[x for group in groups for x in group], *deps)


def even_kernel(sides, group, groups, slab, use_ends, use_inner, starts, spot_ref, *refs):
    views = [ref.at[at:at + 2 * groups] for ref, at in zip(refs[:2 * sides], starts)]
    inner_blocks, end_blocks = views[:sides], views[sides:]
    tables, low_ref = refs[2 * sides:2 * sides + 2]
    total, even, spread, sems = refs[-4:]
    here = spot_ref[0]
    step = pl.program_id(0)
    inner = jnp.logical_and(here > 0, here < sides - 1)
    work = jnp.logical_or(jnp.logical_and(inner, use_inner), jnp.logical_and(jnp.logical_not(inner), use_ends))

    @pl.when(work)
    def _():
        @pl.when(step == 0)
        def _():
            @pl.when(inner)
            def _():
                for at, turn in enumerate((0, 1, 3, 2)):
                    fetch(inner_blocks[at], even.at[here ^ turn], sems.at[at])

            @pl.when(jnp.logical_not(inner))
            def _():
                for at, turn in enumerate((0, 1, 2, 3)):
                    fetch(end_blocks[at], even.at[here ^ turn], sems.at[at])

            total[...] = jnp.zeros_like(total)
            for at in range(sides):
                pltpu.make_async_copy(inner_blocks[at], even.at[at], sems.at[at]).wait()

        expand(even, step, group, groups, (tables,), spread, slab)
        count = spread.shape[1] * spread.shape[2]
        full = total.shape[2]
        one = spread[0].reshape(count, spread.shape[3])
        two = spread[1].reshape(count, spread.shape[3])
        got = jnp.dot(one, low_ref[...], preferred_element_type=jnp.float32)
        total[0] += got[:, :full]
        total[1] += got[:, full:] + jnp.dot(two, low_ref[:, :full], preferred_element_type=jnp.float32)

    @pl.when(jnp.logical_and(step == 0, jnp.logical_not(work)))
    def _():
        total[...] = jnp.zeros_like(total)


def even_product(spot, inner_blocks, end_blocks, deps, table, low, sides, group, groups, slab):
    some = inner_blocks or end_blocks
    use_inner, use_ends = inner_blocks is not None, end_blocks is not None
    blocks = (inner_blocks or some) + (end_blocks or some)
    starts = [at for _, at in blocks]
    _, planes, rows, _ = some[0][0].shape
    height = rows_of(group, slab)
    windows = table.shape[2] // LANES
    full = low.shape[-1] // 2
    count = windows * sides * rows
    whole = lambda arr, **mode: pl.BlockSpec(arr.shape, lambda g, s: (0,) * len(arr.shape), **mode)
    once = dict(pipeline_mode=pl.Buffered(1))

    def busy(spot_ref):
        end = jnp.logical_or(spot_ref[0] == 0, spot_ref[0] == sides - 1)
        return jnp.where(jnp.where(end, use_ends, use_inner), 1, 0)

    part = pl.BlockSpec((height, 2 * full), lambda g, s: (g * busy(s), 0))
    out = jax.ShapeDtypeStruct((2, count, full), jnp.float32)
    flops = 2 * count * groups * height * 3 * full + 4 * sides * rows * groups * group * 3 * LANES * windows * LANES
    return pl.pallas_call(
        functools.partial(even_kernel, sides, group, groups, slab, use_ends, use_inner, starts),
        out_shape=out,
        grid_spec=pltpu.PrefetchScalarGridSpec(
            num_scalar_prefetch=1,
            grid=(groups,),
            in_specs=[pl.BlockSpec(memory_space=pl.ANY)] * (2 * sides)
            + [whole(table, **once), part]
            + [pl.BlockSpec(memory_space=pl.ANY)] * len(deps),
            out_specs=whole(out),
            scratch_shapes=[
                pltpu.VMEM((sides, 2 * groups, planes, rows, LANES), jnp.bfloat16),
                pltpu.VMEM((2, windows, sides * rows, height), jnp.bfloat16),
                pltpu.SemaphoreType.DMA((sides,)),
            ],
        ),
        compiler_params=pltpu.CompilerParams(vmem_limit_bytes=VMEM_BYTES),
        cost_estimate=pl.CostEstimate(flops=flops, bytes_accessed=20 * 2 ** 20, transcendentals=0),
        name="even_product",
    )(spot, *[ref for ref, _ in blocks], table, low, *deps)


def odd_kernel(sides, group, groups, slab, outs, starts, spot_ref, *refs):
    blocks = [ref.at[at:at + groups] for ref, at in zip(refs[:sides], starts)]
    inner_part, end_part = refs[sides:sides + 2]
    tables, next_tables, low_ref, next_low_ref = refs[sides + 2:sides + 6]
    out_refs = refs[-4 - outs:-4]
    odd, spread, total, sems = refs[-4:]
    here, role = spot_ref[0], spot_ref[1]
    step, last = pl.program_id(0), pl.num_programs(0) - 1
    inner = jnp.logical_and(here > 0, here < sides - 1)

    @pl.when(step == 0)
    def _():
        @pl.when(inner)
        def _():
            fetch(inner_part, total, sems.at[sides])
            for at, turn in enumerate((0, 1, 3, 2)):
                fetch(blocks[at], odd.at[here ^ turn], sems.at[at])
            for at in range(sides):
                pltpu.make_async_copy(blocks[at], odd.at[at], sems.at[at]).wait()

        @pl.when(jnp.logical_not(inner))
        def _():
            fetch(end_part, total, sems.at[sides])

        pltpu.make_async_copy(inner_part, total, sems.at[sides]).wait()

    @pl.when(inner)
    def _():
        expand(odd, step, group, groups, (tables, next_tables), spread, slab)
        count = spread.shape[1] * spread.shape[2]
        one = spread[0].reshape(count, spread.shape[3])
        two = spread[1].reshape(count, spread.shape[3])
        total[1] += jnp.dot(one, low_ref[...], preferred_element_type=jnp.float32)
        total[1] += jnp.dot(two, next_low_ref[...], preferred_element_type=jnp.float32)

    @pl.when(step == last)
    def _():
        for offset in range(outs):
            which = offset ^ role
            value = total[which // 2]
            width = value.shape[1] // 2
            value = jnp.where(which % 2 == 1, value[:, width:], value[:, :width])
            out_refs[offset][...] = value.reshape(out_refs[offset].shape).astype(jnp.bfloat16)


def odd_product(spot, blocks, inner_part, end_part, deps, tables, lows, sides, group, groups, slab, outs):
    starts = [at for _, at in blocks]
    _, planes, rows, _ = blocks[0][0].shape
    table, next_table = tables
    low, next_low = lows
    height = rows_of(group, slab)
    windows = table.shape[2] // LANES
    full = low.shape[-1]
    count = windows * sides * rows
    whole = lambda arr, **mode: pl.BlockSpec(arr.shape, lambda g, s: (0,) * len(arr.shape), **mode)
    once = dict(pipeline_mode=pl.Buffered(1))

    def busy(spot_ref):
        return jnp.where(jnp.logical_or(spot_ref[0] == 0, spot_ref[0] == sides - 1), 0, 1)

    part = pl.BlockSpec((height, full), lambda g, s: (g * busy(s), 0))
    out = [jax.ShapeDtypeStruct((windows, sides * rows, full // 2), jnp.bfloat16)] * outs
    flops = 2 * count * groups * height * 2 * full + 4 * sides * rows * groups * group * 3 * LANES * windows * LANES
    return pl.pallas_call(
        functools.partial(odd_kernel, sides, group, groups, slab, outs, starts),
        out_shape=out,
        grid_spec=pltpu.PrefetchScalarGridSpec(
            num_scalar_prefetch=1,
            grid=(groups,),
            in_specs=[pl.BlockSpec(memory_space=pl.ANY)] * (sides + 2)
            + [whole(table, **once), whole(next_table, **once), part, part]
            + [pl.BlockSpec(memory_space=pl.ANY)] * len(deps),
            out_specs=[whole(o) for o in out],
            scratch_shapes=[
                pltpu.VMEM((sides, groups, planes, rows, LANES), jnp.bfloat16),
                pltpu.VMEM((2, windows, sides * rows, height), jnp.bfloat16),
                pltpu.VMEM((2, count, full), jnp.float32),
                pltpu.SemaphoreType.DMA((sides + 1,)),
            ],
        ),
        compiler_params=pltpu.CompilerParams(vmem_limit_bytes=VMEM_BYTES),
        cost_estimate=pl.CostEstimate(flops=flops, bytes_accessed=20 * 2 ** 20, transcendentals=0),
        name="odd_product",
    )(spot, *[ref for ref, _ in blocks], inner_part, end_part, table, next_table, low, next_low, *deps)


def on_device(sizes, tops, bottoms, left_iso, right_iso):
    roles, contrs, sides = sizes
    role = lax.axis_index("role")
    here = lax.axis_index("horiz")
    kinds, depth_all, rows_all, width = tops.shape
    depth = depth_all // roles
    group = group_size(depth)
    groups = depth // group
    share = right_iso.shape[0]
    chunks = split_sizes(rows_all, share)
    unit = share // chunks
    rows = rows_all // chunks
    windows = left_iso.shape[1]
    slab = left_iso.shape[2]
    downs, full = bottoms.shape[3], bottoms.shape[4]
    step = max(contrs // 2, 1)
    spot = jnp.stack([here, role, lax.axis_index("contr") // step]).astype(jnp.int32)

    cut = tops.reshape(kinds, depth_all, contrs, chunks, unit, width)

    def exchange(first, count, place):
        got = []
        for s in range(roles):
            piece = lax.dynamic_slice(
                cut, (0, (place ^ s) * depth, 0, first, 0, 0), (kinds, depth, contrs, count, unit, width)
            ).transpose(3, 0, 1, 2, 4, 5).reshape(count, kinds, depth, rows, width)
            if s:
                piece = lax.ppermute(piece, "role", [(j, j ^ s) for j in range(roles)])
            got.append(piece)
        for t in range(count):
            pieces[first + t] = (got, t)

    def lower(kind, place):
        low = lax.dynamic_slice(
            bottoms, (kind, place * depth, 0, 0, 0), (1, depth, slab, downs, full)
        )
        return low.reshape(depth, slab, downs * full)

    pairs = [(z, z ^ 1) for z in range(sides)]
    hand = [(z, z ^ 1) for z in (0, sides - 1)]
    cross = [(z, z ^ 3) for z in range(1, sides - 1)]
    move = lambda value, perm: lax.ppermute(value, "horiz", perm)

    pieces = {}
    exchange(0, 1, role)
    total = left_iso.shape[0]
    mains = total // LANES
    plane = (mains * group + (group + 1) // 2, rows, LANES)

    def flat_left(left):
        rows = [lax.dynamic_slice_in_dim(left, (role ^ s) * width, width, 0) for s in range(roles)]
        return jnp.concatenate(rows, axis=0).reshape(total, windows * slab)

    near_left = move(left_iso, hand)
    middle = lower(1, role) * jnp.asarray(2, bottoms.dtype)
    tiles = (slab // rows, downs * full // LANES)
    count = depth * tiles[0] * tiles[1]
    units = -(-count // plane[0])
    carried = make_planes(middle, group, tiles, rows, units * plane[0]).reshape((units,) + plane)
    taken = 0

    def take(most):
        nonlocal taken
        at, size = taken, min(most, units - taken)
        taken += size
        return at, size

    own, sent, straight, turned, last = {}, {}, {}, {}, {}
    sums, shares, reduced = {}, {}, {}
    parts = []
    near_low = None
    done = None

    def send_roles(t):
        stages[t] = [shares[t][0]] + [
            lax.ppermute(shares[t][s], "role", [(j, j ^ s) for j in range(roles)]) for s in range(1, roles)
        ]

    def add_roles(ts, deps):
        step = contrs // 2
        keep, give = join_roles(spot, [stages[t] for t in ts], deps)
        halves[ts] = keep, lax.ppermute(give, "contr", [(j, j ^ step) for j in range(contrs)])
        return keep

    def add_contr(ts, deps):
        summed = join(*halves[ts], deps)
        size, step = sides * contrs // 2, contrs // 4
        summed = summed.reshape(len(ts), windows, size, unit, full)
        while step:
            size //= 2
            bit = (lax.axis_index("contr") // step) % 2
            keep = lax.dynamic_slice_in_dim(summed, bit * size, size, 2)
            give = lax.dynamic_slice_in_dim(summed, (1 - bit) * size, size, 2).astype(jnp.bfloat16)
            got = lax.ppermute(give, "contr", [(j, j ^ step) for j in range(contrs)])
            summed = keep + got.astype(jnp.float32)
            step //= 2
        reduced[ts] = summed
        return summed

    def project(groups):
        summed = jnp.concatenate([reduced[ts] for ts in groups], axis=0)
        first, count = groups[0][0], summed.shape[0]
        mine = lax.dynamic_slice_in_dim(summed, here, 1, 2)
        for s in range(1, sides):
            give = lax.dynamic_slice_in_dim(summed, here ^ s, 1, 2).astype(jnp.bfloat16)
            got = lax.ppermute(give, "horiz", [(z, z ^ s) for z in range(sides)])
            mine = mine + got.astype(jnp.float32)
        mine = mine.reshape(count, windows, unit, full).astype(jnp.bfloat16)
        iso = right_iso[first * unit:(first + count) * unit].reshape(count, unit, full, right_iso.shape[2])
        return jnp.einsum("taur,turb->ab", mine, iso, preferred_element_type=jnp.float32)

    halves = {}
    stages, extra = {}, []
    for r in range(chunks + 3):
        if r <= chunks:
            fresh = r < chunks
            base = 3 * groups if fresh else 0
            most = {0: 1, 1: 3}.get(r, 1) * groups if fresh else 0
            at, size = take(most)
            length = max(base + size, 4 * groups) if fresh else 2 * groups
            given = dict(
                sides=sides, groups=groups, back=2 * groups if fresh else 0, kind=base, low=at, count=size
            )
            deps = [sent[r - 1]] if r else [near_left]
            deps += [sums[r - 1]] if r - 1 in sums else []
            out, mine, mark = pack(
                spot, pieces.pop(r) if fresh else ([], 0), straight.get(r - 1), carried, deps + extra, given,
                group, plane, length,
            )
            extra = []
            sent[r] = move(out, pairs)
            if size:
                parts.append((at, sent[r], base, size))
            if fresh:
                own[r] = mine
                straight[r] = move(mine, cross)
            done = out
            for first, size in {0: ((1, 1), (2, 1)), 1: ((3, chunks - 3),)}.get(r, ()):
                if size > 0 and first < chunks:
                    exchange(first, size, mark[1])
            if r == 0:
                late = mark[1]
                outer = [lower(0, late), lower(2, late)]
        t = r - 4
        if 0 <= t < chunks:
            if near_low is None:
                near_low = low_of_planes(
                    sorted(parts, key=lambda p: p[0]), [done], units, group, groups, tiles
                )
            blocks = [(own[t], 2 * groups), (sent[t], 2 * groups), (straight[t], 2 * groups), (turned[t + 1], 2 * groups)]
            shares[t] = odd_product(
                spot, blocks, sums[t + 2], sums[t + 3], [done] + extra, (first_table, near_table),
                (middle_low, near_low), sides, group, groups, slab, roles,
            )
            done = shares[t][0]
            extra = []
            send_roles(t)
            if t - 1 in stages:
                extra.append(add_roles((t - 1,), [done]))
        if 1 <= r <= chunks + 1:
            at, size = take(2 * groups) if 2 <= r else (0, 0)
            given = dict(sides=sides, groups=groups, cross=r <= chunks, low=at, count=size)
            deps = [done] + ([last[r - 1]] if r - 1 in last else [])
            outs = pass_on(spot, sent[r - 1], turned.get(r - 1), carried, deps + extra, given, plane)
            extra = []
            if r <= chunks:
                turned[r] = move(outs[0], cross)
            if r - 1 in turned:
                last[r] = move(outs[-1], pairs)
                if size:
                    parts.append((at, last[r], 0, size))
            done = outs[0]
        if r == 1:
            first_table = make_table(flat_left(left_iso), [done], windows, slab)
            low = make_lows(outer, group)
            extra = [low, first_table]
        if r == 2:
            middle_low = make_lows([middle], group)
        if r >= 2:
            t = r - 2
            inner_blocks = end_blocks = None
            if t < chunks:
                inner_blocks = [(own[t], 0), (sent[t], 0), (straight[t], 0), (turned[t + 1], 0)]
            t = r - 3
            if 0 <= t:
                end_blocks = [
                    (own[t], 0), (sent[t], 0), (sent[t + 1], 2 * groups if t + 1 < chunks else 0), (last[t + 2], 0)
                ]
            sums[r] = even_product(
                spot, inner_blocks, end_blocks, [done] + extra, first_table, low, sides, group, groups, slab
            )
            done = sums[r]
            extra = []
            if r == 3:
                near_table = make_table(flat_left(near_left), [done], windows, slab)
                extra.append(near_table)
            if (r - 5,) in halves and r < chunks + 2:
                extra.append(add_contr((r - 5,), [done]))
    t = chunks - 1
    blocks = [(own[t], 2 * groups), (sent[t], 2 * groups), (straight[t], 2 * groups), (turned[t + 1], 2 * groups)]
    shares[t] = odd_product(
        spot, blocks, sums[t + 2], sums[t + 3], [done] + extra, (first_table, near_table),
        (middle_low, near_low), sides, group, groups, slab, roles,
    )
    send_roles(t)
    late = tuple(c for c in range(chunks) if (c,) not in halves)
    done = [(c,) for c in range(chunks) if (c,) in halves]
    for ts in done:
        if ts not in reduced:
            add_contr(ts, [shares[t][0]])
    projected = project(done) if done else 0.0
    add_roles(late, [])
    add_contr(late, [])
    projected = projected + project([late])
    projected = projected * jnp.where(role >= downs, 0.25, 1.0)
    for axis, size in (("contr", contrs), ("horiz", sides)):
        s = 1
        while s < size:
            projected = projected + lax.ppermute(projected, axis, [(j, j ^ s) for j in range(size)])
            s *= 2
    found = [projected] + [
        lax.ppermute(projected, "role", [(j, j ^ s) for j in range(roles)]) for s in range(1, roles)
    ]
    found = jnp.stack(found)
    order = [lax.dynamic_index_in_dim(found, q ^ role, 0, keepdims=False) for q in range(roles)]
    return jnp.stack(order).reshape(roles // downs, downs, windows, -1)


def solution(mesh):
    placed = (
        P(None, "contr", "horiz", "role"),
        P(None, "contr", "horiz", None, None),
        P(None, None, "horiz"),
        P(("contr", "horiz"), None, None),
    )
    sizes = tuple(mesh.shape[axis] for axis in ("role", "contr", "horiz"))
    body = functools.partial(on_device, sizes)
    return jax.shard_map(body, mesh=mesh, in_specs=placed, out_specs=P(), check_vma=False)
```

```python
import functools

import jax
import jax.numpy as jnp
from jax import lax
from jax.experimental import pallas as pl
from jax.experimental.pallas import tpu as pltpu
from jax.sharding import PartitionSpec as P

LANES = 128
ROWS = 16
VMEM_BYTES = 60 * 2 ** 20


def split_sizes(total, count):
    best = 1
    for n in range(1, count + 1):
        if count % n == 0 and total % n == 0 and (total // n) % ROWS == 0:
            best = n
    return best


def group_size(depth):
    best = depth
    for size in range(2, 21, 2):
        if depth % size == 0:
            best = size
    return best


def row_of(k, slab):
    each = 2 * LANES // slab
    return k // each * 2 * LANES + k % each * slab


def rows_of(group, slab):
    return -(-(row_of(group - 1, slab) + slab) // LANES) * LANES


def pack_kernel(group, parts, given, spot_ref, *refs):
    pieces, crossed_ref, low_ref = refs[:parts], refs[parts], refs[parts + 1]
    sent_ref, own_ref, mark_ref, sem = refs[-4:] if parts else (refs[-3], None, refs[-2], refs[-1])
    here = spot_ref[0]
    sides = given["sides"]
    inner = jnp.logical_and(here > 0, here < sides - 1)
    groups, back_at, low_at, low_count, kind_at = (
        given["groups"], given["back"], given["low"], given["count"], given["kind"]
    )
    mark_ref[0] = spot_ref[0]
    mark_ref[1] = spot_ref[1]

    def back():
        return pltpu.make_async_copy(
            crossed_ref.at[0:2 * groups], sent_ref.at[back_at:back_at + 2 * groups], sem
        )

    def lower():
        return pltpu.make_async_copy(
            low_ref.at[low_at:low_at + low_count], sent_ref.at[kind_at:kind_at + low_count], sem
        )

    if given["has_back"]:
        @pl.when(inner)
        def _():
            back().start()
    if low_count:
        @pl.when(jnp.logical_not(inner))
        def _():
            lower().start()

    if parts:
        kinds, depth, rows, width = pieces[0].shape
        total = width * parts
        mains = total // LANES
        rest = total - mains * LANES
        half = (group + 1) // 2

        def place(slot, shift):
            shape = (width, (mains + 1) * LANES)
            target = slot * width + lax.broadcasted_iota(jnp.int32, shape, 0)
            target = jnp.where(target >= mains * LANES, target + shift, target)
            hit = lax.broadcasted_iota(jnp.int32, shape, 1) == target
            return jnp.where(hit, 1.0, 0.0).astype(jnp.bfloat16)

        tables = [[place(s, shift) for s in range(parts)] for shift in (0, rest)]
        for kind in range(kinds):
            base = (0, 2, 1)[kind] * groups

            def put(lo, hi, value):
                value = value.astype(jnp.bfloat16)
                own_ref[base:base + groups, lo:hi] = value
                if kind != 1:
                    sent_ref[base:base + groups, lo:hi] = value
                else:
                    @pl.when(jnp.logical_not(inner))
                    def _():
                        sent_ref[base:base + groups, lo:hi] = value

            tails = []
            for part, (lo, hi) in enumerate(((0, half), (half, group))):
                if lo == hi:
                    continue
                got = 0.0
                for slot, ref in enumerate(pieces):
                    block = ref[kind].reshape(groups, group, rows, width)[:, lo:hi]
                    got = got + jnp.dot(
                        block.reshape(groups * (hi - lo) * rows, width),
                        tables[part][slot],
                        preferred_element_type=jnp.float32,
                    )
                got = got.reshape(groups, hi - lo, rows, (mains + 1) * LANES)
                for main in range(mains):
                    put(main * group + lo, main * group + hi, got[..., main * LANES:(main + 1) * LANES])
                tails.append(got[..., mains * LANES:])
            start = mains * group
            first = tails[0]
            if len(tails) == 1:
                put(start, start + half, first)
            else:
                both = tails[1].shape[1]
                put(start, start + both, first[:, :both] + tails[1])
                if both < half:
                    put(start + both, start + half, first[:, both:])

    if given["has_back"]:
        @pl.when(inner)
        def _():
            back().wait()
    if low_count:
        @pl.when(jnp.logical_not(inner))
        def _():
            lower().wait()


def pack(spot, pieces, crossed, low, deps, given, group, plane, length):
    has_back = crossed is not None
    pieces, turn = pieces
    given = dict(given, has_back=has_back)
    groups = given["groups"]
    out = [jax.ShapeDtypeStruct((length,) + plane, jnp.bfloat16)]
    specs = [pl.BlockSpec(memory_space=pltpu.VMEM)]
    if pieces:
        out.append(jax.ShapeDtypeStruct((3 * groups,) + plane, jnp.bfloat16))
        specs.append(pl.BlockSpec(memory_space=pltpu.VMEM))
    out.append(jax.ShapeDtypeStruct((2,), jnp.int32))
    specs.append(pl.BlockSpec(memory_space=pltpu.SMEM))
    anywhere = pl.BlockSpec(memory_space=pl.ANY)
    operands = [crossed if has_back else low, low] + list(deps)
    got = pl.pallas_call(
        functools.partial(pack_kernel, group, len(pieces), given),
        out_shape=out,
        grid=(1,),
        in_specs=[pl.BlockSpec(memory_space=pltpu.SMEM)]
        + [pl.BlockSpec((None,) + piece.shape[1:], lambda g: (turn, 0, 0, 0, 0)) for piece in pieces]
        + [anywhere] * len(operands),
        out_specs=specs,
        scratch_shapes=[pltpu.SemaphoreType.DMA],
        compiler_params=pltpu.CompilerParams(vmem_limit_bytes=VMEM_BYTES),
        cost_estimate=pl.CostEstimate(flops=2 * 10 ** 9, bytes_accessed=6 * 2 ** 20, transcendentals=0),
        name="pack",
    )(spot, *pieces, *operands)
    return (got[0], got[1], got[2]) if pieces else (got[0], None, got[1])


def pass_kernel(given, spot_ref, *refs):
    received_ref, crossed_ref, low_ref = refs[:3]
    outs, sems = refs[given["inputs"]:-1], refs[-1]
    here = spot_ref[0]
    sides, groups = given["sides"], given["groups"]
    inner = jnp.logical_and(here > 0, here < sides - 1)
    low_at, low_count = given["low"], given["count"]
    copies = []
    if given["cross"]:
        copies.append((None, pltpu.make_async_copy(received_ref.at[0:3 * groups], outs[0], sems.at[0])))
    if given["back"]:
        copies.append((inner, pltpu.make_async_copy(crossed_ref.at[0:2 * groups], outs[-1], sems.at[1])))
    if low_count:
        copies.append(
            (
                jnp.logical_not(inner),
                pltpu.make_async_copy(
                    low_ref.at[low_at:low_at + low_count], outs[-1].at[0:low_count], sems.at[2]
                ),
            )
        )
    for act in ("start", "wait"):
        for where, copy in copies:
            if where is None:
                getattr(copy, act)()
            else:
                pl.when(where)(getattr(copy, act))


def pass_on(spot, received, crossed, low, deps, given, plane):
    groups = given["groups"]
    given = dict(given, back=crossed is not None, inputs=3 + len(deps))
    out = []
    if given["cross"]:
        out.append(jax.ShapeDtypeStruct((3 * groups,) + plane, jnp.bfloat16))
    if given["back"]:
        out.append(jax.ShapeDtypeStruct((2 * groups,) + plane, jnp.bfloat16))
    anywhere = pl.BlockSpec(memory_space=pl.ANY)
    operands = [received, crossed if crossed is not None else low, low] + list(deps)
    return pl.pallas_call(
        functools.partial(pass_kernel, given),
        out_shape=out,
        in_specs=[pl.BlockSpec(memory_space=pltpu.SMEM)] + [anywhere] * len(operands),
        out_specs=[pl.BlockSpec(memory_space=pltpu.VMEM)] * len(out),
        scratch_shapes=[pltpu.SemaphoreType.DMA((3,))],
        compiler_params=pltpu.CompilerParams(vmem_limit_bytes=VMEM_BYTES),
        cost_estimate=pl.CostEstimate(flops=0, bytes_accessed=4 * 2 ** 20, transcendentals=0),
        name="pass_on",
    )(spot, *operands)


def fetch(src, dst, sem):
    pltpu.make_async_copy(src, dst, sem).start()


def expand(source, step, group, groups, tables, spread, slab):
    sides, _, plane, rows, _ = source.shape
    kinds = source.shape[1] // groups
    half = (group + 1) // 2
    mains = (plane - half) // group
    windows = spread.shape[1]
    each = tables[0].shape[0]
    rest = tables[0].shape[1] - mains * LANES - LANES // 2
    lane = lax.broadcasted_iota(jnp.int32, (sides * rows, LANES), 1)
    keeps = [jnp.where(side, 1.0, 0.0).astype(jnp.bfloat16) for side in (lane < rest, lane >= rest)]

    def row(kind, k):
        def block(at):
            return source[:, kind * groups + step, at].reshape(sides * rows, LANES)

        last = block(mains * group + (k if k < half else k - half)) * keeps[0 if k < half else 1]
        return jnp.concatenate([block(main * group + k) for main in range(mains)] + [last], axis=1)

    wides = []
    for turn in range(min(each, group)):
        wides.append(
            jnp.concatenate([row(kind, k) for kind in range(kinds) for k in range(turn, group, each)], axis=0)
        )
    for slot, table in enumerate(tables):
        got = [
            jnp.dot(wide, table[turn], preferred_element_type=jnp.float32).reshape(
                kinds, -1, sides * rows, windows * LANES
            )
            for turn, wide in enumerate(wides)
        ]
        for kind in range(kinds):
            for first in range(0, group, each):
                members = range(first, min(first + each, group))
                for a in range(windows):
                    window = slice(a * LANES, (a + 1) * LANES)
                    for tile in range(2):
                        value = None
                        for k in members:
                            start = (k - first) * slab - tile * LANES
                            if start + slab <= 0 or start >= LANES:
                                continue
                            mine = got[k - first][kind, k // each, :, window]
                            value = mine if value is None else jnp.where(lane >= start, mine, value)
                        if value is not None:
                            at = first // each * 2 * LANES + tile * LANES
                            spread[slot + kind, a, :, at:at + LANES] = value.astype(jnp.bfloat16)


def table_kernel(windows, slab, left_ref, *refs):
    out_ref = refs[-1]
    total, lanes = left_ref.shape
    rest = LANES // 2
    mains = total - rest
    shape = (lanes, windows * LANES)
    source = lax.broadcasted_iota(jnp.int32, shape, 0)
    target = lax.broadcasted_iota(jnp.int32, shape, 1)
    for turn in range(out_ref.shape[0]):
        column = (source // slab) * LANES + (source % slab + turn * slab) % LANES
        select = jnp.where(column == target, 1.0, 0.0).astype(jnp.bfloat16)
        got = jnp.dot(left_ref[...], select, preferred_element_type=jnp.float32).astype(jnp.bfloat16)
        out_ref[turn, 0:total] = got
        out_ref[turn, total:total + rest] = got[mains:total]


def make_table(left, deps, windows, slab):
    total, lanes = left.shape
    vmem = pl.BlockSpec(memory_space=pltpu.VMEM)
    return pl.pallas_call(
        functools.partial(table_kernel, windows, slab),
        out_shape=jax.ShapeDtypeStruct((2 * LANES // slab, total + LANES // 2, windows * LANES), left.dtype),
        in_specs=[vmem] + [pl.BlockSpec(memory_space=pl.ANY)] * len(deps),
        out_specs=vmem,
        compiler_params=pltpu.CompilerParams(vmem_limit_bytes=VMEM_BYTES),
        name="make_table",
    )(left, *deps)


def low_kernel(*refs):
    parts, out_ref = refs[:-1], refs[-1]
    group, slab, lanes = parts[0].shape
    out_ref[...] = jnp.zeros_like(out_ref)
    for k in range(group):
        for at, ref in enumerate(parts):
            row = row_of(k, slab)
            out_ref[row:row + slab, at * lanes:(at + 1) * lanes] = ref[k]


def make_lows(parts, group):
    depth, slab, lanes = parts[0].shape
    block = pl.BlockSpec((group, slab, lanes), lambda g: (g, 0, 0))
    return pl.pallas_call(
        low_kernel,
        out_shape=jax.ShapeDtypeStruct((depth // group * rows_of(group, slab), len(parts) * lanes), parts[0].dtype),
        grid=(depth // group,),
        in_specs=[block] * len(parts),
        out_specs=pl.BlockSpec((rows_of(group, slab), len(parts) * lanes), lambda g: (g, 0)),
        compiler_params=pltpu.CompilerParams(vmem_limit_bytes=VMEM_BYTES),
        name="make_lows",
    )(*parts)


def split_kernel(tiles, low_ref, out_ref):
    group, rows = low_ref.shape[0], out_ref.shape[1]
    for k in range(group):
        for i in range(tiles[0]):
            for j in range(tiles[1]):
                out_ref[(k * tiles[0] + i) * tiles[1] + j] = low_ref[
                    k, i * rows:(i + 1) * rows, j * LANES:(j + 1) * LANES
                ]


def make_planes(low, group, tiles, rows, planes):
    depth, slab, lanes = low.shape
    each = group * tiles[0] * tiles[1]
    return pl.pallas_call(
        functools.partial(split_kernel, tiles),
        out_shape=jax.ShapeDtypeStruct((planes, rows, LANES), low.dtype),
        grid=(depth // group,),
        in_specs=[pl.BlockSpec((group, slab, lanes), lambda g: (g, 0, 0))],
        out_specs=pl.BlockSpec((each, rows, LANES), lambda g: (g, 0, 0)),
        compiler_params=pltpu.CompilerParams(vmem_limit_bytes=VMEM_BYTES),
        name="make_planes",
    )(low)


def planes_kernel(spans, group, groups, tiles, *refs):
    parts = refs[:len(spans)]
    out_ref, held, sems = refs[-3:]
    step = pl.program_id(0)

    @pl.when(step == 0)
    def _():
        copies = [
            pltpu.make_async_copy(ref.at[first:first + size], held.at[at:at + size], sems.at[i])
            for i, (ref, (at, first, size)) in enumerate(zip(parts, spans))
        ]
        for copy in copies:
            copy.start()
        for copy in copies:
            copy.wait()

    out_ref[...] = jnp.zeros_like(out_ref)
    planes, rows = held.shape[1], held.shape[2]
    each = group * tiles[0] * tiles[1]
    for k in range(group):
        for i in range(tiles[0]):
            for j in range(tiles[1]):
                at = (k * tiles[0] + i) * tiles[1] + j
                if groups == 1:
                    plane = held[at // planes, at % planes]
                elif each % planes == 0:
                    plane = held[step * (each // planes) + at // planes, at % planes]
                else:
                    plane = held[(step * each + at) // planes, (step * each + at) % planes]
                row = row_of(k, tiles[0] * rows) + i * rows
                out_ref[row:row + rows, j * LANES:(j + 1) * LANES] = plane


def low_of_planes(parts, deps, units, group, groups, tiles):
    spans = [(at, first, size) for at, _, first, size in parts]
    shape = parts[0][1].shape[1:]
    height = rows_of(group, tiles[0] * shape[1])
    anywhere = pl.BlockSpec(memory_space=pl.ANY)
    return pl.pallas_call(
        functools.partial(planes_kernel, spans, group, groups, tiles),
        out_shape=jax.ShapeDtypeStruct((groups * height, tiles[1] * LANES), jnp.bfloat16),
        grid=(groups,),
        in_specs=[anywhere] * (len(parts) + len(deps)),
        out_specs=pl.BlockSpec((height, tiles[1] * LANES), lambda g: (g, 0)),
        scratch_shapes=[
            pltpu.VMEM((units,) + shape, jnp.bfloat16),
            pltpu.SemaphoreType.DMA((len(parts),)),
        ],
        compiler_params=pltpu.CompilerParams(vmem_limit_bytes=VMEM_BYTES),
        name="low_of_planes",
    )(*[got for _, got, _, _ in parts], *deps)


def join_kernel(one_ref, two_ref, *refs):
    refs[-1][...] = one_ref[...] + two_ref[...].astype(jnp.float32)


def join(one, two, deps):
    vmem = pl.BlockSpec(memory_space=pltpu.VMEM)
    return pl.pallas_call(
        join_kernel,
        out_shape=jax.ShapeDtypeStruct(one.shape, jnp.float32),
        in_specs=[vmem] * 2 + [pl.BlockSpec(memory_space=pl.ANY)] * len(deps),
        out_specs=vmem,
        compiler_params=pltpu.CompilerParams(vmem_limit_bytes=VMEM_BYTES),
        name="join",
    )(one, two, *deps)


def join_roles_kernel(chunks, pieces, spot_ref, *refs):
    keep_ref, give_ref, held = refs[-3:]
    half = keep_ref.shape[2]
    side = spot_ref[2]
    for t in range(chunks):
        value = refs[t * pieces][...].astype(jnp.float32)
        for i in range(1, pieces):
            value = value + refs[t * pieces + i][...].astype(jnp.float32)
        held[...] = value
        keep_ref[t] = held[:, pl.ds(pl.multiple_of(side * half, half), half)]
        give_ref[t] = held[:, pl.ds(pl.multiple_of((1 - side) * half, half), half)].astype(jnp.bfloat16)


def join_roles(spot, groups, deps):
    windows, rows, full = groups[0][0].shape
    vmem = pl.BlockSpec(memory_space=pltpu.VMEM)
    shape = (len(groups), windows, rows // 2, full)
    return pl.pallas_call(
        functools.partial(join_roles_kernel, len(groups), len(groups[0])),
        out_shape=[jax.ShapeDtypeStruct(shape, jnp.float32), jax.ShapeDtypeStruct(shape, jnp.bfloat16)],
        in_specs=[pl.BlockSpec(memory_space=pltpu.SMEM)]
        + [vmem] * (len(groups) * len(groups[0]))
        + [pl.BlockSpec(memory_space=pl.ANY)] * len(deps),
        out_specs=[vmem] * 2,
        scratch_shapes=[pltpu.VMEM((windows, rows, full), jnp.float32)],
        compiler_params=pltpu.CompilerParams(vmem_limit_bytes=VMEM_BYTES),
        name="join_roles",
    )(spot, *[x for group in groups for x in group], *deps)


def even_kernel(sides, group, groups, slab, use_ends, use_inner, starts, spot_ref, *refs):
    views = [ref.at[at:at + 2 * groups] for ref, at in zip(refs[:2 * sides], starts)]
    inner_blocks, end_blocks = views[:sides], views[sides:]
    tables, low_ref = refs[2 * sides:2 * sides + 2]
    total, even, spread, sems = refs[-4:]
    here = spot_ref[0]
    step = pl.program_id(0)
    inner = jnp.logical_and(here > 0, here < sides - 1)
    work = jnp.logical_or(jnp.logical_and(inner, use_inner), jnp.logical_and(jnp.logical_not(inner), use_ends))

    @pl.when(work)
    def _():
        @pl.when(step == 0)
        def _():
            @pl.when(inner)
            def _():
                for at, turn in enumerate((0, 1, 3, 2)):
                    fetch(inner_blocks[at], even.at[here ^ turn], sems.at[at])

            @pl.when(jnp.logical_not(inner))
            def _():
                for at, turn in enumerate((0, 1, 2, 3)):
                    fetch(end_blocks[at], even.at[here ^ turn], sems.at[at])

            total[...] = jnp.zeros_like(total)
            for at in range(sides):
                pltpu.make_async_copy(inner_blocks[at], even.at[at], sems.at[at]).wait()

        expand(even, step, group, groups, (tables,), spread, slab)
        count = spread.shape[1] * spread.shape[2]
        full = total.shape[2]
        one = spread[0].reshape(count, spread.shape[3])
        two = spread[1].reshape(count, spread.shape[3])
        got = jnp.dot(one, low_ref[...], preferred_element_type=jnp.float32)
        total[0] += got[:, :full]
        total[1] += got[:, full:] + jnp.dot(two, low_ref[:, :full], preferred_element_type=jnp.float32)

    @pl.when(jnp.logical_and(step == 0, jnp.logical_not(work)))
    def _():
        total[...] = jnp.zeros_like(total)


def even_product(spot, inner_blocks, end_blocks, deps, table, low, sides, group, groups, slab):
    some = inner_blocks or end_blocks
    use_inner, use_ends = inner_blocks is not None, end_blocks is not None
    blocks = (inner_blocks or some) + (end_blocks or some)
    starts = [at for _, at in blocks]
    _, planes, rows, _ = some[0][0].shape
    height = rows_of(group, slab)
    windows = table.shape[2] // LANES
    full = low.shape[-1] // 2
    count = windows * sides * rows
    whole = lambda arr, **mode: pl.BlockSpec(arr.shape, lambda g, s: (0,) * len(arr.shape), **mode)
    once = dict(pipeline_mode=pl.Buffered(1))

    def busy(spot_ref):
        end = jnp.logical_or(spot_ref[0] == 0, spot_ref[0] == sides - 1)
        return jnp.where(jnp.where(end, use_ends, use_inner), 1, 0)

    part = pl.BlockSpec((height, 2 * full), lambda g, s: (g * busy(s), 0))
    out = jax.ShapeDtypeStruct((2, count, full), jnp.float32)
    flops = 2 * count * groups * height * 3 * full + 4 * sides * rows * groups * group * 3 * LANES * windows * LANES
    return pl.pallas_call(
        functools.partial(even_kernel, sides, group, groups, slab, use_ends, use_inner, starts),
        out_shape=out,
        grid_spec=pltpu.PrefetchScalarGridSpec(
            num_scalar_prefetch=1,
            grid=(groups,),
            in_specs=[pl.BlockSpec(memory_space=pl.ANY)] * (2 * sides)
            + [whole(table, **once), part]
            + [pl.BlockSpec(memory_space=pl.ANY)] * len(deps),
            out_specs=whole(out),
            scratch_shapes=[
                pltpu.VMEM((sides, 2 * groups, planes, rows, LANES), jnp.bfloat16),
                pltpu.VMEM((2, windows, sides * rows, height), jnp.bfloat16),
                pltpu.SemaphoreType.DMA((sides,)),
            ],
        ),
        compiler_params=pltpu.CompilerParams(vmem_limit_bytes=VMEM_BYTES),
        cost_estimate=pl.CostEstimate(flops=flops, bytes_accessed=20 * 2 ** 20, transcendentals=0),
        name="even_product",
    )(spot, *[ref for ref, _ in blocks], table, low, *deps)


def odd_kernel(sides, group, groups, slab, outs, starts, spot_ref, *refs):
    blocks = [ref.at[at:at + groups] for ref, at in zip(refs[:sides], starts)]
    inner_part, end_part = refs[sides:sides + 2]
    tables, next_tables, low_ref, next_low_ref = refs[sides + 2:sides + 6]
    out_refs = refs[-4 - outs:-4]
    odd, spread, total, sems = refs[-4:]
    here, role = spot_ref[0], spot_ref[1]
    step, last = pl.program_id(0), pl.num_programs(0) - 1
    inner = jnp.logical_and(here > 0, here < sides - 1)

    @pl.when(step == 0)
    def _():
        @pl.when(inner)
        def _():
            fetch(inner_part, total, sems.at[sides])
            for at, turn in enumerate((0, 1, 3, 2)):
                fetch(blocks[at], odd.at[here ^ turn], sems.at[at])
            for at in range(sides):
                pltpu.make_async_copy(blocks[at], odd.at[at], sems.at[at]).wait()

        @pl.when(jnp.logical_not(inner))
        def _():
            fetch(end_part, total, sems.at[sides])

        pltpu.make_async_copy(inner_part, total, sems.at[sides]).wait()

    @pl.when(inner)
    def _():
        expand(odd, step, group, groups, (tables, next_tables), spread, slab)
        count = spread.shape[1] * spread.shape[2]
        one = spread[0].reshape(count, spread.shape[3])
        two = spread[1].reshape(count, spread.shape[3])
        total[1] += jnp.dot(one, low_ref[...], preferred_element_type=jnp.float32)
        total[1] += jnp.dot(two, next_low_ref[...], preferred_element_type=jnp.float32)

    @pl.when(step == last)
    def _():
        for offset in range(outs):
            which = offset ^ role
            value = total[which // 2]
            width = value.shape[1] // 2
            value = jnp.where(which % 2 == 1, value[:, width:], value[:, :width])
            out_refs[offset][...] = value.reshape(out_refs[offset].shape).astype(jnp.bfloat16)


def odd_product(spot, blocks, inner_part, end_part, deps, tables, lows, sides, group, groups, slab, outs):
    starts = [at for _, at in blocks]
    _, planes, rows, _ = blocks[0][0].shape
    table, next_table = tables
    low, next_low = lows
    height = rows_of(group, slab)
    windows = table.shape[2] // LANES
    full = low.shape[-1]
    count = windows * sides * rows
    whole = lambda arr, **mode: pl.BlockSpec(arr.shape, lambda g, s: (0,) * len(arr.shape), **mode)
    once = dict(pipeline_mode=pl.Buffered(1))

    def busy(spot_ref):
        return jnp.where(jnp.logical_or(spot_ref[0] == 0, spot_ref[0] == sides - 1), 0, 1)

    part = pl.BlockSpec((height, full), lambda g, s: (g * busy(s), 0))
    out = [jax.ShapeDtypeStruct((windows, sides * rows, full // 2), jnp.bfloat16)] * outs
    flops = 2 * count * groups * height * 2 * full + 4 * sides * rows * groups * group * 3 * LANES * windows * LANES
    return pl.pallas_call(
        functools.partial(odd_kernel, sides, group, groups, slab, outs, starts),
        out_shape=out,
        grid_spec=pltpu.PrefetchScalarGridSpec(
            num_scalar_prefetch=1,
            grid=(groups,),
            in_specs=[pl.BlockSpec(memory_space=pl.ANY)] * (sides + 2)
            + [whole(table, **once), whole(next_table, **once), part, part]
            + [pl.BlockSpec(memory_space=pl.ANY)] * len(deps),
            out_specs=[whole(o) for o in out],
            scratch_shapes=[
                pltpu.VMEM((sides, groups, planes, rows, LANES), jnp.bfloat16),
                pltpu.VMEM((2, windows, sides * rows, height), jnp.bfloat16),
                pltpu.VMEM((2, count, full), jnp.float32),
                pltpu.SemaphoreType.DMA((sides + 1,)),
            ],
        ),
        compiler_params=pltpu.CompilerParams(vmem_limit_bytes=VMEM_BYTES),
        cost_estimate=pl.CostEstimate(flops=flops, bytes_accessed=20 * 2 ** 20, transcendentals=0),
        name="odd_product",
    )(spot, *[ref for ref, _ in blocks], inner_part, end_part, table, next_table, low, next_low, *deps)


def on_device(sizes, tops, bottoms, left_iso, right_iso):
    roles, contrs, sides = sizes
    role = lax.axis_index("role")
    here = lax.axis_index("horiz")
    kinds, depth_all, rows_all, width = tops.shape
    depth = depth_all // roles
    group = group_size(depth)
    groups = depth // group
    share = right_iso.shape[0]
    chunks = split_sizes(rows_all, share)
    unit = share // chunks
    rows = rows_all // chunks
    windows = left_iso.shape[1]
    slab = left_iso.shape[2]
    downs, full = bottoms.shape[3], bottoms.shape[4]
    step = max(contrs // 2, 1)
    spot = jnp.stack([here, role, lax.axis_index("contr") // step]).astype(jnp.int32)

    cut = tops.reshape(kinds, depth_all, contrs, chunks, unit, width)

    def exchange(first, count, place):
        got = []
        for s in range(roles):
            piece = lax.dynamic_slice(
                cut, (0, (place ^ s) * depth, 0, first, 0, 0), (kinds, depth, contrs, count, unit, width)
            ).transpose(3, 0, 1, 2, 4, 5).reshape(count, kinds, depth, rows, width)
            if s:
                piece = lax.ppermute(piece, "role", [(j, j ^ s) for j in range(roles)])
            got.append(piece)
        for t in range(count):
            pieces[first + t] = (got, t)

    def lower(kind, place):
        low = lax.dynamic_slice(
            bottoms, (kind, place * depth, 0, 0, 0), (1, depth, slab, downs, full)
        )
        return low.reshape(depth, slab, downs * full)

    pairs = [(z, z ^ 1) for z in range(sides)]
    hand = [(z, z ^ 1) for z in (0, sides - 1)]
    cross = [(z, z ^ 3) for z in range(1, sides - 1)]
    move = lambda value, perm: lax.ppermute(value, "horiz", perm)

    pieces = {}
    exchange(0, 1, role)
    total = left_iso.shape[0]
    mains = total // LANES
    plane = (mains * group + (group + 1) // 2, rows, LANES)

    def flat_left(left):
        rows = [lax.dynamic_slice_in_dim(left, (role ^ s) * width, width, 0) for s in range(roles)]
        return jnp.concatenate(rows, axis=0).reshape(total, windows * slab)

    near_left = move(left_iso, hand)
    middle = lower(1, role) * jnp.asarray(2, bottoms.dtype)
    tiles = (slab // rows, downs * full // LANES)
    count = depth * tiles[0] * tiles[1]
    units = -(-count // plane[0])
    carried = make_planes(middle, group, tiles, rows, units * plane[0]).reshape((units,) + plane)
    taken = 0

    def take(most):
        nonlocal taken
        at, size = taken, min(most, units - taken)
        taken += size
        return at, size

    own, sent, straight, turned, last = {}, {}, {}, {}, {}
    sums, shares, reduced = {}, {}, {}
    parts = []
    near_low = None
    done = None

    def send_roles(t):
        stages[t] = [shares[t][0]] + [
            lax.ppermute(shares[t][s], "role", [(j, j ^ s) for j in range(roles)]) for s in range(1, roles)
        ]

    def add_roles(ts, deps):
        step = contrs // 2
        keep, give = join_roles(spot, [stages[t] for t in ts], deps)
        halves[ts] = keep, lax.ppermute(give, "contr", [(j, j ^ step) for j in range(contrs)])
        return keep

    def add_contr(ts, deps):
        summed = join(*halves[ts], deps)
        size, step = sides * contrs // 2, contrs // 4
        summed = summed.reshape(len(ts), windows, size, unit, full)
        while step:
            size //= 2
            bit = (lax.axis_index("contr") // step) % 2
            keep = lax.dynamic_slice_in_dim(summed, bit * size, size, 2)
            give = lax.dynamic_slice_in_dim(summed, (1 - bit) * size, size, 2).astype(jnp.bfloat16)
            got = lax.ppermute(give, "contr", [(j, j ^ step) for j in range(contrs)])
            summed = keep + got.astype(jnp.float32)
            step //= 2
        reduced[ts] = summed
        return summed

    def project(groups):
        summed = jnp.concatenate([reduced[ts] for ts in groups], axis=0)
        first, count = groups[0][0], summed.shape[0]
        mine = lax.dynamic_slice_in_dim(summed, here, 1, 2)
        for s in range(1, sides):
            give = lax.dynamic_slice_in_dim(summed, here ^ s, 1, 2).astype(jnp.bfloat16)
            got = lax.ppermute(give, "horiz", [(z, z ^ s) for z in range(sides)])
            mine = mine + got.astype(jnp.float32)
        mine = mine.reshape(count, windows, unit, full).astype(jnp.bfloat16)
        iso = right_iso[first * unit:(first + count) * unit].reshape(count, unit, full, right_iso.shape[2])
        return jnp.einsum("taur,turb->ab", mine, iso, preferred_element_type=jnp.float32)

    halves = {}
    stages, extra = {}, []
    for r in range(chunks + 3):
        if r <= chunks:
            fresh = r < chunks
            base = 3 * groups if fresh else 0
            most = {0: 1, 1: 3}.get(r, 1) * groups if fresh else 0
            at, size = take(most)
            length = max(base + size, 4 * groups) if fresh else 2 * groups
            given = dict(
                sides=sides, groups=groups, back=2 * groups if fresh else 0, kind=base, low=at, count=size
            )
            deps = [sent[r - 1]] if r else [near_left]
            deps += [sums[r - 1]] if r - 1 in sums else []
            out, mine, mark = pack(
                spot, pieces.pop(r) if fresh else ([], 0), straight.get(r - 1), carried, deps + extra, given,
                group, plane, length,
            )
            extra = []
            sent[r] = move(out, pairs)
            if size:
                parts.append((at, sent[r], base, size))
            if fresh:
                own[r] = mine
                straight[r] = move(mine, cross)
            done = out
            for first, size in {0: ((1, 1), (2, 1)), 1: ((3, chunks - 3),)}.get(r, ()):
                if size > 0 and first < chunks:
                    exchange(first, size, mark[1])
            if r == 0:
                late = mark[1]
                outer = [lower(0, late), lower(2, late)]
                extra = outer[:1]
        t = r - 4
        if 0 <= t < chunks:
            if near_low is None:
                near_low = low_of_planes(
                    sorted(parts, key=lambda p: p[0]), [done], units, group, groups, tiles
                )
            blocks = [(own[t], 2 * groups), (sent[t], 2 * groups), (straight[t], 2 * groups), (turned[t + 1], 2 * groups)]
            shares[t] = odd_product(
                spot, blocks, sums[t + 2], sums[t + 3], [done] + extra, (first_table, near_table),
                (middle_low, near_low), sides, group, groups, slab, roles,
            )
            done = shares[t][0]
            extra = []
            send_roles(t)
            if t - 1 in stages:
                extra.append(add_roles((t - 1,), [done]))
        if 1 <= r <= chunks + 1:
            at, size = take(2 * groups) if 2 <= r else (0, 0)
            given = dict(sides=sides, groups=groups, cross=r <= chunks, low=at, count=size)
            deps = [done] + ([last[r - 1]] if r - 1 in last else [])
            outs = pass_on(spot, sent[r - 1], turned.get(r - 1), carried, deps + extra, given, plane)
            extra = []
            if r <= chunks:
                turned[r] = move(outs[0], cross)
            if r - 1 in turned:
                last[r] = move(outs[-1], pairs)
                if size:
                    parts.append((at, last[r], 0, size))
            done = outs[0]
        if r == 1:
            first_table = make_table(flat_left(left_iso), [done], windows, slab)
            low = make_lows(outer, group)
            extra = [low, first_table]
        if r == 2:
            middle_low = make_lows([middle], group)
        if r >= 2:
            t = r - 2
            inner_blocks = end_blocks = None
            if t < chunks:
                inner_blocks = [(own[t], 0), (sent[t], 0), (straight[t], 0), (turned[t + 1], 0)]
            t = r - 3
            if 0 <= t:
                end_blocks = [
                    (own[t], 0), (sent[t], 0), (sent[t + 1], 2 * groups if t + 1 < chunks else 0), (last[t + 2], 0)
                ]
            sums[r] = even_product(
                spot, inner_blocks, end_blocks, [done] + extra, first_table, low, sides, group, groups, slab
            )
            done = sums[r]
            extra = []
            if r == 3:
                near_table = make_table(flat_left(near_left), [done], windows, slab)
                extra.append(near_table)
            if (r - 5,) in halves:
                extra.append(add_contr((r - 5,), [done]))
    t = chunks - 1
    blocks = [(own[t], 2 * groups), (sent[t], 2 * groups), (straight[t], 2 * groups), (turned[t + 1], 2 * groups)]
    shares[t] = odd_product(
        spot, blocks, sums[t + 2], sums[t + 3], [done] + extra, (first_table, near_table),
        (middle_low, near_low), sides, group, groups, slab, roles,
    )
    send_roles(t)
    late = tuple(t for t in range(chunks) if (t,) not in halves)
    done = [(t,) for t in range(chunks) if (t,) in halves]
    projected = project(done) if done else 0.0
    add_roles(late, [])
    add_contr(late, [])
    projected = projected + project([late])
    projected = projected * jnp.where(role >= downs, 0.25, 1.0)
    for axis, size in (("contr", contrs), ("horiz", sides)):
        s = 1
        while s < size:
            projected = projected + lax.ppermute(projected, axis, [(j, j ^ s) for j in range(size)])
            s *= 2
    found = [projected] + [
        lax.ppermute(projected, "role", [(j, j ^ s) for j in range(roles)]) for s in range(1, roles)
    ]
    found = jnp.stack(found)
    order = [lax.dynamic_index_in_dim(found, q ^ role, 0, keepdims=False) for q in range(roles)]
    return jnp.stack(order).reshape(roles // downs, downs, windows, -1)


def solution(mesh):
    placed = (
        P(None, "contr", "horiz", "role"),
        P(None, "contr", "horiz", None, None),
        P(None, None, "horiz"),
        P(("contr", "horiz"), None, None),
    )
    sizes = tuple(mesh.shape[axis] for axis in ("role", "contr", "horiz"))
    body = functools.partial(on_device, sizes)
    return jax.shard_map(body, mesh=mesh, in_specs=placed, out_specs=P(), check_vma=False)
```
